512 devices in a mesh: gx: 32 (over y, z_lo), gy: 16 (over x, z_hi, core).
Axes of the slice: x: 4, y: 4, z: 16 (z_hi: 2, z_lo: 8; z = z_hi * 8 + z_lo), core: 2. Of those that a mesh axis runs over, the one named last changes fastest.
Arguments:
- velocity: bfloat16 [3, 8, 256, 2048], P(None, None, 'gx', 'gy'), may hold values from -6 to 6
- kept_lm_qn: float32 [2, 8, 256, 2048], P(None, None, 'gx', 'gy'), may hold values from -3 to 3
- kept_mm_nn: float32 [2, 8, 256, 2048], P(None, None, 'gx', 'gy'), may hold values from 0.5 to 4
- back_src: int32 [8, 256, 256], P(None, 'gx', 'gy'), may hold values from 0 to 255, as said below
- solid_flags: int32 [8, 256, 2048], P(None, 'gx', 'gy'), may hold values from 0 to 1, as said below
- clip_flags: int32 [8, 256, 2048], P(None, 'gx', 'gy'), may hold values 0 or 1
Outputs:
- stress: float32 [6, 8, 256, 2048], P(None, None, 'gx', 'gy')
- kept_new: float32 [4, 8, 256, 2048], P(None, None, 'gx', 'gy')
The draws below stay inside these ranges and needn't reach their ends.
Inputs may be any that keep to these rules, and one draw needn't show every extreme that they name: `back_src`: each block's source row lies 0 to 16 rows upstream of the block's own row, cyclically along the streamwise dimension; on one wall-normal level every block lies exactly 16 rows upstream. `solid_flags`: the ones form one pipe lying along the spanwise dimension, of circular section with radius max(2, 1) cells, centred that many levels above the bed.
All inputs are finite; a program needn't handle non-finite values. No bound on the sum of `clip_flags` on one device may be relied on, other than what follows from the above.
Results may differ from the reference program's by a relative error of at most 0.00105.
Values may be sent and summed in bfloat16 or wider, within the bound.
No kernel may reach another device: no remote copies, remote signals or barrier semaphores. Data moves between devices by JAX's collectives and lax.ppermute only.
A program may use at most 64 MiB of HBM per device.

```python
import math
import jax
import jax.numpy as jnp
from jax import lax

CX = 8
NZ = 8
BLOCK = 8
NX = 256
NY = 2048


def draw_back_src(key, part):
    key_dist, key_level = jax.random.split(key)
    distance = jax.random.randint(key_dist, (NZ, NX, NY // BLOCK), 0, 2 * CX + 1)
    level = jax.random.randint(key_level, (), 0, NZ)
    depth = jnp.arange(NZ, dtype=jnp.int32)[:, None, None]
    distance = jnp.where(depth == level, 2 * CX, distance)
    rows_here = jnp.arange(NX, dtype=jnp.int32)[None, :, None]
    return ((rows_here - distance) % NX).astype(jnp.int32)


def draw_solid_flags(key, part):
    radius = max(NZ // 4, 1)
    centre = jax.random.randint(key, (), radius, NX - radius)
    rows_here = jnp.arange(NX, dtype=jnp.int32)[None, :, None]
    depth = jnp.arange(NZ, dtype=jnp.int32)[:, None, None]
    inside = (rows_here - centre) * (rows_here - centre) + (depth - radius) * (depth - radius) <= radius * radius
    return jnp.broadcast_to(inside, (NZ, NX, NY)).astype(jnp.int32)


def set_ends(array, stream_key, low, top_value):
    shape = array.shape
    place = [jax.random.randint(jax.random.fold_in(stream_key, axis), (), 0, shape[axis]) for axis in range(len(shape))]
    array = array.at[tuple(place)].set(low)
    longest = shape.index(max(shape))
    place[longest] = (place[longest] + 1) % shape[longest]
    return array.at[tuple(place)].set(top_value)


def shard_levels(rng, shape, cuts, low, largest):
    def one(axis_at, parts):
        steps = jax.random.uniform(jax.random.fold_in(jax.random.fold_in(rng, 6), axis_at), (parts,), jnp.float32, low / len(cuts), largest / len(cuts))
        return jnp.repeat(jnp.exp(steps), shape[axis_at] // parts).reshape((-1,) + (1,) * (len(shape) - axis_at - 1))

    gain = one(*cuts[0])
    for cut in cuts[1:]:
        gain = gain * one(*cut)
    return gain


def gaussian(rng, dims, deviation, most, shards=(), kind=jnp.bfloat16):
    result = deviation * jax.random.normal(rng, dims, jnp.float32)
    if shards:
        result = result * shard_levels(rng, dims, shards, -0.22, 0.18)
    return jnp.clip(result, -most, most).astype(kind)


def setup_inputs(seed: int = 0) -> dict:
    key_list = jax.random.split(jax.random.key(seed), 7)
    velocity = gaussian(key_list[0], (3, NZ, NX, NY), 1.0, 6.0, ((2, 32), (3, 16)))
    kept_lm_qn = gaussian(key_list[1], (2, NZ, NX, NY), 0.3, 3.0, ((2, 32), (3, 16)), jnp.float32)
    kept_mm_nn = jnp.clip(jnp.exp(math.log(4.0) - 2.0794415 * jax.random.uniform(key_list[2], (2, NZ, NX, NY), jnp.float32) ** shard_levels(key_list[2], (2, NZ, NX, NY), ((2, 32), (3, 16)), -0.2, 0.2)), 0.5, 4.0)
    back_src = draw_back_src(jax.random.fold_in(key_list[6], 71), 0)
    solid_flags = draw_solid_flags(jax.random.fold_in(key_list[6], 71), 0)
    clip_flags = set_ends((jax.random.randint(key_list[5], (NZ, NX, NY), 0, 2) < 1).astype(jnp.int32), jax.random.fold_in(key_list[5], 1), 0, 1)
    return {"velocity": velocity, "kept_lm_qn": kept_lm_qn, "kept_mm_nn": kept_mm_nn, "back_src": back_src, "solid_flags": solid_flags, "clip_flags": clip_flags}


TEST_NARROW = (0.25, 0.5, 0.25)
TEST_WIDE = (0.125, 0.25, 0.25, 0.25, 0.125)
PRODUCT_FLOOR = 0.05
RATE_SCALE = 0.5
CLIP_CAP = 0.1
RATIO_FLOOR = 0.02
PAIRS = ((0, 0), (1, 1), (2, 2), (0, 1), (0, 2), (1, 2))

def box_filter(field, weights):
    reach = (len(weights) - 1) // 2
    span_x = field.shape[-2] - 2 * reach
    along_x = sum((weights[k] * field[..., k:k + span_x, :] for k in range(len(weights))))
    span_y = field.shape[-1] - 2 * reach
    return sum((weights[k] * along_x[..., k:k + span_y] for k in range(len(weights))))

def contract(left, right):
    return lax.optimization_barrier(jnp.sum(left[:3] * right[:3], axis=0)) + 2.0 * lax.optimization_barrier(jnp.sum(left[3:] * right[3:], axis=0))

def vertical_diff(field):
    padded = jnp.concatenate([field[..., :1, :, :], field, field[..., -1:, :, :]], axis=-3)
    return (padded[..., 2:, :, :] - padded[..., :-2, :, :]) * 0.5

def strain_rate(vel):
    grad_x = (vel[..., 2:, 1:-1] - vel[..., :-2, 1:-1]) * 0.5
    grad_y = (vel[..., 1:-1, 2:] - vel[..., 1:-1, :-2]) * 0.5
    grad_z = vertical_diff(vel)[..., 1:-1, 1:-1]
    grads = (grad_x, grad_y, grad_z)
    tensor = jnp.stack([0.5 * (grads[j][i] + grads[i][j]) for i, j in PAIRS])
    return (tensor, jnp.sqrt(2.0 * contract(tensor, tensor)))

def pair_products(vel):
    return jnp.stack([vel[i] * vel[j] for i, j in PAIRS])

def channels(vel):
    tensor, mag = strain_rate(vel)
    inner = vel[..., 1:-1, 1:-1]
    return (jnp.concatenate([inner, pair_products(inner), mag[None] * tensor], axis=0), tensor, mag)

def relax_weight(product):
    rate = RATE_SCALE * jnp.power(jnp.maximum(product, PRODUCT_FLOOR), 0.125)
    return rate / (1.0 + rate)

def finish(chans, strain_in, mag_in, sources, solid, clipped):
    narrow = box_filter(chans, TEST_NARROW)
    wide = box_filter(chans, TEST_WIDE)
    strain_narrow, mag_narrow = strain_rate(narrow[:3, ..., 1:-1, 1:-1])
    strain_wide, mag_wide = strain_rate(wide[:3])
    narrow_in = narrow[..., 2:-2, 2:-2]
    wide_in = wide[..., 1:-1, 1:-1]
    leonard_narrow = narrow_in[3:9] - pair_products(narrow_in[:3])
    leonard_wide = wide_in[3:9] - pair_products(wide_in[:3])
    model_narrow = 2.0 * (narrow_in[9:15] - 4.0 * mag_narrow[None] * strain_narrow)
    model_wide = 2.0 * (wide_in[9:15] - 16.0 * mag_wide[None] * strain_wide)
    lm_now = contract(leonard_narrow, model_narrow)
    mm_now = contract(model_narrow, model_narrow)
    qn_now = contract(leonard_wide, model_wide)
    nn_now = contract(model_wide, model_wide)
    old_lm, old_qn, old_mm, old_nn = (sources[0], sources[1], sources[2], sources[3])
    weight_narrow = relax_weight(old_lm * old_mm)
    weight_wide = relax_weight(old_qn * old_nn)
    new_lm = weight_narrow * lm_now + (1.0 - weight_narrow) * old_lm
    new_mm = weight_narrow * mm_now + (1.0 - weight_narrow) * old_mm
    new_qn = weight_wide * qn_now + (1.0 - weight_wide) * old_qn
    new_nn = weight_wide * nn_now + (1.0 - weight_wide) * old_nn
    coeff_narrow = jnp.maximum(new_lm, 0.0) / new_mm
    coeff_wide = jnp.maximum(new_qn, 0.0) / new_nn
    coeff = coeff_narrow * coeff_narrow / jnp.maximum(jnp.maximum(coeff_wide, 0.125 * coeff_narrow), RATIO_FLOOR)
    coeff = jnp.where(clipped == 1, jnp.minimum(coeff, CLIP_CAP), coeff)
    stress = -2.0 * coeff[None] * mag_in[None] * strain_in
    stress = jnp.where(solid[None] == 1, 0.0, stress)
    return (stress, jnp.stack([new_lm, new_mm, new_qn, new_nn]))

def reference(velocity, kept_lm_qn, kept_mm_nn, back_src, solid_flags, clip_flags):
    masked = jnp.where(solid_flags[None] == 1, jnp.zeros((), velocity.dtype), velocity).astype(jnp.float32)
    padded = jnp.pad(masked, ((0, 0), (0, 0), (4, 4), (4, 4)), mode='wrap')
    own = jnp.concatenate([kept_lm_qn, kept_mm_nn], axis=0)

    def one_block(index):
        first = (index * CX).astype(jnp.int32)
        vel_block = lax.dynamic_slice_in_dim(padded, first, CX + 8, axis=2)
        chans, strain_all, mag_all = channels(vel_block)
        source_rows = lax.dynamic_slice_in_dim(back_src, first, CX, axis=1)
        source_rows = jnp.repeat(source_rows, BLOCK, axis=2).astype(jnp.int32)
        picked = jnp.take_along_axis(own, jnp.broadcast_to(source_rows[None], (4,) + source_rows.shape), axis=2)
        solid = lax.dynamic_slice_in_dim(solid_flags, first, CX, axis=1)
        clipped = lax.dynamic_slice_in_dim(clip_flags, first, CX, axis=1)
        return finish(chans, strain_all[..., 3:-3, 3:-3], mag_all[..., 3:-3, 3:-3], picked, solid, clipped)
    stress, kept = lax.map(one_block, jnp.arange(NX // CX, dtype=jnp.int32))
    stress = jnp.transpose(stress, (1, 2, 0, 3, 4)).reshape(6, NZ, NX, NY)
    kept = jnp.transpose(kept, (1, 2, 0, 3, 4)).reshape(4, NZ, NX, NY)
    return (stress, kept)
```

```python
import jax
import jax.numpy as jnp
from jax import lax
from jax.experimental import pallas as pl
from jax.experimental.pallas import tpu as pltpu
from jax.sharding import PartitionSpec as P

PRODUCT_FLOOR = 0.05
RATE_SCALE = 0.5
CLIP_CAP = 0.1
RATIO_FLOOR = 0.02
PAIRS = ((0, 0), (1, 1), (2, 2), (0, 1), (0, 2), (1, 2))
KEPT_SCALE = 32767.0 / 1.4142137
F32 = jnp.float32
BF16 = jnp.bfloat16
VMEM_LIMIT = 32 * 1024 * 1024


def row(ref, x, lead=None):
    at = (pl.ds(x, 8, stride=8), slice(None))
    return ref[at] if lead is None else ref[(lead,) + at]


def masked_rows(vel_ref, solid_ref, scratch):
    solid = solid_ref[...] == 1
    for c in range(3):
        scratch[c] = jnp.where(solid, 0.0, vel_ref[c].astype(F32))


def encode(x):
    root = jnp.sqrt(jnp.sqrt(jnp.abs(x)))
    scaled = jnp.where(x < 0, -root, root) * KEPT_SCALE
    return jnp.round(scaled).astype(jnp.int32).astype(jnp.int16)


def decode(code):
    y = code.astype(jnp.int32).astype(F32) * (1.0 / KEPT_SCALE)
    y2 = y * y
    return jnp.where(y < 0, -y2, y2) * y2


def pack_kernel(vel_ref, solid_ref, lq_ref, mn_ref, head_ref, tail_ref, kept_ref, scratch):
    masked_rows(vel_ref, solid_ref, scratch)
    for first, out in ((0, head_ref), (4, tail_ref)):
        rows = [row(scratch, first + x, c) for c in range(3) for x in range(4)]
        out[...] = jnp.concatenate(rows, axis=0).astype(BF16)
    kept_ref[pl.ds(0, 128), :] = encode(lq_ref[...])
    kept_ref[pl.ds(128, 128), :] = encode(mn_ref[...])


def halo_rows(scratch, lo_ref, hi_ref):
    lo = lo_ref[...].astype(F32).reshape(3, 4, 8, 128)
    hi = hi_ref[...].astype(F32).reshape(3, 4, 8, 128)
    out = []
    for c in range(3):
        rows = [lo[c, x] for x in (1, 2, 3)]
        rows += [row(scratch, x, c) for x in range(8)]
        rows += [hi[c, x] for x in (0, 1, 2)]
        out.append(rows)
    return out


def strip_kernel(par_ref, vel_ref, solid_ref, lo_ref, hi_ref, near_ref, far_ref, scratch):
    masked_rows(vel_ref, solid_ref, scratch)
    rows = halo_rows(scratch, lo_ref, hi_ref)
    lane = lax.broadcasted_iota(jnp.int32, (8, 128), 1)
    left, right = [], []
    for c in range(3):
        lefts = jnp.zeros((8, 128), F32)
        rights = jnp.zeros((8, 128), F32)
        for i in range(14):
            here = (lane >= 4 * i) & (lane < 4 * i + 4)
            lefts = jnp.where(here, pltpu.roll(rows[c][i], 4 * i, 1) if i else rows[c][i], lefts)
            rights = jnp.where(here, pltpu.roll(rows[c][i], 4 * i + 4, 1), rights)
        left.append(lefts)
        right.append(rights)
    left = jnp.concatenate(left + [jnp.zeros((8, 128), F32)], axis=0)
    right = jnp.concatenate(right + [jnp.zeros((8, 128), F32)], axis=0)
    even = par_ref[0] == 0
    near_ref[...] = jnp.where(even, right, left).astype(BF16)
    far_ref[...] = jnp.where(even, left, right).astype(BF16)


def shift_y(a, b, k, lane):
    if k > 0:
        return pltpu.roll(jnp.where(lane < k, b, a), 128 - k, 1)
    return pltpu.roll(jnp.where(lane >= 128 + k, b, a), -k, 1)


def diff_z(f, sub):
    up = jnp.where(sub == 7, f, pltpu.roll(f, 7, 0))
    down = jnp.where(sub == 0, f, pltpu.roll(f, 1, 0))
    return up - down


def strain(dx, dy, dz):
    d = (dx, dy, dz)
    s = [0.5 * d[i][i] for i in range(3)] + [0.25 * (d[j][i] + d[i][j]) for i, j in PAIRS[3:]]
    diag = s[0] * s[0] + s[1] * s[1] + s[2] * s[2]
    off = s[3] * s[3] + s[4] * s[4] + s[5] * s[5]
    return s, jnp.sqrt(2.0 * diag + 4.0 * off)


def contract(a, b):
    return (a[0] * b[0] + a[1] * b[1] + a[2] * b[2]) + 2.0 * (a[3] * b[3] + a[4] * b[4] + a[5] * b[5])


def relax_weight(product):
    r = RATE_SCALE * jnp.sqrt(jnp.sqrt(jnp.sqrt(jnp.maximum(product, PRODUCT_FLOOR))))
    return r / (1.0 + r)


def main_kernel(par_ref, vel_ref, solid_ref, clip_ref, lo_ref, hi_ref, near_ref, far_ref, src_ref,
                lq_ref, mn_ref, up1_ref, up2_ref, stress_ref, new_ref, scratch, old):
    lane = lax.broadcasted_iota(jnp.int32, (8, 128), 1)
    sub = lax.broadcasted_iota(jnp.int32, (8, 128), 0)
    here = lax.broadcasted_iota(jnp.int32, (64, 16), 0) % 8
    back = (par_ref[1] + here - src_ref[...] + 512) % 256
    spread = (lax.broadcasted_iota(jnp.int32, (16, 128), 1) // 8 == lax.broadcasted_iota(jnp.int32, (16, 128), 0))
    local = jnp.dot((16 + here - back).astype(F32), spread.astype(F32), preferred_element_type=F32)
    local = (local + 0.5).astype(jnp.int32)
    for z in range(8):
        at = pl.ds(8 * z, 8)
        idx = local[8 * z : 8 * z + 8]
        inner = idx & 7
        for f in range(4):
            rows = pl.ds(64 * f + 8 * z, 8)
            own_ref = lq_ref if f < 2 else mn_ref
            own = own_ref[pl.ds(64 * (f % 2) + 8 * z, 8), :]
            got = jnp.take_along_axis(own, inner, axis=0)
            one = jnp.take_along_axis(decode(up1_ref[f, at, :]), inner, axis=0)
            two = jnp.take_along_axis(decode(up2_ref[f, at, :]), inner, axis=0)
            old[f, at, :] = jnp.where(idx < 8, two, jnp.where(idx < 16, one, got))
    masked_rows(vel_ref, solid_ref, scratch)
    core = halo_rows(scratch, lo_ref, hi_ref)
    near = near_ref[...].astype(F32)
    far = far_ref[...].astype(F32)
    even = par_ref[0] == 0
    left = jnp.where(even, far, near).reshape(4, 8, 128)
    right = jnp.where(even, near, far).reshape(4, 8, 128)
    edge = []
    for c in range(3):
        rows = []
        for i in range(14):
            r = pltpu.roll(right[c], 128 - 4 * i, 1) if i else right[c]
            l = pltpu.roll(left[c], 124 - 4 * i, 1)
            rows.append(jnp.where(lane < 64, r, l))
        edge.append(rows)
    vn, vw, vdn, vdw = ([[None] * 14 for _ in range(3)] for _ in range(4))
    near_y = [[None] * 14 for _ in range(3)]
    for c in range(3):
        for i in range(14):
            a, b = core[c][i], edge[c][i]
            p1, m1 = shift_y(a, b, 1, lane), shift_y(a, b, -1, lane)
            p2, m2 = shift_y(a, b, 2, lane), shift_y(a, b, -2, lane)
            s1, d1, s2, d2 = p1 + m1, p1 - m1, p2 + m2, p2 - m2
            near_y[c][i] = d1
            if 1 <= i <= 12:
                vn[c][i] = a + a + s1
            t = a + s1
            vw[c][i] = t + t + s2
            if 2 <= i <= 11:
                vdn[c][i] = d1 + d1 + d2
            if 1 <= i <= 12:
                d3 = shift_y(a, b, 3, lane) - shift_y(a, b, -3, lane)
                vdw[c][i] = d1 + d2 + d2 + d3
    yn, yw = [None] * 14, [None] * 14
    own_flux = [None] * 14
    for i in range(1, 13):
        flux = []
        for t, o in ((core, edge), (edge, core)):
            dx = [t[c][i + 1] - t[c][i - 1] for c in range(3)]
            if t is core:
                dy = [near_y[c][i] for c in range(3)]
            else:
                dy = [shift_y(t[c][i], o[c][i], 1, lane) - shift_y(t[c][i], o[c][i], -1, lane) for c in range(3)]
            dz = [diff_z(t[c][i], sub) for c in range(3)]
            s, mag = strain(dx, dy, dz)
            prods = [t[p][i] * t[q][i] for p, q in PAIRS]
            flux.append(prods + [mag * e for e in s])
        own_flux[i] = flux[0][6:]
        ns, ws = [], []
        for a, b in zip(*flux):
            s1 = shift_y(a, b, 1, lane) + shift_y(a, b, -1, lane)
            s2 = shift_y(a, b, 2, lane) + shift_y(a, b, -2, lane)
            t = a + s1
            ns.append(a + t)
            ws.append(t + t + s2)
        yn[i], yw[i] = ns, ws

    def filt_n(r, i):
        return (r[i - 1] + r[i + 1] + (r[i] + r[i])) * 0.0625

    def filt_w(r, i):
        t = r[i - 1] + r[i] + r[i + 1]
        return (r[i - 2] + r[i + 2] + (t + t)) * 0.015625

    def column(r, k):
        return [None if v is None else v[k] for v in r]

    un = [[filt_n(vn[c], i) if 2 <= i <= 11 else None for i in range(14)] for c in range(3)]
    uw = [[filt_w(vw[c], i) if 2 <= i <= 11 else None for i in range(14)] for c in range(3)]
    for x in range(8):
        i = x + 3
        result = []
        for u, ydiff, filt, flux, factor in ((un, vdn, filt_n, yn, 4.0), (uw, vdw, filt_w, yw, 16.0)):
            dx = [u[c][i + 1] - u[c][i - 1] for c in range(3)]
            dy = [filt(ydiff[c], i) for c in range(3)]
            dz = [diff_z(u[c][i], sub) for c in range(3)]
            s, mag = strain(dx, dy, dz)
            f = [filt(column(flux, k), i) for k in range(12)]
            lhs = [f[k] - u[p][i] * u[q][i] for k, (p, q) in enumerate(PAIRS)]
            fm = factor * mag
            rhs = [f[6 + k] - fm * s[k] for k in range(6)]
            result.append((2.0 * contract(lhs, rhs), 4.0 * contract(rhs, rhs)))
        (lm, mm), (qn, nn) = result
        o_lm, o_qn, o_mm, o_nn = (row(old, x, f) for f in range(4))
        wn = relax_weight(o_lm * o_mm)
        ww = relax_weight(o_qn * o_nn)
        new_lm = wn * lm + (1.0 - wn) * o_lm
        new_mm = wn * mm + (1.0 - wn) * o_mm
        new_qn = ww * qn + (1.0 - ww) * o_qn
        new_nn = ww * nn + (1.0 - ww) * o_nn
        c2 = jnp.maximum(new_lm, 0.0) / new_mm
        c4 = jnp.maximum(new_qn, 0.0) / new_nn
        cs = c2 * c2 / jnp.maximum(jnp.maximum(c4, 0.125 * c2), RATIO_FLOOR)
        cs = jnp.where(row(clip_ref, x) == 1, jnp.minimum(cs, CLIP_CAP), cs)
        cs = jnp.where(row(solid_ref, x) == 1, 0.0, -2.0 * cs)
        at = (pl.ds(x, 8, stride=8), slice(None))
        for k in range(6):
            stress_ref[(k,) + at] = cs * own_flux[i][k]
        for k, v in enumerate((new_lm, new_mm, new_qn, new_nn)):
            new_ref[(k,) + at] = v


SMEM = pl.BlockSpec(memory_space=pltpu.SMEM)
VM = pl.BlockSpec(memory_space=pltpu.VMEM)


def call(kernel, outs, specs, scratch):
    return pl.pallas_call(
        kernel, out_shape=outs, in_specs=specs, out_specs=[VM] * len(outs), scratch_shapes=scratch,
        compiler_params=pltpu.CompilerParams(vmem_limit_bytes=VMEM_LIMIT),
    )


def ring(n, by):
    return [(i, (i + by) % n) for i in range(n)]


def local(velocity, kept_lm_qn, kept_mm_nn, back_src, solid_flags, clip_flags):
    sds = jax.ShapeDtypeStruct
    vel = velocity.reshape(3, 64, 128)
    solid = solid_flags.reshape(64, 128)
    clip = clip_flags.reshape(64, 128)
    lq = kept_lm_qn.reshape(128, 128)
    mn = kept_mm_nn.reshape(128, 128)
    src = back_src.reshape(64, 16)
    gx, gy = lax.axis_index("gx"), lax.axis_index("gy")
    par = jnp.stack([gy % 2, gx * 8]).astype(jnp.int32)
    trans = pltpu.VMEM((3, 64, 128), F32)
    head, tail, kept = call(
        pack_kernel, [sds((96, 128), BF16), sds((96, 128), BF16), sds((256, 128), jnp.int16)], [VM] * 4, [trans]
    )(vel, solid, lq, mn)
    up2 = lax.ppermute(kept, "gx", ring(32, 2))
    up1 = lax.ppermute(kept, "gx", ring(32, 1))
    lo = lax.ppermute(tail, "gx", ring(32, 1))
    hi = lax.ppermute(head, "gx", ring(32, -1))
    near, far = call(strip_kernel, [sds((32, 128), BF16)] * 2, [SMEM] + [VM] * 4, [trans])(par, vel, solid, lo, hi)
    near = lax.ppermute(near, "gy", [(i, i ^ 1) for i in range(16)])
    far = lax.ppermute(far, "gy", [(i, (i + 1) % 16 if i % 2 else (i - 1) % 16) for i in range(16)])
    stress, new = call(
        main_kernel, [sds((6, 64, 128), F32), sds((4, 64, 128), F32)], [SMEM] + [VM] * 12,
        [trans, pltpu.VMEM((4, 64, 128), F32)],
    )(par, vel, solid, clip, lo, hi, near, far, src, lq, mn, up1.reshape(4, 64, 128), up2.reshape(4, 64, 128))
    return stress.reshape(6, 8, 8, 128), new.reshape(4, 8, 8, 128)


def solution(mesh):
    in_specs = (
        P(None, None, "gx", "gy"),
        P(None, None, "gx", "gy"),
        P(None, None, "gx", "gy"),
        P(None, "gx", "gy"),
        P(None, "gx", "gy"),
        P(None, "gx", "gy"),
    )
    out_specs = (P(None, None, "gx", "gy"), P(None, None, "gx", "gy"))
    return jax.shard_map(local, mesh=mesh, in_specs=in_specs, out_specs=out_specs, check_vma=False)
```

```python
import jax
import jax.numpy as jnp
from jax import lax
from jax.experimental import pallas as pl
from jax.experimental.pallas import tpu as pltpu
from jax.sharding import PartitionSpec as P

PRODUCT_FLOOR = 0.05
RATE_SCALE = 0.5
CLIP_CAP = 0.1
RATIO_FLOOR = 0.02
PAIRS = ((0, 0), (1, 1), (2, 2), (0, 1), (0, 2), (1, 2))
KEPT_SCALE = 32767.0 / 1.4142137
F32 = jnp.float32
BF16 = jnp.bfloat16
VMEM_LIMIT = 32 * 1024 * 1024
PACK_LIMIT = 60 * 1024 * 1024


def row(ref, x, lead=None):
    at = (pl.ds(x, 8, stride=8), slice(None))
    return ref[at] if lead is None else ref[(lead,) + at]


def masked_rows(vel_ref, solid_ref, scratch):
    solid = solid_ref[...] == 1
    for c in range(3):
        scratch[c] = jnp.where(solid, 0.0, vel_ref[c].astype(F32))


def encode(x):
    root = jnp.sqrt(jnp.sqrt(jnp.abs(x)))
    scaled = jnp.where(x < 0, -root, root) * KEPT_SCALE
    return jnp.round(scaled).astype(jnp.int32).astype(jnp.int16)


def decode(code):
    y = code.astype(jnp.int32).astype(F32) * (1.0 / KEPT_SCALE)
    y2 = y * y
    return jnp.where(y < 0, -y2, y2) * y2


def pack_kernel(vel_hbm, solid_hbm, lq_hbm, mn_hbm, head_ref, tail_ref, kept_ref, vel, solid, kept, scratch, sems):
    copies = [
        pltpu.make_async_copy(vel_hbm, vel, sems.at[0]),
        pltpu.make_async_copy(solid_hbm, solid, sems.at[1]),
        pltpu.make_async_copy(lq_hbm, kept.at[pl.ds(0, 128)], sems.at[2]),
        pltpu.make_async_copy(mn_hbm, kept.at[pl.ds(128, 128)], sems.at[3]),
    ]
    for copy in copies:
        copy.start()
    copies[0].wait()
    copies[1].wait()
    masked_rows(vel, solid, scratch)
    head = [row(scratch, x, c) for c in range(3) for x in range(4)]
    head_ref[...] = jnp.concatenate(head, axis=0).astype(BF16)
    tail = [row(scratch, 4 + x, c) for c in range(3) for x in range(4)]
    tail_ref[pl.ds(0, 96), :] = jnp.concatenate(tail, axis=0).astype(BF16)
    copies[2].wait()
    copies[3].wait()
    old = kept[...]
    kept_ref[...] = encode(old)
    high = old.astype(BF16)
    tail_ref[pl.ds(96, 256), :] = high
    tail_ref[pl.ds(352, 256), :] = (old - high.astype(F32)).astype(BF16)


def halo_rows(scratch, lo_ref, hi_ref):
    lo = lo_ref[pl.ds(0, 96), :].astype(F32).reshape(3, 4, 8, 128)
    hi = hi_ref[...].astype(F32).reshape(3, 4, 8, 128)
    out = []
    for c in range(3):
        rows = [lo[c, x] for x in (1, 2, 3)]
        rows += [row(scratch, x, c) for x in range(8)]
        rows += [hi[c, x] for x in (0, 1, 2)]
        out.append(rows)
    return out


def strip_kernel(par_ref, vel_ref, solid_ref, lo_ref, hi_ref, far_ref, near_ref, scratch):
    masked_rows(vel_ref, solid_ref, scratch)
    rows = halo_rows(scratch, lo_ref, hi_ref)
    lane = lax.broadcasted_iota(jnp.int32, (8, 128), 1)
    left, right = [], []
    for c in range(3):
        lefts = jnp.zeros((8, 128), F32)
        rights = jnp.zeros((8, 128), F32)
        for i in range(14):
            here = (lane >= 4 * i) & (lane < 4 * i + 4)
            lefts = jnp.where(here, pltpu.roll(rows[c][i], 4 * i, 1) if i else rows[c][i], lefts)
            rights = jnp.where(here, pltpu.roll(rows[c][i], 4 * i + 4, 1), rights)
        left.append(lefts)
        right.append(rights)
    left = jnp.concatenate(left + [jnp.zeros((8, 128), F32)], axis=0)
    right = jnp.concatenate(right + [jnp.zeros((8, 128), F32)], axis=0)
    even = par_ref[0] == 0
    near_ref[...] = jnp.where(even, right, left).astype(BF16)
    far_ref[...] = jnp.where(even, left, right).astype(BF16)


def shift_y(a, b, k, lane):
    if k > 0:
        return pltpu.roll(jnp.where(lane < k, b, a), 128 - k, 1)
    return pltpu.roll(jnp.where(lane >= 128 + k, b, a), -k, 1)


def diff_z(f, sub):
    up = jnp.where(sub == 7, f, pltpu.roll(f, 7, 0))
    down = jnp.where(sub == 0, f, pltpu.roll(f, 1, 0))
    return up - down


def strain(dx, dy, dz):
    d = (dx, dy, dz)
    s = [0.5 * d[i][i] for i in range(3)] + [0.25 * (d[j][i] + d[i][j]) for i, j in PAIRS[3:]]
    diag = s[0] * s[0] + s[1] * s[1] + s[2] * s[2]
    off = s[3] * s[3] + s[4] * s[4] + s[5] * s[5]
    return s, jnp.sqrt(2.0 * diag + 4.0 * off)


def contract(a, b):
    return (a[0] * b[0] + a[1] * b[1] + a[2] * b[2]) + 2.0 * (a[3] * b[3] + a[4] * b[4] + a[5] * b[5])


def relax_weight(product):
    r = RATE_SCALE * jnp.sqrt(jnp.sqrt(jnp.sqrt(jnp.maximum(product, PRODUCT_FLOOR))))
    return r / (1.0 + r)


def main_kernel(par_ref, vel_ref, solid_ref, clip_ref, lo_ref, hi_ref, far_ref, near_ref, src_ref,
                lq_ref, mn_ref, up2_ref, stress_ref, new_ref, scratch, old):
    lane = lax.broadcasted_iota(jnp.int32, (8, 128), 1)
    sub = lax.broadcasted_iota(jnp.int32, (8, 128), 0)
    here = lax.broadcasted_iota(jnp.int32, (64, 16), 0) % 8
    back = (par_ref[1] + here - src_ref[...] + 512) % 256
    spread = (lax.broadcasted_iota(jnp.int32, (16, 128), 1) // 8 == lax.broadcasted_iota(jnp.int32, (16, 128), 0))
    local = jnp.dot((16 + here - back).astype(F32), spread.astype(F32), preferred_element_type=F32)
    local = (local + 0.5).astype(jnp.int32)
    one_high = lo_ref[pl.ds(96, 256), :].astype(F32).reshape(4, 64, 128)
    one_low = lo_ref[pl.ds(352, 256), :].astype(F32).reshape(4, 64, 128)
    up2 = decode(up2_ref[...]).reshape(4, 64, 128)
    for z in range(8):
        at = pl.ds(8 * z, 8)
        idx = local[8 * z : 8 * z + 8]
        inner = idx & 7
        for f in range(4):
            own_ref = lq_ref if f < 2 else mn_ref
            own = own_ref[pl.ds(64 * (f % 2) + 8 * z, 8), :]
            got = jnp.take_along_axis(own, inner, axis=0)
            up1 = one_high[f, 8 * z : 8 * z + 8] + one_low[f, 8 * z : 8 * z + 8]
            one = jnp.take_along_axis(up1, inner, axis=0)
            two = jnp.take_along_axis(up2[f, 8 * z : 8 * z + 8], inner, axis=0)
            old[f, at, :] = jnp.where(idx < 8, two, jnp.where(idx < 16, one, got))
    masked_rows(vel_ref, solid_ref, scratch)
    core = halo_rows(scratch, lo_ref, hi_ref)
    near = near_ref[...].astype(F32)
    far = far_ref[...].astype(F32)
    even = par_ref[0] == 0
    left = jnp.where(even, far, near).reshape(4, 8, 128)
    right = jnp.where(even, near, far).reshape(4, 8, 128)
    edge = []
    for c in range(3):
        rows = []
        for i in range(14):
            r = pltpu.roll(right[c], 128 - 4 * i, 1) if i else right[c]
            l = pltpu.roll(left[c], 124 - 4 * i, 1)
            rows.append(jnp.where(lane < 64, r, l))
        edge.append(rows)
    vn, vw, vdn, vdw = ([[None] * 14 for _ in range(3)] for _ in range(4))
    near_y = [[None] * 14 for _ in range(3)]
    for c in range(3):
        for i in range(14):
            a, b = core[c][i], edge[c][i]
            p1, m1 = shift_y(a, b, 1, lane), shift_y(a, b, -1, lane)
            p2, m2 = shift_y(a, b, 2, lane), shift_y(a, b, -2, lane)
            s1, d1, s2, d2 = p1 + m1, p1 - m1, p2 + m2, p2 - m2
            near_y[c][i] = d1
            if 1 <= i <= 12:
                vn[c][i] = a + a + s1
            t = a + s1
            vw[c][i] = t + t + s2
            if 2 <= i <= 11:
                vdn[c][i] = d1 + d1 + d2
            if 1 <= i <= 12:
                d3 = shift_y(a, b, 3, lane) - shift_y(a, b, -3, lane)
                vdw[c][i] = d1 + d2 + d2 + d3
    yn, yw = [None] * 14, [None] * 14
    own_flux = [None] * 14
    for i in range(1, 13):
        flux = []
        for t, o in ((core, edge), (edge, core)):
            dx = [t[c][i + 1] - t[c][i - 1] for c in range(3)]
            if t is core:
                dy = [near_y[c][i] for c in range(3)]
            else:
                dy = [shift_y(t[c][i], o[c][i], 1, lane) - shift_y(t[c][i], o[c][i], -1, lane) for c in range(3)]
            dz = [diff_z(t[c][i], sub) for c in range(3)]
            s, mag = strain(dx, dy, dz)
            prods = [t[p][i] * t[q][i] for p, q in PAIRS]
            flux.append(prods + [mag * e for e in s])
        own_flux[i] = flux[0][6:]
        ns, ws = [], []
        for a, b in zip(*flux):
            s1 = shift_y(a, b, 1, lane) + shift_y(a, b, -1, lane)
            s2 = shift_y(a, b, 2, lane) + shift_y(a, b, -2, lane)
            t = a + s1
            ns.append(a + t)
            ws.append(t + t + s2)
        yn[i], yw[i] = ns, ws

    def filt_n(r, i):
        return (r[i - 1] + r[i + 1] + (r[i] + r[i])) * 0.0625

    def filt_w(r, i):
        t = r[i - 1] + r[i] + r[i + 1]
        return (r[i - 2] + r[i + 2] + (t + t)) * 0.015625

    def column(r, k):
        return [None if v is None else v[k] for v in r]

    un = [[filt_n(vn[c], i) if 2 <= i <= 11 else None for i in range(14)] for c in range(3)]
    uw = [[filt_w(vw[c], i) if 2 <= i <= 11 else None for i in range(14)] for c in range(3)]
    for x in range(8):
        i = x + 3
        result = []
        for u, ydiff, filt, flux, factor in ((un, vdn, filt_n, yn, 4.0), (uw, vdw, filt_w, yw, 16.0)):
            dx = [u[c][i + 1] - u[c][i - 1] for c in range(3)]
            dy = [filt(ydiff[c], i) for c in range(3)]
            dz = [diff_z(u[c][i], sub) for c in range(3)]
            s, mag = strain(dx, dy, dz)
            f = [filt(column(flux, k), i) for k in range(12)]
            lhs = [f[k] - u[p][i] * u[q][i] for k, (p, q) in enumerate(PAIRS)]
            fm = factor * mag
            rhs = [f[6 + k] - fm * s[k] for k in range(6)]
            result.append((2.0 * contract(lhs, rhs), 4.0 * contract(rhs, rhs)))
        (lm, mm), (qn, nn) = result
        o_lm, o_qn, o_mm, o_nn = (row(old, x, f) for f in range(4))
        wn = relax_weight(o_lm * o_mm)
        ww = relax_weight(o_qn * o_nn)
        new_lm = wn * lm + (1.0 - wn) * o_lm
        new_mm = wn * mm + (1.0 - wn) * o_mm
        new_qn = ww * qn + (1.0 - ww) * o_qn
        new_nn = ww * nn + (1.0 - ww) * o_nn
        c2 = jnp.maximum(new_lm, 0.0) / new_mm
        c4 = jnp.maximum(new_qn, 0.0) / new_nn
        cs = c2 * c2 / jnp.maximum(jnp.maximum(c4, 0.125 * c2), RATIO_FLOOR)
        cs = jnp.where(row(clip_ref, x) == 1, jnp.minimum(cs, CLIP_CAP), cs)
        cs = jnp.where(row(solid_ref, x) == 1, 0.0, -2.0 * cs)
        at = (pl.ds(x, 8, stride=8), slice(None))
        for k in range(6):
            stress_ref[(k,) + at] = cs * own_flux[i][k]
        for k, v in enumerate((new_lm, new_mm, new_qn, new_nn)):
            new_ref[(k,) + at] = v


SMEM = pl.BlockSpec(memory_space=pltpu.SMEM)
VM = pl.BlockSpec(memory_space=pltpu.VMEM)
HBM = pl.BlockSpec(memory_space=pltpu.HBM)


def call(kernel, outs, specs, scratch, limit=VMEM_LIMIT):
    return pl.pallas_call(
        kernel, out_shape=outs, in_specs=specs, out_specs=[VM] * len(outs), scratch_shapes=scratch,
        compiler_params=pltpu.CompilerParams(vmem_limit_bytes=limit),
    )


def ring(n, by):
    return [(i, (i + by) % n) for i in range(n)]


def local(velocity, kept_lm_qn, kept_mm_nn, back_src, solid_flags, clip_flags):
    sds = jax.ShapeDtypeStruct
    vel = velocity.reshape(3, 64, 128)
    solid = solid_flags.reshape(64, 128)
    clip = clip_flags.reshape(64, 128)
    lq = kept_lm_qn.reshape(128, 128)
    mn = kept_mm_nn.reshape(128, 128)
    src = back_src.reshape(64, 16)
    gx, gy = lax.axis_index("gx"), lax.axis_index("gy")
    par = jnp.stack([gy % 2, gx * 8]).astype(jnp.int32)
    trans = pltpu.VMEM((3, 64, 128), F32)
    head, tail, kept = call(
        pack_kernel,
        [sds((96, 128), BF16), sds((608, 128), BF16), sds((256, 128), jnp.int16)],
        [HBM] * 4,
        [pltpu.VMEM((3, 64, 128), BF16), pltpu.VMEM((64, 128), jnp.int32), pltpu.VMEM((256, 128), F32), trans,
         pltpu.SemaphoreType.DMA((4,))],
        PACK_LIMIT,
    )(vel, solid, lq, mn)
    lo = lax.ppermute(tail, "gx", ring(32, 1))
    hi = lax.ppermute(head, "gx", ring(32, -1))
    up2 = lax.ppermute(kept, "gx", ring(32, 2))
    far, near = call(strip_kernel, [sds((32, 128), BF16)] * 2, [SMEM] + [VM] * 4, [trans])(par, vel, solid, lo, hi)
    far = lax.ppermute(far, "gy", [(i, (i + 1) % 16 if i % 2 else (i - 1) % 16) for i in range(16)])
    near = lax.ppermute(near, "gy", [(i, i ^ 1) for i in range(16)])
    stress, new = call(
        main_kernel, [sds((6, 64, 128), F32), sds((4, 64, 128), F32)], [SMEM] + [VM] * 11,
        [trans, pltpu.VMEM((4, 64, 128), F32)],
    )(par, vel, solid, clip, lo, hi, far, near, src, lq, mn, up2)
    return stress.reshape(6, 8, 8, 128), new.reshape(4, 8, 8, 128)


def solution(mesh):
    in_specs = (
        P(None, None, "gx", "gy"),
        P(None, None, "gx", "gy"),
        P(None, None, "gx", "gy"),
        P(None, "gx", "gy"),
        P(None, "gx", "gy"),
        P(None, "gx", "gy"),
    )
    out_specs = (P(None, None, "gx", "gy"), P(None, None, "gx", "gy"))
    return jax.shard_map(local, mesh=mesh, in_specs=in_specs, out_specs=out_specs, check_vma=False)
```

```python
import jax
import jax.numpy as jnp
from jax import lax
from jax.experimental import pallas as pl
from jax.experimental.pallas import tpu as pltpu
from jax.sharding import PartitionSpec as P

PRODUCT_FLOOR = 0.05
RATE_SCALE = 0.5
CLIP_CAP = 0.1
RATIO_FLOOR = 0.02
PAIRS = ((0, 0), (1, 1), (2, 2), (0, 1), (0, 2), (1, 2))
KEPT_SCALE = 32767.0 / 1.4142137
F32 = jnp.float32
BF16 = jnp.bfloat16
VMEM_LIMIT = 32 * 1024 * 1024
PACK_LIMIT = 60 * 1024 * 1024
STRIP_FLOPS = 1_000_000_000


def row(ref, x, lead=None):
    at = (pl.ds(x, 8, stride=8), slice(None))
    return ref[at] if lead is None else ref[(lead,) + at]


def masked_rows(vel_ref, solid_ref, scratch):
    solid = solid_ref[...] == 1
    for c in range(3):
        scratch[c] = jnp.where(solid, 0.0, vel_ref[c].astype(F32))


def encode(x):
    root = jnp.sqrt(jnp.sqrt(jnp.abs(x)))
    scaled = jnp.where(x < 0, -root, root) * KEPT_SCALE
    return jnp.round(scaled).astype(jnp.int32).astype(jnp.int16)


def decode(code):
    y = code.astype(jnp.int32).astype(F32) * (1.0 / KEPT_SCALE)
    y2 = y * y
    return jnp.where(y < 0, -y2, y2) * y2


def pack_kernel(vel_hbm, solid_hbm, lq_hbm, mn_hbm, head_ref, tail_ref, kept_ref, vel, solid, kept, scratch, sems):
    copies = [
        pltpu.make_async_copy(vel_hbm, vel, sems.at[0]),
        pltpu.make_async_copy(solid_hbm, solid, sems.at[1]),
        pltpu.make_async_copy(lq_hbm, kept.at[pl.ds(0, 128)], sems.at[2]),
        pltpu.make_async_copy(mn_hbm, kept.at[pl.ds(128, 128)], sems.at[3]),
    ]
    for copy in copies:
        copy.start()
    copies[0].wait()
    copies[1].wait()
    masked_rows(vel, solid, scratch)
    head = [row(scratch, x, c) for c in range(3) for x in range(4)]
    head_ref[...] = jnp.concatenate(head, axis=0).astype(BF16)
    tail = [row(scratch, 4 + x, c) for c in range(3) for x in range(4)]
    tail_ref[pl.ds(0, 96), :] = jnp.concatenate(tail, axis=0).astype(BF16)
    copies[2].wait()
    copies[3].wait()
    old = kept[...]
    kept_ref[...] = encode(old)
    high = old.astype(BF16)
    tail_ref[pl.ds(96, 256), :] = high
    tail_ref[pl.ds(352, 256), :] = (old - high.astype(F32)).astype(BF16)


def halo_rows(scratch, lo_ref, hi_ref):
    lo = lo_ref[pl.ds(0, 96), :].astype(F32).reshape(3, 4, 8, 128)
    hi = hi_ref[...].astype(F32).reshape(3, 4, 8, 128)
    out = []
    for c in range(3):
        rows = [lo[c, x] for x in (1, 2, 3)]
        rows += [row(scratch, x, c) for x in range(8)]
        rows += [hi[c, x] for x in (0, 1, 2)]
        out.append(rows)
    return out


def strip_kernel(vel_ref, solid_ref, lo_ref, hi_ref, far_ref, near_ref, scratch):
    masked_rows(vel_ref, solid_ref, scratch)
    rows = halo_rows(scratch, lo_ref, hi_ref)
    lane = lax.broadcasted_iota(jnp.int32, (8, 128), 1)
    left, right = [], []
    for c in range(3):
        lefts = jnp.zeros((8, 128), F32)
        rights = jnp.zeros((8, 128), F32)
        for i in range(14):
            here = (lane >= 4 * i) & (lane < 4 * i + 4)
            lefts = jnp.where(here, pltpu.roll(rows[c][i], 4 * i, 1) if i else rows[c][i], lefts)
            rights = jnp.where(here, pltpu.roll(rows[c][i], 4 * i + 4, 1), rights)
        left.append(lefts)
        right.append(rights)
    left = jnp.concatenate(left + [jnp.zeros((8, 128), F32)], axis=0)
    right = jnp.concatenate(right + [jnp.zeros((8, 128), F32)], axis=0)
    even = lax.axis_index("gy") % 2 == 0
    near_ref[...] = jnp.where(even, right, left).astype(BF16)
    far_ref[...] = jnp.where(even, left, right).astype(BF16)


def shift_y(a, b, k, lane):
    if k > 0:
        return pltpu.roll(jnp.where(lane < k, b, a), 128 - k, 1)
    return pltpu.roll(jnp.where(lane >= 128 + k, b, a), -k, 1)


def diff_z(f, sub):
    up = jnp.where(sub == 7, f, pltpu.roll(f, 7, 0))
    down = jnp.where(sub == 0, f, pltpu.roll(f, 1, 0))
    return up - down


def strain(dx, dy, dz):
    d = (dx, dy, dz)
    s = [0.5 * d[i][i] for i in range(3)] + [0.25 * (d[j][i] + d[i][j]) for i, j in PAIRS[3:]]
    diag = s[0] * s[0] + s[1] * s[1] + s[2] * s[2]
    off = s[3] * s[3] + s[4] * s[4] + s[5] * s[5]
    return s, jnp.sqrt(2.0 * diag + 4.0 * off)


def contract(a, b):
    return (a[0] * b[0] + a[1] * b[1] + a[2] * b[2]) + 2.0 * (a[3] * b[3] + a[4] * b[4] + a[5] * b[5])


def relax_weight(product):
    inverse = lax.rsqrt(lax.rsqrt(lax.rsqrt(jnp.maximum(product, PRODUCT_FLOOR))))
    return 1.0 / (1.0 + (1.0 / RATE_SCALE) * inverse)


def main_kernel(vel_ref, solid_ref, clip_ref, lo_ref, hi_ref, far_ref, near_ref, src_ref,
                lq_ref, mn_ref, up2_ref, stress_ref, new_ref, scratch, old):
    lane = lax.broadcasted_iota(jnp.int32, (8, 128), 1)
    sub = lax.broadcasted_iota(jnp.int32, (8, 128), 0)
    here = lax.broadcasted_iota(jnp.int32, (64, 16), 0) % 8
    back = (lax.axis_index("gx") * 8 + here - src_ref[...] + 512) & 255
    spread = (lax.broadcasted_iota(jnp.int32, (16, 128), 1) // 8 == lax.broadcasted_iota(jnp.int32, (16, 128), 0))
    local = jnp.dot((16 + here - back).astype(F32), spread.astype(F32), preferred_element_type=F32)
    local = (local + 0.5).astype(jnp.int32)
    one_high = lo_ref[pl.ds(96, 256), :].astype(F32).reshape(4, 64, 128)
    one_low = lo_ref[pl.ds(352, 256), :].astype(F32).reshape(4, 64, 128)
    up2 = decode(up2_ref[...]).reshape(4, 64, 128)
    for z in range(8):
        at = pl.ds(8 * z, 8)
        idx = local[8 * z : 8 * z + 8]
        inner = idx & 7
        for f in range(4):
            own_ref = lq_ref if f < 2 else mn_ref
            own = own_ref[pl.ds(64 * (f % 2) + 8 * z, 8), :]
            got = jnp.take_along_axis(own, inner, axis=0)
            up1 = one_high[f, 8 * z : 8 * z + 8] + one_low[f, 8 * z : 8 * z + 8]
            one = jnp.take_along_axis(up1, inner, axis=0)
            two = jnp.take_along_axis(up2[f, 8 * z : 8 * z + 8], inner, axis=0)
            old[f, at, :] = jnp.where(idx < 8, two, jnp.where(idx < 16, one, got))
    masked_rows(vel_ref, solid_ref, scratch)
    core = halo_rows(scratch, lo_ref, hi_ref)
    near = near_ref[...].astype(F32)
    far = far_ref[...].astype(F32)
    even = lax.axis_index("gy") % 2 == 0
    left = jnp.where(even, far, near).reshape(4, 8, 128)
    right = jnp.where(even, near, far).reshape(4, 8, 128)
    edge = []
    for c in range(3):
        rows = []
        for i in range(14):
            r = pltpu.roll(right[c], 128 - 4 * i, 1) if i else right[c]
            l = pltpu.roll(left[c], 124 - 4 * i, 1)
            rows.append(jnp.where(lane < 64, r, l))
        edge.append(rows)
    vn, vw, vdn, vdw = ([[None] * 14 for _ in range(3)] for _ in range(4))
    near_y = [[None] * 14 for _ in range(3)]
    for c in range(3):
        for i in range(14):
            a, b = core[c][i], edge[c][i]
            p1, m1 = shift_y(a, b, 1, lane), shift_y(a, b, -1, lane)
            p2, m2 = shift_y(a, b, 2, lane), shift_y(a, b, -2, lane)
            s1, d1, s2, d2 = p1 + m1, p1 - m1, p2 + m2, p2 - m2
            near_y[c][i] = d1
            if 1 <= i <= 12:
                vn[c][i] = a + a + s1
            t = a + s1
            vw[c][i] = t + t + s2
            if 2 <= i <= 11:
                vdn[c][i] = d1 + d1 + d2
            if 1 <= i <= 12:
                d3 = shift_y(a, b, 3, lane) - shift_y(a, b, -3, lane)
                vdw[c][i] = d1 + d2 + d2 + d3
    yn, yw = [None] * 14, [None] * 14
    own_flux = [None] * 14
    for i in range(1, 13):
        flux = []
        for t, o in ((core, edge), (edge, core)):
            dx = [t[c][i + 1] - t[c][i - 1] for c in range(3)]
            if t is core:
                dy = [near_y[c][i] for c in range(3)]
            else:
                dy = [shift_y(t[c][i], o[c][i], 1, lane) - shift_y(t[c][i], o[c][i], -1, lane) for c in range(3)]
            dz = [diff_z(t[c][i], sub) for c in range(3)]
            s, mag = strain(dx, dy, dz)
            prods = [t[p][i] * t[q][i] for p, q in PAIRS]
            flux.append(prods + [mag * e for e in s])
        own_flux[i] = flux[0][6:]
        ns, ws = [], []
        for a, b in zip(*flux):
            s1 = shift_y(a, b, 1, lane) + shift_y(a, b, -1, lane)
            s2 = shift_y(a, b, 2, lane) + shift_y(a, b, -2, lane)
            t = a + s1
            ns.append(a + t)
            ws.append(t + t + s2)
        yn[i], yw[i] = ns, ws

    def filt_n(r, i):
        return (r[i - 1] + r[i + 1] + (r[i] + r[i])) * 0.0625

    def filt_w(r, i):
        t = r[i - 1] + r[i] + r[i + 1]
        return (r[i - 2] + r[i + 2] + (t + t)) * 0.015625

    def column(r, k):
        return [None if v is None else v[k] for v in r]

    un = [[filt_n(vn[c], i) if 2 <= i <= 11 else None for i in range(14)] for c in range(3)]
    uw = [[filt_w(vw[c], i) if 2 <= i <= 11 else None for i in range(14)] for c in range(3)]
    for x in range(8):
        i = x + 3
        result = []
        for u, ydiff, filt, flux, factor in ((un, vdn, filt_n, yn, 4.0), (uw, vdw, filt_w, yw, 16.0)):
            dx = [u[c][i + 1] - u[c][i - 1] for c in range(3)]
            dy = [filt(ydiff[c], i) for c in range(3)]
            dz = [diff_z(u[c][i], sub) for c in range(3)]
            s, mag = strain(dx, dy, dz)
            f = [filt(column(flux, k), i) for k in range(12)]
            lhs = [f[k] - u[p][i] * u[q][i] for k, (p, q) in enumerate(PAIRS)]
            fm = factor * mag
            rhs = [f[6 + k] - fm * s[k] for k in range(6)]
            result.append((2.0 * contract(lhs, rhs), 4.0 * contract(rhs, rhs)))
        (lm, mm), (qn, nn) = result
        o_lm, o_qn, o_mm, o_nn = (row(old, x, f) for f in range(4))
        wn = relax_weight(o_lm * o_mm)
        ww = relax_weight(o_qn * o_nn)
        new_lm = wn * lm + (1.0 - wn) * o_lm
        new_mm = wn * mm + (1.0 - wn) * o_mm
        new_qn = ww * qn + (1.0 - ww) * o_qn
        new_nn = ww * nn + (1.0 - ww) * o_nn
        c2 = jnp.maximum(new_lm, 0.0) / new_mm
        c4 = jnp.maximum(new_qn, 0.0) / new_nn
        cs = c2 * c2 / jnp.maximum(jnp.maximum(c4, 0.125 * c2), RATIO_FLOOR)
        cs = jnp.where(row(clip_ref, x) == 1, jnp.minimum(cs, CLIP_CAP), cs)
        cs = jnp.where(row(solid_ref, x) == 1, 0.0, -2.0 * cs)
        at = (pl.ds(x, 8, stride=8), slice(None))
        for k in range(6):
            stress_ref[(k,) + at] = cs * own_flux[i][k]
        for k, v in enumerate((new_lm, new_mm, new_qn, new_nn)):
            new_ref[(k,) + at] = v


VM = pl.BlockSpec(memory_space=pltpu.VMEM)
HBM = pl.BlockSpec(memory_space=pltpu.HBM)


def call(kernel, outs, specs, scratch, limit=VMEM_LIMIT, flops=0):
    return pl.pallas_call(
        kernel, out_shape=outs, in_specs=specs, out_specs=[VM] * len(outs), scratch_shapes=scratch,
        compiler_params=pltpu.CompilerParams(vmem_limit_bytes=limit),
        cost_estimate=pl.CostEstimate(flops=flops, bytes_accessed=400_000, transcendentals=0),
    )


def ring(n, by):
    return [(i, (i + by) % n) for i in range(n)]


def local(velocity, kept_lm_qn, kept_mm_nn, back_src, solid_flags, clip_flags):
    sds = jax.ShapeDtypeStruct
    vel = velocity.reshape(3, 64, 128)
    solid = solid_flags.reshape(64, 128)
    clip = clip_flags.reshape(64, 128)
    lq = kept_lm_qn.reshape(128, 128)
    mn = kept_mm_nn.reshape(128, 128)
    src = back_src.reshape(64, 16)
    trans = pltpu.VMEM((3, 64, 128), F32)
    head, tail, kept = call(
        pack_kernel,
        [sds((96, 128), BF16), sds((608, 128), BF16), sds((256, 128), jnp.int16)],
        [HBM] * 4,
        [pltpu.VMEM((3, 64, 128), BF16), pltpu.VMEM((64, 128), jnp.int32), pltpu.VMEM((256, 128), F32), trans,
         pltpu.SemaphoreType.DMA((4,))],
        PACK_LIMIT,
    )(vel, solid, lq, mn)
    lo = lax.ppermute(tail, "gx", ring(32, 1))
    hi = lax.ppermute(head, "gx", ring(32, -1))
    up2 = lax.ppermute(kept, "gx", ring(32, 2))
    far, near = call(strip_kernel, [sds((32, 128), BF16)] * 2, [VM] * 4, [trans], flops=STRIP_FLOPS)(vel, solid, lo, hi)
    far = lax.ppermute(far, "gy", [(i, (i + 1) % 16 if i % 2 else (i - 1) % 16) for i in range(16)])
    near = lax.ppermute(near, "gy", [(i, i ^ 1) for i in range(16)])
    stress, new = call(
        main_kernel, [sds((6, 64, 128), F32), sds((4, 64, 128), F32)], [VM] * 11,
        [trans, pltpu.VMEM((4, 64, 128), F32)],
    )(vel, solid, clip, lo, hi, far, near, src, lq, mn, up2)
    return stress.reshape(6, 8, 8, 128), new.reshape(4, 8, 8, 128)


def solution(mesh):
    in_specs = (
        P(None, None, "gx", "gy"),
        P(None, None, "gx", "gy"),
        P(None, None, "gx", "gy"),
        P(None, "gx", "gy"),
        P(None, "gx", "gy"),
        P(None, "gx", "gy"),
    )
    out_specs = (P(None, None, "gx", "gy"), P(None, None, "gx", "gy"))
    return jax.shard_map(local, mesh=mesh, in_specs=in_specs, out_specs=out_specs, check_vma=False)
```

```python
import jax
import jax.numpy as jnp
from jax import lax
from jax.experimental import pallas as pl
from jax.experimental.pallas import tpu as pltpu
from jax.sharding import PartitionSpec as P

PRODUCT_FLOOR = 0.05
RATE_SCALE = 0.5
CLIP_CAP = 0.1
RATIO_FLOOR = 0.02
PAIRS = ((0, 0), (1, 1), (2, 2), (0, 1), (0, 2), (1, 2))
KEPT_SCALE = 32767.0 / 1.4142137
F32 = jnp.float32
BF16 = jnp.bfloat16
VMEM_LIMIT = 32 * 1024 * 1024
PACK_LIMIT = 60 * 1024 * 1024
BIG = 1_000_000_000
SIDE = 256


def row(ref, x, lead=None):
    at = (pl.ds(x, 8, stride=8), slice(None))
    return ref[at] if lead is None else ref[(lead,) + at]


def encode(x):
    root = jnp.sqrt(jnp.sqrt(jnp.abs(x)))
    scaled = jnp.where(x < 0, -root, root) * KEPT_SCALE
    return jnp.round(scaled).astype(jnp.int32).astype(jnp.int16)


def decode(code):
    y = code.astype(jnp.int32).astype(F32) * (1.0 / KEPT_SCALE)
    y2 = y * y
    return jnp.where(y < 0, -y2, y2) * y2


def place():
    return lax.axis_index("gx") & 7, (lax.axis_index("gy") & 1) == 0


def edges(rows, first):
    lane = lax.broadcasted_iota(jnp.int32, (8, 128), 1)
    left, right = [], []
    for c in range(3):
        lefts = jnp.zeros((8, 128), F32)
        rights = jnp.zeros((8, 128), F32)
        for k, value in enumerate(rows[c]):
            i = first + k
            here = (lane >= 4 * i) & (lane < 4 * i + 4)
            lefts = jnp.where(here, pltpu.roll(value, 4 * i, 1) if i else value, lefts)
            rights = jnp.where(here, pltpu.roll(value, 4 * i + 4, 1), rights)
        left.append(lefts)
        right.append(rights)
    none = [jnp.zeros((8, 128), F32)]
    return jnp.concatenate(left + none, axis=0), jnp.concatenate(right + none, axis=0)


def own_rows(vel_ref, solid_ref, scratch):
    inside = solid_ref[...] == 1
    for c in range(3):
        scratch[c] = jnp.where(inside, 0.0, vel_ref[c].astype(F32))
    return [[row(scratch, x, c) for x in range(8)] for c in range(3)]


def pack_kernel(vel_hbm, solid_hbm, lq_hbm, mn_hbm, tail_ref, head_ref, side_ref, code_ref,
                vel, solid, kept, scratch, sems):
    copies = [
        pltpu.make_async_copy(vel_hbm, vel, sems.at[0]),
        pltpu.make_async_copy(solid_hbm, solid, sems.at[1]),
        pltpu.make_async_copy(lq_hbm, kept.at[pl.ds(0, 128)], sems.at[2]),
        pltpu.make_async_copy(mn_hbm, kept.at[pl.ds(128, 128)], sems.at[3]),
    ]
    for copy in copies:
        copy.start()
    copies[0].wait()
    copies[1].wait()
    rows = own_rows(vel, solid, scratch)
    head_ref[...] = jnp.concatenate([rows[c][x] for c in range(3) for x in range(4)], axis=0).astype(BF16)
    tail = jnp.concatenate([rows[c][4 + x] for c in range(3) for x in range(4)], axis=0).astype(BF16)
    tail_ref[pl.ds(0, 96), :] = tail
    side_ref[pl.ds(0, 96), :] = tail
    side_ref[pl.ds(96, SIDE - 96), :] = jnp.zeros((SIDE - 96, 128), BF16)
    copies[2].wait()
    copies[3].wait()
    old = kept[...]
    code_ref[...] = encode(old)
    high = old.astype(BF16)
    tail_ref[pl.ds(96, 256), :] = high
    tail_ref[pl.ds(352, 256), :] = (old - high.astype(F32)).astype(BF16)


def all_rows(own, lo, hi):
    lo = lo.reshape(3, 4, 8, 128)
    hi = hi.reshape(3, 4, 8, 128)
    out = []
    for c in range(3):
        rows = [lo[c, x] for x in (1, 2, 3)]
        rows += own[c]
        rows += [hi[c, x] for x in (0, 1, 2)]
        out.append(rows)
    return out


def lead(ref, n):
    return ref[pl.ds(0, n), :].astype(F32)


def far_kernel(vel_ref, solid_ref, lo_ref, hi_ref, wide_ref, strip_ref, scratch):
    own = own_rows(vel_ref, solid_ref, scratch)
    rows = all_rows(own, lead(lo_ref, 96), lead(hi_ref, 96))
    left, right = edges(rows, 0)
    _, even = place()
    strip = jnp.where(even, left, right).astype(BF16)
    strip_ref[...] = strip
    wide_ref[pl.ds(96, 32), :] = strip
    wide_ref[pl.ds(0, 96), :] = jnp.concatenate([own[c][x] for c in range(3) for x in range(4)], axis=0).astype(BF16)


def relay_kernel(wide_ref, strip_ref, head_ref, side_ref, two_ref, relay_ref, strip_out):
    relay_ref[pl.ds(0, 96), :] = wide_ref[pl.ds(0, 96), :]
    relay_ref[pl.ds(96, 96), :] = head_ref[...]
    strip_out[...] = strip_ref[...]


def near_kernel(vel_ref, solid_ref, lo_ref, wrap_ref, hi_ref, relay_ref, strip_ref, scratch):
    at, even = place()
    own = own_rows(vel_ref, solid_ref, scratch)
    lo = jnp.where(at == 0, lead(wrap_ref, 96), lead(lo_ref, 96))
    hi = jnp.where(at == 7, lead(relay_ref, 96), lead(hi_ref, 96))
    left, right = edges(all_rows(own, lo, hi), 0)
    strip_ref[...] = jnp.where(even, right, left).astype(BF16)


def shift_y(a, b, k, lane):
    if k > 0:
        return pltpu.roll(jnp.where(lane < k, b, a), 128 - k, 1)
    return pltpu.roll(jnp.where(lane >= 128 + k, b, a), -k, 1)


def diff_z(f, sub):
    up = jnp.where(sub == 7, f, pltpu.roll(f, 7, 0))
    down = jnp.where(sub == 0, f, pltpu.roll(f, 1, 0))
    return up - down


def strain(dx, dy, dz):
    d = (dx, dy, dz)
    s = [0.5 * d[i][i] for i in range(3)] + [0.25 * (d[j][i] + d[i][j]) for i, j in PAIRS[3:]]
    diag = s[0] * s[0] + s[1] * s[1] + s[2] * s[2]
    off = s[3] * s[3] + s[4] * s[4] + s[5] * s[5]
    return s, jnp.sqrt(2.0 * diag + 4.0 * off)


def contract(a, b):
    return (a[0] * b[0] + a[1] * b[1] + a[2] * b[2]) + 2.0 * (a[3] * b[3] + a[4] * b[4] + a[5] * b[5])


def relax_weight(product):
    inverse = lax.rsqrt(lax.rsqrt(lax.rsqrt(jnp.maximum(product, PRODUCT_FLOOR))))
    return 1.0 / (1.0 + (1.0 / RATE_SCALE) * inverse)


def main_kernel(vel_ref, solid_ref, clip_ref, lo_ref, wrap_ref, hi_ref, relay_ref, far_ref, wide_ref, side_ref,
                near_ref, src_ref, lq_ref, mn_ref, two_ref, stress_ref, new_ref, scratch, old):
    lane = lax.broadcasted_iota(jnp.int32, (8, 128), 1)
    sub = lax.broadcasted_iota(jnp.int32, (8, 128), 0)
    run, even = place()
    here = lax.broadcasted_iota(jnp.int32, (64, 16), 0) % 8
    back = (lax.axis_index("gx") * 8 + here - src_ref[...] + 512) & 255
    spread = (lax.broadcasted_iota(jnp.int32, (16, 128), 1) // 8 == lax.broadcasted_iota(jnp.int32, (16, 128), 0))
    local = jnp.dot((16 + here - back).astype(F32), spread.astype(F32), preferred_element_type=F32)
    local = (local + 0.5).astype(jnp.int32)
    tile = lo_ref[pl.ds(96, 256), :].astype(F32) + lo_ref[pl.ds(352, 256), :].astype(F32)
    wrap = wrap_ref[pl.ds(96, 256), :].astype(F32) + wrap_ref[pl.ds(352, 256), :].astype(F32)
    up1 = jnp.where(run == 0, wrap, tile).reshape(4, 64, 128)
    up2 = decode(two_ref[...]).reshape(4, 64, 128)
    for z in range(8):
        at = pl.ds(8 * z, 8)
        idx = local[8 * z : 8 * z + 8]
        inner = idx & 7
        for f in range(4):
            own_ref = lq_ref if f < 2 else mn_ref
            own = own_ref[pl.ds(64 * (f % 2) + 8 * z, 8), :]
            got = jnp.take_along_axis(own, inner, axis=0)
            one = jnp.take_along_axis(up1[f, 8 * z : 8 * z + 8], inner, axis=0)
            two = jnp.take_along_axis(up2[f, 8 * z : 8 * z + 8], inner, axis=0)
            old[f, at, :] = jnp.where(idx < 8, two, jnp.where(idx < 16, one, got))
    lo = jnp.where(run == 0, lead(wrap_ref, 96), lead(lo_ref, 96))
    hi = jnp.where(run == 7, lead(relay_ref, 96), lead(hi_ref, 96))
    core = all_rows(own_rows(vel_ref, solid_ref, scratch), lo, hi)
    near = near_ref[...].astype(F32).reshape(4, 8, 128)
    far = jnp.where(run == 0, wide_ref[pl.ds(96, 32), :].astype(F32), far_ref[...].astype(F32)).reshape(4, 8, 128)
    below = lead(side_ref, 96).reshape(3, 4, 8, 128)
    above = relay_ref[pl.ds(96, 96), :].astype(F32).reshape(3, 4, 8, 128)
    edge = []
    for c in range(3):
        left = jnp.where(even, far[c], near[c])
        right = jnp.where(even, near[c], far[c])
        rows = []
        for i in range(14):
            r = pltpu.roll(right, 128 - 4 * i, 1) if i else right
            l = pltpu.roll(left, 124 - 4 * i, 1)
            value = jnp.where(lane < 64, r, l)
            if i < 3:
                value = jnp.where((run == 0) & ((lane >= 64) == even), below[c, i + 1], value)
            if i > 10:
                value = jnp.where((run == 7) & ((lane >= 64) == even), above[c, i - 11], value)
            rows.append(value)
        edge.append(rows)
    vn, vw, vdn, vdw = ([[None] * 14 for _ in range(3)] for _ in range(4))
    near_y = [[None] * 14 for _ in range(3)]
    for c in range(3):
        for i in range(14):
            a, b = core[c][i], edge[c][i]
            p1, m1 = shift_y(a, b, 1, lane), shift_y(a, b, -1, lane)
            p2, m2 = shift_y(a, b, 2, lane), shift_y(a, b, -2, lane)
            s1, d1, s2, d2 = p1 + m1, p1 - m1, p2 + m2, p2 - m2
            near_y[c][i] = d1
            if 1 <= i <= 12:
                vn[c][i] = a + a + s1
            t = a + s1
            vw[c][i] = t + t + s2
            if 2 <= i <= 11:
                vdn[c][i] = d1 + d1 + d2
            if 1 <= i <= 12:
                d3 = shift_y(a, b, 3, lane) - shift_y(a, b, -3, lane)
                vdw[c][i] = d1 + d2 + d2 + d3
    yn, yw = [None] * 14, [None] * 14
    own_flux = [None] * 14
    for i in range(1, 13):
        flux = []
        for t, o in ((core, edge), (edge, core)):
            dx = [t[c][i + 1] - t[c][i - 1] for c in range(3)]
            if t is core:
                dy = [near_y[c][i] for c in range(3)]
            else:
                dy = [shift_y(t[c][i], o[c][i], 1, lane) - shift_y(t[c][i], o[c][i], -1, lane) for c in range(3)]
            dz = [diff_z(t[c][i], sub) for c in range(3)]
            s, mag = strain(dx, dy, dz)
            prods = [t[p][i] * t[q][i] for p, q in PAIRS]
            flux.append(prods + [mag * e for e in s])
        own_flux[i] = flux[0][6:]
        ns, ws = [], []
        for a, b in zip(*flux):
            s1 = shift_y(a, b, 1, lane) + shift_y(a, b, -1, lane)
            s2 = shift_y(a, b, 2, lane) + shift_y(a, b, -2, lane)
            t = a + s1
            ns.append(a + t)
            ws.append(t + t + s2)
        yn[i], yw[i] = ns, ws

    def filt_n(r, i):
        return (r[i - 1] + r[i + 1] + (r[i] + r[i])) * 0.0625

    def filt_w(r, i):
        t = r[i - 1] + r[i] + r[i + 1]
        return (r[i - 2] + r[i + 2] + (t + t)) * 0.015625

    def column(r, k):
        return [None if v is None else v[k] for v in r]

    un = [[filt_n(vn[c], i) if 2 <= i <= 11 else None for i in range(14)] for c in range(3)]
    uw = [[filt_w(vw[c], i) if 2 <= i <= 11 else None for i in range(14)] for c in range(3)]
    for x in range(8):
        i = x + 3
        result = []
        for u, ydiff, filt, flux, factor in ((un, vdn, filt_n, yn, 4.0), (uw, vdw, filt_w, yw, 16.0)):
            dx = [u[c][i + 1] - u[c][i - 1] for c in range(3)]
            dy = [filt(ydiff[c], i) for c in range(3)]
            dz = [diff_z(u[c][i], sub) for c in range(3)]
            s, mag = strain(dx, dy, dz)
            f = [filt(column(flux, k), i) for k in range(12)]
            lhs = [f[k] - u[p][i] * u[q][i] for k, (p, q) in enumerate(PAIRS)]
            fm = factor * mag
            rhs = [f[6 + k] - fm * s[k] for k in range(6)]
            result.append((2.0 * contract(lhs, rhs), 4.0 * contract(rhs, rhs)))
        (lm, mm), (qn, nn) = result
        o_lm, o_qn, o_mm, o_nn = (row(old, x, f) for f in range(4))
        wn = relax_weight(o_lm * o_mm)
        ww = relax_weight(o_qn * o_nn)
        new_lm = wn * lm + (1.0 - wn) * o_lm
        new_mm = wn * mm + (1.0 - wn) * o_mm
        new_qn = ww * qn + (1.0 - ww) * o_qn
        new_nn = ww * nn + (1.0 - ww) * o_nn
        c2 = jnp.maximum(new_lm, 0.0) / new_mm
        c4 = jnp.maximum(new_qn, 0.0) / new_nn
        cs = c2 * c2 / jnp.maximum(jnp.maximum(c4, 0.125 * c2), RATIO_FLOOR)
        cs = jnp.where(row(clip_ref, x) == 1, jnp.minimum(cs, CLIP_CAP), cs)
        cs = jnp.where(row(solid_ref, x) == 1, 0.0, -2.0 * cs)
        at = (pl.ds(x, 8, stride=8), slice(None))
        for k in range(6):
            stress_ref[(k,) + at] = cs * own_flux[i][k]
        for k, v in enumerate((new_lm, new_mm, new_qn, new_nn)):
            new_ref[(k,) + at] = v


VM = pl.BlockSpec(memory_space=pltpu.VMEM)
HBM = pl.BlockSpec(memory_space=pltpu.HBM)


def call(kernel, outs, specs, scratch, limit=VMEM_LIMIT, flops=0):
    return pl.pallas_call(
        kernel, out_shape=outs, in_specs=specs, out_specs=[VM] * len(outs), scratch_shapes=scratch,
        compiler_params=pltpu.CompilerParams(vmem_limit_bytes=limit),
        cost_estimate=pl.CostEstimate(flops=flops, bytes_accessed=400_000, transcendentals=0),
    )


def far_side(gy):
    return (gy + 1) % 16 if gy % 2 else (gy - 1) % 16


def send(x, target):
    pairs = []
    for gx in range(32):
        for gy in range(16):
            to = target(gx % 8, gx, gy)
            if to is not None:
                pairs.append((gx * 16 + gy, to[0] % 32 * 16 + to[1]))
    return lax.ppermute(x, ("gx", "gy"), pairs)


def local(velocity, kept_lm_qn, kept_mm_nn, back_src, solid_flags, clip_flags):
    sds = jax.ShapeDtypeStruct
    vel = velocity.reshape(3, 64, 128)
    solid = solid_flags.reshape(64, 128)
    clip = clip_flags.reshape(64, 128)
    lq = kept_lm_qn.reshape(128, 128)
    mn = kept_mm_nn.reshape(128, 128)
    src = back_src.reshape(64, 16)
    strip_type = sds((32, 128), BF16)
    code_type = sds((256, 128), jnp.int16)
    trans = pltpu.VMEM((3, 64, 128), F32)
    tail, head, side, code = call(
        pack_kernel,
        [sds((608, 128), BF16), sds((96, 128), BF16), sds((SIDE, 128), BF16), code_type],
        [HBM] * 4,
        [pltpu.VMEM((3, 64, 128), BF16), pltpu.VMEM((64, 128), jnp.int32), pltpu.VMEM((256, 128), F32),
         trans, pltpu.SemaphoreType.DMA((4,))],
        PACK_LIMIT,
    )(vel, solid, lq, mn)
    lo = send(tail, lambda run, gx, gy: (gx + 1, gy) if run < 7 else None)
    hi = send(head, lambda run, gx, gy: (gx - 1, gy) if run > 0 else None)
    side = send(side, lambda run, gx, gy: (gx + 1, far_side(gy)) if run == 7 else None)
    wrap = send(tail, lambda run, gx, gy: (gx + 1, gy) if run == 7 else None)
    two = send(code, lambda run, gx, gy: (gx + 2, gy))
    wide, strip = call(far_kernel, [sds((128, 128), BF16), strip_type], [VM] * 4, [trans], flops=BIG)(vel, solid, lo, hi)
    wide = send(wide, lambda run, gx, gy: (gx, far_side(gy)) if run == 0 else None)
    relay, strip = call(relay_kernel, [sds((192, 128), BF16), strip_type], [VM] * 5, [])(wide, strip, head, side, two)
    relay = send(relay, lambda run, gx, gy: (gx - 1, far_side(gy)) if run == 0 else None)
    far = send(strip, lambda run, gx, gy: (gx, far_side(gy)) if run > 0 else None)
    (near,) = call(near_kernel, [strip_type], [VM] * 6, [trans])(vel, solid, lo, wrap, hi, relay)
    near = send(near, lambda run, gx, gy: (gx, gy ^ 1))
    stress, new = call(
        main_kernel, [sds((6, 64, 128), F32), sds((4, 64, 128), F32)], [VM] * 15, [trans, pltpu.VMEM((4, 64, 128), F32)],
    )(vel, solid, clip, lo, wrap, hi, relay, far, wide, side, near, src, lq, mn, two)
    return stress.reshape(6, 8, 8, 128), new.reshape(4, 8, 8, 128)


def solution(mesh):
    in_specs = (
        P(None, None, "gx", "gy"),
        P(None, None, "gx", "gy"),
        P(None, None, "gx", "gy"),
        P(None, "gx", "gy"),
        P(None, "gx", "gy"),
        P(None, "gx", "gy"),
    )
    out_specs = (P(None, None, "gx", "gy"), P(None, None, "gx", "gy"))
    return jax.shard_map(local, mesh=mesh, in_specs=in_specs, out_specs=out_specs, check_vma=False)
```

```python
import jax
import jax.numpy as jnp
from jax import lax
from jax.experimental import pallas as pl
from jax.experimental.pallas import tpu as pltpu
from jax.sharding import PartitionSpec as P

PRODUCT_FLOOR = 0.05
RATE_SCALE = 0.5
CLIP_CAP = 0.1
RATIO_FLOOR = 0.02
PAIRS = ((0, 0), (1, 1), (2, 2), (0, 1), (0, 2), (1, 2))
KEPT_SCALE = 32767.0 / 1.4142137
F32 = jnp.float32
BF16 = jnp.bfloat16
VMEM_LIMIT = 32 * 1024 * 1024
PACK_LIMIT = 60 * 1024 * 1024
BIG = 1_000_000_000
SIDE = 256


def row(ref, x, lead=None):
    at = (pl.ds(x, 8, stride=8), slice(None))
    return ref[at] if lead is None else ref[(lead,) + at]


def encode(x):
    root = jnp.sqrt(jnp.sqrt(jnp.abs(x)))
    scaled = jnp.where(x < 0, -root, root) * KEPT_SCALE
    return jnp.round(scaled).astype(jnp.int32).astype(jnp.int16)


def decode(code):
    y = code.astype(jnp.int32).astype(F32) * (1.0 / KEPT_SCALE)
    y2 = y * y
    return jnp.where(y < 0, -y2, y2) * y2


def place():
    return lax.axis_index("gx") & 7, (lax.axis_index("gy") & 1) == 0


def edges(rows, first):
    lane = lax.broadcasted_iota(jnp.int32, (8, 128), 1)
    left, right = [], []
    for c in range(3):
        lefts = jnp.zeros((8, 128), F32)
        rights = jnp.zeros((8, 128), F32)
        for k, value in enumerate(rows[c]):
            i = first + k
            here = (lane >= 4 * i) & (lane < 4 * i + 4)
            lefts = jnp.where(here, pltpu.roll(value, 4 * i, 1) if i else value, lefts)
            rights = jnp.where(here, pltpu.roll(value, 4 * i + 4, 1), rights)
        left.append(lefts)
        right.append(rights)
    none = [jnp.zeros((8, 128), F32)]
    return jnp.concatenate(left + none, axis=0), jnp.concatenate(right + none, axis=0)


def own_rows(vel_ref, solid_ref, scratch):
    inside = solid_ref[...] == 1
    for c in range(3):
        scratch[c] = jnp.where(inside, 0.0, vel_ref[c].astype(F32))
    return [[row(scratch, x, c) for x in range(8)] for c in range(3)]


def pack_kernel(vel_hbm, solid_hbm, lq_hbm, mn_hbm, tail_ref, head_ref, side_ref, code_ref,
                vel, solid, kept, scratch, sems):
    copies = [
        pltpu.make_async_copy(vel_hbm, vel, sems.at[0]),
        pltpu.make_async_copy(solid_hbm, solid, sems.at[1]),
        pltpu.make_async_copy(lq_hbm, kept.at[pl.ds(0, 128)], sems.at[2]),
        pltpu.make_async_copy(mn_hbm, kept.at[pl.ds(128, 128)], sems.at[3]),
    ]
    for copy in copies:
        copy.start()
    copies[0].wait()
    copies[1].wait()
    rows = own_rows(vel, solid, scratch)
    head_ref[...] = jnp.concatenate([rows[c][x] for c in range(3) for x in range(4)], axis=0).astype(BF16)
    tail = jnp.concatenate([rows[c][4 + x] for c in range(3) for x in range(4)], axis=0).astype(BF16)
    tail_ref[pl.ds(0, 96), :] = tail
    side_ref[pl.ds(0, 96), :] = tail
    side_ref[pl.ds(96, SIDE - 96), :] = jnp.zeros((SIDE - 96, 128), BF16)
    copies[2].wait()
    copies[3].wait()
    old = kept[...]
    code_ref[...] = encode(old)
    high = old.astype(BF16)
    tail_ref[pl.ds(96, 256), :] = high
    tail_ref[pl.ds(352, 256), :] = (old - high.astype(F32)).astype(BF16)


def all_rows(own, lo, hi):
    lo = lo.reshape(3, 4, 8, 128)
    hi = hi.reshape(3, 4, 8, 128)
    out = []
    for c in range(3):
        rows = [lo[c, x] for x in (1, 2, 3)]
        rows += own[c]
        rows += [hi[c, x] for x in (0, 1, 2)]
        out.append(rows)
    return out


def lead(ref, n):
    return ref[pl.ds(0, n), :].astype(F32)


def far_kernel(vel_ref, solid_ref, lo_ref, hi_ref, wide_ref, strip_ref, scratch):
    own = own_rows(vel_ref, solid_ref, scratch)
    rows = all_rows(own, lead(lo_ref, 96), lead(hi_ref, 96))
    left, right = edges(rows, 0)
    _, even = place()
    strip = jnp.where(even, left, right).astype(BF16)
    strip_ref[...] = strip
    wide_ref[pl.ds(96, 32), :] = strip
    wide_ref[pl.ds(0, 96), :] = jnp.concatenate([own[c][x] for c in range(3) for x in range(4)], axis=0).astype(BF16)


def relay_kernel(wide_ref, strip_ref, head_ref, side_ref, two_ref, relay_ref, strip_out):
    relay_ref[pl.ds(0, 96), :] = wide_ref[pl.ds(0, 96), :]
    relay_ref[pl.ds(96, 96), :] = head_ref[...]
    strip_out[...] = strip_ref[...]


def near_kernel(vel_ref, solid_ref, lo_ref, wrap_ref, hi_ref, relay_ref, strip_ref, scratch):
    at, even = place()
    own = own_rows(vel_ref, solid_ref, scratch)
    lo = jnp.where(at == 0, lead(wrap_ref, 96), lead(lo_ref, 96))
    hi = jnp.where(at == 7, lead(relay_ref, 96), lead(hi_ref, 96))
    left, right = edges(all_rows(own, lo, hi), 0)
    strip_ref[...] = jnp.where(even, right, left).astype(BF16)


def shift_y(a, b, k, lane):
    if k > 0:
        return pltpu.roll(jnp.where(lane < k, b, a), 128 - k, 1)
    return pltpu.roll(jnp.where(lane >= 128 + k, b, a), -k, 1)


def diff_z(f, sub):
    up = jnp.where(sub == 7, f, pltpu.roll(f, 7, 0))
    down = jnp.where(sub == 0, f, pltpu.roll(f, 1, 0))
    return up - down


def strain(dx, dy, dz):
    d = (dx, dy, dz)
    s = [0.5 * d[i][i] for i in range(3)] + [0.25 * (d[j][i] + d[i][j]) for i, j in PAIRS[3:]]
    diag = s[0] * s[0] + s[1] * s[1] + s[2] * s[2]
    off = s[3] * s[3] + s[4] * s[4] + s[5] * s[5]
    return s, jnp.sqrt(2.0 * diag + 4.0 * off)


def contract(a, b):
    return (a[0] * b[0] + a[1] * b[1] + a[2] * b[2]) + 2.0 * (a[3] * b[3] + a[4] * b[4] + a[5] * b[5])


def relax_weight(product):
    inverse = lax.rsqrt(lax.rsqrt(lax.rsqrt(jnp.maximum(product, PRODUCT_FLOOR))))
    return 1.0 / (1.0 + (1.0 / RATE_SCALE) * inverse)


def main_kernel(vel_ref, solid_ref, clip_ref, lo_ref, wrap_ref, hi_ref, relay_ref, far_ref, wide_ref, side_ref,
                near_ref, src_ref, lq_ref, mn_ref, two_ref, two_wrap_ref, stress_ref, new_ref, scratch, old):
    lane = lax.broadcasted_iota(jnp.int32, (8, 128), 1)
    sub = lax.broadcasted_iota(jnp.int32, (8, 128), 0)
    run, even = place()
    here = lax.broadcasted_iota(jnp.int32, (64, 16), 0) % 8
    back = (lax.axis_index("gx") * 8 + here - src_ref[...] + 512) & 255
    spread = (lax.broadcasted_iota(jnp.int32, (16, 128), 1) // 8 == lax.broadcasted_iota(jnp.int32, (16, 128), 0))
    local = jnp.dot((16 + here - back).astype(F32), spread.astype(F32), preferred_element_type=F32)
    local = (local + 0.5).astype(jnp.int32)
    tile = lo_ref[pl.ds(96, 256), :].astype(F32) + lo_ref[pl.ds(352, 256), :].astype(F32)
    wrap = wrap_ref[pl.ds(96, 256), :].astype(F32) + wrap_ref[pl.ds(352, 256), :].astype(F32)
    up1 = jnp.where(run == 0, wrap, tile).reshape(4, 64, 128)
    up2 = decode(jnp.where(run == 0, two_wrap_ref[...].astype(jnp.int32), two_ref[...].astype(jnp.int32))).reshape(4, 64, 128)
    for z in range(8):
        at = pl.ds(8 * z, 8)
        idx = local[8 * z : 8 * z + 8]
        inner = idx & 7
        for f in range(4):
            own_ref = lq_ref if f < 2 else mn_ref
            own = own_ref[pl.ds(64 * (f % 2) + 8 * z, 8), :]
            got = jnp.take_along_axis(own, inner, axis=0)
            one = jnp.take_along_axis(up1[f, 8 * z : 8 * z + 8], inner, axis=0)
            two = jnp.take_along_axis(up2[f, 8 * z : 8 * z + 8], inner, axis=0)
            old[f, at, :] = jnp.where(idx < 8, two, jnp.where(idx < 16, one, got))
    lo = jnp.where(run == 0, lead(wrap_ref, 96), lead(lo_ref, 96))
    hi = jnp.where(run == 7, lead(relay_ref, 96), lead(hi_ref, 96))
    core = all_rows(own_rows(vel_ref, solid_ref, scratch), lo, hi)
    near = near_ref[...].astype(F32).reshape(4, 8, 128)
    far = jnp.where(run == 0, wide_ref[pl.ds(96, 32), :].astype(F32), far_ref[...].astype(F32)).reshape(4, 8, 128)
    below = lead(side_ref, 96).reshape(3, 4, 8, 128)
    above = relay_ref[pl.ds(96, 96), :].astype(F32).reshape(3, 4, 8, 128)
    edge = []
    for c in range(3):
        left = jnp.where(even, far[c], near[c])
        right = jnp.where(even, near[c], far[c])
        rows = []
        for i in range(14):
            r = pltpu.roll(right, 128 - 4 * i, 1) if i else right
            l = pltpu.roll(left, 124 - 4 * i, 1)
            value = jnp.where(lane < 64, r, l)
            if i < 3:
                value = jnp.where((run == 0) & ((lane >= 64) == even), below[c, i + 1], value)
            if i > 10:
                value = jnp.where((run == 7) & ((lane >= 64) == even), above[c, i - 11], value)
            rows.append(value)
        edge.append(rows)
    vn, vw, vdn, vdw = ([[None] * 14 for _ in range(3)] for _ in range(4))
    near_y = [[None] * 14 for _ in range(3)]
    for c in range(3):
        for i in range(14):
            a, b = core[c][i], edge[c][i]
            p1, m1 = shift_y(a, b, 1, lane), shift_y(a, b, -1, lane)
            p2, m2 = shift_y(a, b, 2, lane), shift_y(a, b, -2, lane)
            s1, d1, s2, d2 = p1 + m1, p1 - m1, p2 + m2, p2 - m2
            near_y[c][i] = d1
            if 1 <= i <= 12:
                vn[c][i] = a + a + s1
            t = a + s1
            vw[c][i] = t + t + s2
            if 2 <= i <= 11:
                vdn[c][i] = d1 + d1 + d2
            if 1 <= i <= 12:
                d3 = shift_y(a, b, 3, lane) - shift_y(a, b, -3, lane)
                vdw[c][i] = d1 + d2 + d2 + d3
    yn, yw = [None] * 14, [None] * 14
    own_flux = [None] * 14
    for i in range(1, 13):
        flux = []
        for t, o in ((core, edge), (edge, core)):
            dx = [t[c][i + 1] - t[c][i - 1] for c in range(3)]
            if t is core:
                dy = [near_y[c][i] for c in range(3)]
            else:
                dy = [shift_y(t[c][i], o[c][i], 1, lane) - shift_y(t[c][i], o[c][i], -1, lane) for c in range(3)]
            dz = [diff_z(t[c][i], sub) for c in range(3)]
            s, mag = strain(dx, dy, dz)
            prods = [t[p][i] * t[q][i] for p, q in PAIRS]
            flux.append(prods + [mag * e for e in s])
        own_flux[i] = flux[0][6:]
        ns, ws = [], []
        for a, b in zip(*flux):
            s1 = shift_y(a, b, 1, lane) + shift_y(a, b, -1, lane)
            s2 = shift_y(a, b, 2, lane) + shift_y(a, b, -2, lane)
            t = a + s1
            ns.append(a + t)
            ws.append(t + t + s2)
        yn[i], yw[i] = ns, ws

    def filt_n(r, i):
        return (r[i - 1] + r[i + 1] + (r[i] + r[i])) * 0.0625

    def filt_w(r, i):
        t = r[i - 1] + r[i] + r[i + 1]
        return (r[i - 2] + r[i + 2] + (t + t)) * 0.015625

    def column(r, k):
        return [None if v is None else v[k] for v in r]

    un = [[filt_n(vn[c], i) if 2 <= i <= 11 else None for i in range(14)] for c in range(3)]
    uw = [[filt_w(vw[c], i) if 2 <= i <= 11 else None for i in range(14)] for c in range(3)]
    for x in range(8):
        i = x + 3
        result = []
        for u, ydiff, filt, flux, factor in ((un, vdn, filt_n, yn, 4.0), (uw, vdw, filt_w, yw, 16.0)):
            dx = [u[c][i + 1] - u[c][i - 1] for c in range(3)]
            dy = [filt(ydiff[c], i) for c in range(3)]
            dz = [diff_z(u[c][i], sub) for c in range(3)]
            s, mag = strain(dx, dy, dz)
            f = [filt(column(flux, k), i) for k in range(12)]
            lhs = [f[k] - u[p][i] * u[q][i] for k, (p, q) in enumerate(PAIRS)]
            fm = factor * mag
            rhs = [f[6 + k] - fm * s[k] for k in range(6)]
            result.append((2.0 * contract(lhs, rhs), 4.0 * contract(rhs, rhs)))
        (lm, mm), (qn, nn) = result
        o_lm, o_qn, o_mm, o_nn = (row(old, x, f) for f in range(4))
        wn = relax_weight(o_lm * o_mm)
        ww = relax_weight(o_qn * o_nn)
        new_lm = wn * lm + (1.0 - wn) * o_lm
        new_mm = wn * mm + (1.0 - wn) * o_mm
        new_qn = ww * qn + (1.0 - ww) * o_qn
        new_nn = ww * nn + (1.0 - ww) * o_nn
        c2 = jnp.maximum(new_lm, 0.0) / new_mm
        c4 = jnp.maximum(new_qn, 0.0) / new_nn
        cs = c2 * c2 / jnp.maximum(jnp.maximum(c4, 0.125 * c2), RATIO_FLOOR)
        cs = jnp.where(row(clip_ref, x) == 1, jnp.minimum(cs, CLIP_CAP), cs)
        cs = jnp.where(row(solid_ref, x) == 1, 0.0, -2.0 * cs)
        at = (pl.ds(x, 8, stride=8), slice(None))
        for k in range(6):
            stress_ref[(k,) + at] = cs * own_flux[i][k]
        for k, v in enumerate((new_lm, new_mm, new_qn, new_nn)):
            new_ref[(k,) + at] = v


VM = pl.BlockSpec(memory_space=pltpu.VMEM)
HBM = pl.BlockSpec(memory_space=pltpu.HBM)


def call(kernel, outs, specs, scratch, limit=VMEM_LIMIT, flops=0):
    return pl.pallas_call(
        kernel, out_shape=outs, in_specs=specs, out_specs=[VM] * len(outs), scratch_shapes=scratch,
        compiler_params=pltpu.CompilerParams(vmem_limit_bytes=limit),
        cost_estimate=pl.CostEstimate(flops=flops, bytes_accessed=400_000, transcendentals=0),
    )


def far_side(gy):
    return (gy + 1) % 16 if gy % 2 else (gy - 1) % 16


def send(x, target):
    pairs = []
    for gx in range(32):
        for gy in range(16):
            to = target(gx % 8, gx, gy)
            if to is not None:
                pairs.append((gx * 16 + gy, to[0] % 32 * 16 + to[1]))
    return lax.ppermute(x, ("gx", "gy"), pairs)


def local(velocity, kept_lm_qn, kept_mm_nn, back_src, solid_flags, clip_flags):
    sds = jax.ShapeDtypeStruct
    vel = velocity.reshape(3, 64, 128)
    solid = solid_flags.reshape(64, 128)
    clip = clip_flags.reshape(64, 128)
    lq = kept_lm_qn.reshape(128, 128)
    mn = kept_mm_nn.reshape(128, 128)
    src = back_src.reshape(64, 16)
    strip_type = sds((32, 128), BF16)
    code_type = sds((256, 128), jnp.int16)
    trans = pltpu.VMEM((3, 64, 128), F32)
    tail, head, side, code = call(
        pack_kernel,
        [sds((608, 128), BF16), sds((96, 128), BF16), sds((SIDE, 128), BF16), code_type],
        [HBM] * 4,
        [pltpu.VMEM((3, 64, 128), BF16), pltpu.VMEM((64, 128), jnp.int32), pltpu.VMEM((256, 128), F32),
         trans, pltpu.SemaphoreType.DMA((4,))],
        PACK_LIMIT,
    )(vel, solid, lq, mn)
    lo = send(tail, lambda run, gx, gy: (gx + 1, gy) if run < 7 else None)
    hi = send(head, lambda run, gx, gy: (gx - 1, gy) if run > 0 else None)
    side = send(side, lambda run, gx, gy: (gx + 1, far_side(gy)) if run == 7 else None)
    wrap = send(tail, lambda run, gx, gy: (gx + 1, gy) if run == 7 else None)
    two_wrap = send(code, lambda run, gx, gy: (gx + 2, gy) if run == 6 else None)
    two = send(code, lambda run, gx, gy: (gx + 2, gy) if run != 6 else None)
    wide, strip = call(far_kernel, [sds((128, 128), BF16), strip_type], [VM] * 4, [trans], flops=BIG)(vel, solid, lo, hi)
    wide = send(wide, lambda run, gx, gy: (gx, far_side(gy)) if run == 0 else None)
    relay, strip = call(relay_kernel, [sds((192, 128), BF16), strip_type], [VM] * 5, [])(wide, strip, head, side, two_wrap)
    relay = send(relay, lambda run, gx, gy: (gx - 1, far_side(gy)) if run == 0 else None)
    far = send(strip, lambda run, gx, gy: (gx, far_side(gy)) if run > 0 else None)
    (near,) = call(near_kernel, [strip_type], [VM] * 6, [trans])(vel, solid, lo, wrap, hi, relay)
    near = send(near, lambda run, gx, gy: (gx, gy ^ 1))
    stress, new = call(
        main_kernel, [sds((6, 64, 128), F32), sds((4, 64, 128), F32)], [VM] * 16, [trans, pltpu.VMEM((4, 64, 128), F32)],
    )(vel, solid, clip, lo, wrap, hi, relay, far, wide, side, near, src, lq, mn, two, two_wrap)
    return stress.reshape(6, 8, 8, 128), new.reshape(4, 8, 8, 128)


def solution(mesh):
    in_specs = (
        P(None, None, "gx", "gy"),
        P(None, None, "gx", "gy"),
        P(None, None, "gx", "gy"),
        P(None, "gx", "gy"),
        P(None, "gx", "gy"),
        P(None, "gx", "gy"),
    )
    out_specs = (P(None, None, "gx", "gy"), P(None, None, "gx", "gy"))
    return jax.shard_map(local, mesh=mesh, in_specs=in_specs, out_specs=out_specs, check_vma=False)
```

```python
import jax
import jax.numpy as jnp
from jax import lax
from jax.experimental import pallas as pl
from jax.experimental.pallas import tpu as pltpu
from jax.sharding import PartitionSpec as P

PRODUCT_FLOOR = 0.05
RATE_SCALE = 0.5
CLIP_CAP = 0.1
RATIO_FLOOR = 0.02
PAIRS = ((0, 0), (1, 1), (2, 2), (0, 1), (0, 2), (1, 2))
KEPT_SCALE = 32767.0 / 1.4142137
F32 = jnp.float32
BF16 = jnp.bfloat16
VMEM_LIMIT = 32 * 1024 * 1024
PACK_LIMIT = 60 * 1024 * 1024
BIG = 1_000_000_000
SIDE = 256
ROWS_A = 7
ROWS_B = 4
ROWS_C = 2


def row(ref, x, lead=None):
    at = (pl.ds(x, 8, stride=8), slice(None))
    return ref[at] if lead is None else ref[(lead,) + at]


def encode(x):
    root = jnp.sqrt(jnp.sqrt(jnp.abs(x)))
    scaled = jnp.where(x < 0, -root, root) * KEPT_SCALE
    return jnp.round(scaled).astype(jnp.int32).astype(jnp.int16)


def decode(code):
    y = code.astype(jnp.int32).astype(F32) * (1.0 / KEPT_SCALE)
    y2 = y * y
    return jnp.where(y < 0, -y2, y2) * y2


def place():
    return lax.axis_index("gx") & 7, (lax.axis_index("gy") & 1) == 0


def edges(rows, first):
    lane = lax.broadcasted_iota(jnp.int32, (8, 128), 1)
    left, right = [], []
    for c in range(3):
        lefts = jnp.zeros((8, 128), F32)
        rights = jnp.zeros((8, 128), F32)
        for k, value in enumerate(rows[c]):
            i = first + k
            here = (lane >= 4 * i) & (lane < 4 * i + 4)
            lefts = jnp.where(here, pltpu.roll(value, 4 * i, 1) if i else value, lefts)
            rights = jnp.where(here, pltpu.roll(value, 4 * i + 4, 1), rights)
        left.append(lefts)
        right.append(rights)
    none = [jnp.zeros((8, 128), F32)]
    return jnp.concatenate(left + none, axis=0), jnp.concatenate(right + none, axis=0)


def own_rows(vel_ref, solid_ref, scratch):
    inside = solid_ref[...] == 1
    for c in range(3):
        scratch[c] = jnp.where(inside, 0.0, vel_ref[c].astype(F32))
    return [[row(scratch, x, c) for x in range(8)] for c in range(3)]


def pack_kernel(vel_hbm, solid_hbm, lq_hbm, mn_hbm, tail_ref, head_ref, side_ref, code_ref,
                vel, solid, kept, scratch, sems):
    copies = [
        pltpu.make_async_copy(vel_hbm, vel, sems.at[0]),
        pltpu.make_async_copy(solid_hbm, solid, sems.at[1]),
        pltpu.make_async_copy(lq_hbm, kept.at[pl.ds(0, 128)], sems.at[2]),
        pltpu.make_async_copy(mn_hbm, kept.at[pl.ds(128, 128)], sems.at[3]),
    ]
    for copy in copies:
        copy.start()
    copies[0].wait()
    copies[1].wait()
    rows = own_rows(vel, solid, scratch)
    head_ref[...] = jnp.concatenate([rows[c][x] for c in range(3) for x in range(4)], axis=0).astype(BF16)
    tail = jnp.concatenate([rows[c][4 + x] for c in range(3) for x in range(4)], axis=0).astype(BF16)
    tail_ref[pl.ds(0, 96), :] = tail
    side_ref[pl.ds(0, 96), :] = tail
    side_ref[pl.ds(96, SIDE - 96), :] = jnp.zeros((SIDE - 96, 128), BF16)
    copies[2].wait()
    copies[3].wait()
    old = kept[...]
    code_ref[...] = encode(old)
    high = old.astype(BF16)
    tail_ref[pl.ds(96, 256), :] = high
    tail_ref[pl.ds(352, 256), :] = (old - high.astype(F32)).astype(BF16)


def all_rows(own, lo, hi):
    lo = lo.reshape(3, 4, 8, 128)
    hi = hi.reshape(3, 4, 8, 128)
    out = []
    for c in range(3):
        rows = [lo[c, x] for x in (1, 2, 3)]
        rows += own[c]
        rows += [hi[c, x] for x in (0, 1, 2)]
        out.append(rows)
    return out


def lead(ref, n):
    return ref[pl.ds(0, n), :].astype(F32)


def wide_kernel(vel_ref, solid_ref, hi_ref, wide_ref, scratch):
    own = own_rows(vel_ref, solid_ref, scratch)
    hi = lead(hi_ref, 96)
    left, right = edges(all_rows(own, jnp.zeros_like(hi), hi), 0)
    _, even = place()
    wide_ref[pl.ds(96, 32), :] = jnp.where(even, left, right).astype(BF16)
    wide_ref[pl.ds(0, 96), :] = jnp.concatenate([own[c][x] for c in range(3) for x in range(4)], axis=0).astype(BF16)


def far_kernel(vel_ref, solid_ref, lo_ref, hi_ref, strip_ref, scratch):
    rows = all_rows(own_rows(vel_ref, solid_ref, scratch), lead(lo_ref, 96), lead(hi_ref, 96))
    left, right = edges(rows, 0)
    _, even = place()
    strip_ref[...] = jnp.where(even, left, right).astype(BF16)


def relay_kernel(wide_ref, strip_ref, head_ref, side_ref, two_ref, relay_ref, strip_out):
    relay_ref[pl.ds(0, 96), :] = wide_ref[pl.ds(0, 96), :]
    relay_ref[pl.ds(96, 96), :] = head_ref[...]
    strip_out[...] = strip_ref[...]


def near_kernel(vel_ref, solid_ref, lo_ref, wrap_ref, hi_ref, relay_ref, strip_ref, scratch):
    at, even = place()
    own = own_rows(vel_ref, solid_ref, scratch)
    lo = jnp.where(at == 0, lead(wrap_ref, 96), lead(lo_ref, 96))
    hi = jnp.where(at == 7, lead(relay_ref, 96), lead(hi_ref, 96))
    left, right = edges(all_rows(own, lo, hi), 0)
    strip_ref[...] = jnp.where(even, right, left).astype(BF16)


def shift_y(a, b, k, lane):
    if k > 0:
        return pltpu.roll(jnp.where(lane < k, b, a), 128 - k, a.ndim - 1)
    return pltpu.roll(jnp.where(lane >= 128 + k, b, a), -k, a.ndim - 1)


def diff_z(f, sub):
    up = jnp.where(sub == 7, f, pltpu.roll(f, 7, f.ndim - 2))
    down = jnp.where(sub == 0, f, pltpu.roll(f, 1, f.ndim - 2))
    return up - down


def strain(dx, dy, dz):
    d = (dx, dy, dz)
    s = [0.5 * d[i][i] for i in range(3)] + [0.25 * (d[j][i] + d[i][j]) for i, j in PAIRS[3:]]
    diag = s[0] * s[0] + s[1] * s[1] + s[2] * s[2]
    off = s[3] * s[3] + s[4] * s[4] + s[5] * s[5]
    return s, jnp.sqrt(2.0 * diag + 4.0 * off)


def contract(a, b):
    return (a[0] * b[0] + a[1] * b[1] + a[2] * b[2]) + 2.0 * (a[3] * b[3] + a[4] * b[4] + a[5] * b[5])


def relax_weight(product):
    inverse = lax.rsqrt(lax.rsqrt(lax.rsqrt(jnp.maximum(product, PRODUCT_FLOOR))))
    return 1.0 / (1.0 + (1.0 / RATE_SCALE) * inverse)


def main_kernel(vel_ref, solid_ref, clip_ref, lo_ref, wrap_ref, hi_ref, relay_ref, far_ref, wide_ref, side_ref,
                near_ref, src_ref, lq_ref, mn_ref, two_ref, two_wrap_ref, stress_ref, new_ref, scratch, old):
    lane = lax.broadcasted_iota(jnp.int32, (8, 128), 1)
    sub = lax.broadcasted_iota(jnp.int32, (8, 128), 0)
    run, even = place()
    here = lax.broadcasted_iota(jnp.int32, (64, 16), 0) % 8
    back = (lax.axis_index("gx") * 8 + here - src_ref[...] + 512) & 255
    spread = (lax.broadcasted_iota(jnp.int32, (16, 128), 1) // 8 == lax.broadcasted_iota(jnp.int32, (16, 128), 0))
    local = jnp.dot((16 + here - back).astype(F32), spread.astype(F32), preferred_element_type=F32)
    local = (local + 0.5).astype(jnp.int32)
    tile = lo_ref[pl.ds(96, 256), :].astype(F32) + lo_ref[pl.ds(352, 256), :].astype(F32)
    wrap = wrap_ref[pl.ds(96, 256), :].astype(F32) + wrap_ref[pl.ds(352, 256), :].astype(F32)
    up1 = jnp.where(run == 0, wrap, tile).reshape(4, 64, 128)
    up2 = decode(jnp.where(run == 0, two_wrap_ref[...].astype(jnp.int32), two_ref[...].astype(jnp.int32))).reshape(4, 64, 128)
    for z in range(8):
        at = pl.ds(8 * z, 8)
        idx = local[8 * z : 8 * z + 8]
        inner = idx & 7
        for f in range(4):
            own_ref = lq_ref if f < 2 else mn_ref
            own = own_ref[pl.ds(64 * (f % 2) + 8 * z, 8), :]
            got = jnp.take_along_axis(own, inner, axis=0)
            one = jnp.take_along_axis(up1[f, 8 * z : 8 * z + 8], inner, axis=0)
            two = jnp.take_along_axis(up2[f, 8 * z : 8 * z + 8], inner, axis=0)
            old[f, at, :] = jnp.where(idx < 8, two, jnp.where(idx < 16, one, got))
    lo = jnp.where(run == 0, lead(wrap_ref, 96), lead(lo_ref, 96))
    hi = jnp.where(run == 7, lead(relay_ref, 96), lead(hi_ref, 96))
    core = all_rows(own_rows(vel_ref, solid_ref, scratch), lo, hi)
    near = near_ref[...].astype(F32).reshape(4, 8, 128)
    far = jnp.where(run == 0, wide_ref[pl.ds(96, 32), :].astype(F32), far_ref[...].astype(F32)).reshape(4, 8, 128)
    lower = (lax.axis_index("gy") & 3) < 2
    below = jnp.where(lower, lead(side_ref, 96), lead(lo_ref, 96)).reshape(3, 4, 8, 128)
    above = relay_ref[pl.ds(96, 96), :].astype(F32).reshape(3, 4, 8, 128)
    edge = []
    for c in range(3):
        left = jnp.where(even, far[c], near[c])
        right = jnp.where(even, near[c], far[c])
        rows = []
        for i in range(14):
            r = pltpu.roll(right, 128 - 4 * i, 1) if i else right
            l = pltpu.roll(left, 124 - 4 * i, 1)
            value = jnp.where(lane < 64, r, l)
            if i < 3:
                value = jnp.where((run == 0) & ((lane >= 64) == even), below[c, i + 1], value)
            if i > 10:
                value = jnp.where((run == 7) & ((lane >= 64) == even), above[c, i - 11], value)
            rows.append(value)
        edge.append(jnp.stack(rows))
    core = [jnp.stack(rows) for rows in core]

    def chunks(first, last, size):
        return [(k, min(k + size, last)) for k in range(first, last, size)]

    flow = [[[] for _ in range(5)] for _ in range(3)]
    for lo_i, hi_i in chunks(0, 14, ROWS_A):
        for c in range(3):
            a, b = core[c][lo_i:hi_i], edge[c][lo_i:hi_i]
            p1, m1 = shift_y(a, b, 1, lane), shift_y(a, b, -1, lane)
            p2, m2 = shift_y(a, b, 2, lane), shift_y(a, b, -2, lane)
            p3, m3 = shift_y(a, b, 3, lane), shift_y(a, b, -3, lane)
            s1, d1, s2, d2 = p1 + m1, p1 - m1, p2 + m2, p2 - m2
            t = a + s1
            for k, v in enumerate((a + t, t + t + s2, d1 + d1 + d2, d1 + d2 + d2 + (p3 - m3), d1)):
                flow[c][k].append(v)
    flow = [[jnp.concatenate(v, axis=0) for v in per] for per in flow]
    yn, yw, own_flux = ([[] for _ in range(k)] for k in (12, 12, 6))
    for lo_i, hi_i in chunks(1, 13, ROWS_B):
        flux = []
        for t, o in ((core, edge), (edge, core)):
            mid = [t[c][lo_i:hi_i] for c in range(3)]
            dx = [t[c][lo_i + 1 : hi_i + 1] - t[c][lo_i - 1 : hi_i - 1] for c in range(3)]
            if t is core:
                dy = [flow[c][4][lo_i:hi_i] for c in range(3)]
            else:
                oth = [o[c][lo_i:hi_i] for c in range(3)]
                dy = [shift_y(mid[c], oth[c], 1, lane) - shift_y(mid[c], oth[c], -1, lane) for c in range(3)]
            dz = [diff_z(mid[c], sub) for c in range(3)]
            s, mag = strain(dx, dy, dz)
            flux.append([mid[p] * mid[q] for p, q in PAIRS] + [mag * e for e in s])
        for k in range(6):
            own_flux[k].append(flux[0][6 + k])
        for k, (a, b) in enumerate(zip(*flux)):
            s1 = shift_y(a, b, 1, lane) + shift_y(a, b, -1, lane)
            s2 = shift_y(a, b, 2, lane) + shift_y(a, b, -2, lane)
            t = a + s1
            yn[k].append(a + t)
            yw[k].append(t + t + s2)
    yn, yw, own_flux = ([jnp.concatenate(v, axis=0) for v in g] for g in (yn, yw, own_flux))

    def filt_n(r, base, lo_i, hi_i):
        at = lambda k: r[lo_i + k - base : hi_i + k - base]
        return (at(-1) + at(1) + (at(0) + at(0))) * 0.0625

    def filt_w(r, base, lo_i, hi_i):
        at = lambda k: r[lo_i + k - base : hi_i + k - base]
        t = at(-1) + at(0) + at(1)
        return (at(-2) + at(2) + (t + t)) * 0.015625

    un = [filt_n(flow[c][0], 0, 2, 12) for c in range(3)]
    uw = [filt_w(flow[c][1], 0, 2, 12) for c in range(3)]
    for lo_i, hi_i in chunks(3, 11, ROWS_C):
        result = []
        for u, which, filt, flux, factor in ((un, 2, filt_n, yn, 4.0), (uw, 3, filt_w, yw, 16.0)):
            mid = [u[c][lo_i - 2 : hi_i - 2] for c in range(3)]
            dx = [u[c][lo_i - 1 : hi_i - 1] - u[c][lo_i - 3 : hi_i - 3] for c in range(3)]
            dy = [filt(flow[c][which], 0, lo_i, hi_i) for c in range(3)]
            dz = [diff_z(mid[c], sub) for c in range(3)]
            s, mag = strain(dx, dy, dz)
            f = [filt(flux[k], 1, lo_i, hi_i) for k in range(12)]
            lhs = [f[k] - mid[p] * mid[q] for k, (p, q) in enumerate(PAIRS)]
            fm = factor * mag
            rhs = [f[6 + k] - fm * s[k] for k in range(6)]
            result.append((2.0 * contract(lhs, rhs), 4.0 * contract(rhs, rhs)))
        (lm, mm), (qn, nn) = result
        span = range(lo_i - 3, hi_i - 3)
        o_lm, o_qn, o_mm, o_nn = (jnp.stack([row(old, x, f) for x in span]) for f in range(4))
        wn = relax_weight(o_lm * o_mm)
        ww = relax_weight(o_qn * o_nn)
        new_lm = wn * lm + (1.0 - wn) * o_lm
        new_mm = wn * mm + (1.0 - wn) * o_mm
        new_qn = ww * qn + (1.0 - ww) * o_qn
        new_nn = ww * nn + (1.0 - ww) * o_nn
        c2 = jnp.maximum(new_lm, 0.0) / new_mm
        c4 = jnp.maximum(new_qn, 0.0) / new_nn
        cs = c2 * c2 / jnp.maximum(jnp.maximum(c4, 0.125 * c2), RATIO_FLOOR)
        clipped = jnp.stack([row(clip_ref, x) for x in span]) == 1
        blocked = jnp.stack([row(solid_ref, x) for x in span]) == 1
        cs = jnp.where(clipped, jnp.minimum(cs, CLIP_CAP), cs)
        cs = jnp.where(blocked, 0.0, -2.0 * cs)
        out = [cs * own_flux[k][lo_i - 1 : hi_i - 1] for k in range(6)]
        for j, x in enumerate(span):
            at = (pl.ds(x, 8, stride=8), slice(None))
            for k in range(6):
                stress_ref[(k,) + at] = out[k][j]
            for k, v in enumerate((new_lm, new_mm, new_qn, new_nn)):
                new_ref[(k,) + at] = v[j]


VM = pl.BlockSpec(memory_space=pltpu.VMEM)
HBM = pl.BlockSpec(memory_space=pltpu.HBM)


def call(kernel, outs, specs, scratch, limit=VMEM_LIMIT, flops=0):
    return pl.pallas_call(
        kernel, out_shape=outs, in_specs=specs, out_specs=[VM] * len(outs), scratch_shapes=scratch,
        compiler_params=pltpu.CompilerParams(vmem_limit_bytes=limit),
        cost_estimate=pl.CostEstimate(flops=flops, bytes_accessed=400_000, transcendentals=0),
    )


def far_side(gy):
    return (gy + 1) % 16 if gy % 2 else (gy - 1) % 16


def low(gy):
    return gy % 4 < 2


def send(x, target):
    pairs = []
    for gx in range(32):
        for gy in range(16):
            to = target(gx % 8, gx, gy)
            if to is not None:
                pairs.append((gx * 16 + gy, to[0] % 32 * 16 + to[1]))
    return lax.ppermute(x, ("gx", "gy"), pairs)


def local(velocity, kept_lm_qn, kept_mm_nn, back_src, solid_flags, clip_flags):
    sds = jax.ShapeDtypeStruct
    vel = velocity.reshape(3, 64, 128)
    solid = solid_flags.reshape(64, 128)
    clip = clip_flags.reshape(64, 128)
    lq = kept_lm_qn.reshape(128, 128)
    mn = kept_mm_nn.reshape(128, 128)
    src = back_src.reshape(64, 16)
    strip_type = sds((32, 128), BF16)
    code_type = sds((256, 128), jnp.int16)
    trans = pltpu.VMEM((3, 64, 128), F32)
    tail, head, side, code = call(
        pack_kernel,
        [sds((608, 128), BF16), sds((96, 128), BF16), sds((SIDE, 128), BF16), code_type],
        [HBM] * 4,
        [pltpu.VMEM((3, 64, 128), BF16), pltpu.VMEM((64, 128), jnp.int32), pltpu.VMEM((256, 128), F32),
         trans, pltpu.SemaphoreType.DMA((4,))],
        PACK_LIMIT,
    )(vel, solid, lq, mn)
    lo = send(tail, lambda run, gx, gy: (gx + 1, gy) if run < 7 else (gx + 1, far_side(gy)) if low(gy) else None)
    hi = send(head, lambda run, gx, gy: (gx - 1, gy) if run > 0 else None)
    side = send(side, lambda run, gx, gy: (gx + 1, far_side(gy)) if run == 7 and not low(gy) else None)
    wrap = send(tail, lambda run, gx, gy: (gx + 1, gy) if run == 7 else None)
    two_wrap = send(code, lambda run, gx, gy: (gx + 2, gy) if run == 6 else None)
    two = send(code, lambda run, gx, gy: (gx + 2, gy) if run != 6 else None)
    (wide,) = call(wide_kernel, [sds((128, 128), BF16)], [VM] * 3, [trans], flops=BIG)(vel, solid, hi)
    (strip,) = call(far_kernel, [strip_type], [VM] * 4, [trans])(vel, solid, lo, hi)
    wide = send(wide, lambda run, gx, gy: (gx, far_side(gy)) if run == 0 else None)
    relay, strip = call(relay_kernel, [sds((192, 128), BF16), strip_type], [VM] * 5, [])(wide, strip, head, side, two_wrap)
    relay = send(relay, lambda run, gx, gy: (gx - 1, far_side(gy)) if run == 0 else None)
    far = send(strip, lambda run, gx, gy: (gx, far_side(gy)) if run > 0 else None)
    (near,) = call(near_kernel, [strip_type], [VM] * 6, [trans])(vel, solid, lo, wrap, hi, relay)
    near = send(near, lambda run, gx, gy: (gx, gy ^ 1))
    stress, new = call(
        main_kernel, [sds((6, 64, 128), F32), sds((4, 64, 128), F32)], [VM] * 16, [trans, pltpu.VMEM((4, 64, 128), F32)],
    )(vel, solid, clip, lo, wrap, hi, relay, far, wide, side, near, src, lq, mn, two, two_wrap)
    return stress.reshape(6, 8, 8, 128), new.reshape(4, 8, 8, 128)


def solution(mesh):
    in_specs = (
        P(None, None, "gx", "gy"),
        P(None, None, "gx", "gy"),
        P(None, None, "gx", "gy"),
        P(None, "gx", "gy"),
        P(None, "gx", "gy"),
        P(None, "gx", "gy"),
    )
    out_specs = (P(None, None, "gx", "gy"), P(None, None, "gx", "gy"))
    return jax.shard_map(local, mesh=mesh, in_specs=in_specs, out_specs=out_specs, check_vma=False)
```

```python
import jax
import jax.numpy as jnp
from jax import lax
from jax.experimental import pallas as pl
from jax.experimental.pallas import tpu as pltpu
from jax.sharding import PartitionSpec as P

PRODUCT_FLOOR = 0.05
RATE_SCALE = 0.5
CLIP_CAP = 0.1
RATIO_FLOOR = 0.02
PAIRS = ((0, 0), (1, 1), (2, 2), (0, 1), (0, 2), (1, 2))
KEPT_SCALE = 32767.0 / 1.4142137
F32 = jnp.float32
BF16 = jnp.bfloat16
VMEM_LIMIT = 32 * 1024 * 1024
PACK_LIMIT = 60 * 1024 * 1024
BIG = 1_000_000_000
SIDE = 256
ROWS_A = 7
ROWS_B = 4
ROWS_C = 2


def row(ref, x, lead=None):
    at = (pl.ds(x, 8, stride=8), slice(None))
    return ref[at] if lead is None else ref[(lead,) + at]


def encode(x):
    root = jnp.sqrt(jnp.sqrt(jnp.abs(x)))
    scaled = jnp.where(x < 0, -root, root) * KEPT_SCALE
    return jnp.round(scaled).astype(jnp.int32).astype(jnp.int16)


def decode(code):
    y = code.astype(jnp.int32).astype(F32) * (1.0 / KEPT_SCALE)
    y2 = y * y
    return jnp.where(y < 0, -y2, y2) * y2


def place():
    return lax.axis_index("gx") & 7, (lax.axis_index("gy") & 1) == 0


def edges(rows, first):
    lane = lax.broadcasted_iota(jnp.int32, (8, 128), 1)
    left, right = [], []
    for c in range(3):
        lefts = jnp.zeros((8, 128), F32)
        rights = jnp.zeros((8, 128), F32)
        for k, value in enumerate(rows[c]):
            i = first + k
            here = (lane >= 4 * i) & (lane < 4 * i + 4)
            lefts = jnp.where(here, pltpu.roll(value, 4 * i, 1) if i else value, lefts)
            rights = jnp.where(here, pltpu.roll(value, 4 * i + 4, 1), rights)
        left.append(lefts)
        right.append(rights)
    none = [jnp.zeros((8, 128), F32)]
    return jnp.concatenate(left + none, axis=0), jnp.concatenate(right + none, axis=0)


def own_rows(vel_ref, solid_ref, scratch):
    inside = solid_ref[...] == 1
    for c in range(3):
        scratch[c] = jnp.where(inside, 0.0, vel_ref[c].astype(F32))
    return [[row(scratch, x, c) for x in range(8)] for c in range(3)]


def pack_kernel(vel_hbm, solid_hbm, lq_hbm, mn_hbm, tail_ref, head_ref, side_ref, code_ref,
                vel, solid, kept, scratch, sems):
    copies = [
        pltpu.make_async_copy(vel_hbm, vel, sems.at[0]),
        pltpu.make_async_copy(solid_hbm, solid, sems.at[1]),
        pltpu.make_async_copy(lq_hbm, kept.at[pl.ds(0, 128)], sems.at[2]),
        pltpu.make_async_copy(mn_hbm, kept.at[pl.ds(128, 128)], sems.at[3]),
    ]
    for copy in copies:
        copy.start()
    copies[0].wait()
    copies[1].wait()
    rows = own_rows(vel, solid, scratch)
    head_ref[...] = jnp.concatenate([rows[c][x] for c in range(3) for x in range(4)], axis=0).astype(BF16)
    tail = jnp.concatenate([rows[c][4 + x] for c in range(3) for x in range(4)], axis=0).astype(BF16)
    tail_ref[pl.ds(0, 96), :] = tail
    side_ref[pl.ds(0, 96), :] = tail
    side_ref[pl.ds(96, SIDE - 96), :] = jnp.zeros((SIDE - 96, 128), BF16)
    copies[2].wait()
    copies[3].wait()
    old = kept[...]
    code_ref[...] = encode(old)
    high = old.astype(BF16)
    tail_ref[pl.ds(96, 256), :] = high
    tail_ref[pl.ds(352, 256), :] = (old - high.astype(F32)).astype(BF16)


def all_rows(own, lo, hi):
    lo = lo.reshape(3, 4, 8, 128)
    hi = hi.reshape(3, 4, 8, 128)
    out = []
    for c in range(3):
        rows = [lo[c, x] for x in (1, 2, 3)]
        rows += own[c]
        rows += [hi[c, x] for x in (0, 1, 2)]
        out.append(rows)
    return out


def lead(ref, n):
    return ref[pl.ds(0, n), :].astype(F32)


def wide_kernel(vel_ref, solid_ref, hi_ref, wide_ref, scratch):
    own = own_rows(vel_ref, solid_ref, scratch)
    hi = lead(hi_ref, 96)
    left, right = edges(all_rows(own, jnp.zeros_like(hi), hi), 0)
    _, even = place()
    wide_ref[pl.ds(96, 32), :] = jnp.where(even, left, right).astype(BF16)
    wide_ref[pl.ds(0, 96), :] = jnp.concatenate([own[c][x] for c in range(3) for x in range(4)], axis=0).astype(BF16)


def far_kernel(vel_ref, solid_ref, lo_ref, hi_ref, strip_ref, scratch):
    rows = all_rows(own_rows(vel_ref, solid_ref, scratch), lead(lo_ref, 96), lead(hi_ref, 96))
    left, right = edges(rows, 0)
    _, even = place()
    strip_ref[...] = jnp.where(even, left, right).astype(BF16)


def relay_kernel(wide_ref, strip_ref, head_ref, side_ref, two_ref, relay_ref, strip_out):
    relay_ref[pl.ds(0, 96), :] = wide_ref[pl.ds(0, 96), :]
    relay_ref[pl.ds(96, 96), :] = head_ref[...]
    strip_out[...] = strip_ref[...]


def near_kernel(vel_ref, solid_ref, lo_ref, wrap_ref, hi_ref, relay_ref, strip_ref, scratch):
    at, even = place()
    own = own_rows(vel_ref, solid_ref, scratch)
    lo = jnp.where(at == 0, lead(wrap_ref, 96), lead(lo_ref, 96))
    hi = jnp.where(at == 7, lead(relay_ref, 96), lead(hi_ref, 96))
    left, right = edges(all_rows(own, lo, hi), 0)
    strip_ref[...] = jnp.where(even, right, left).astype(BF16)


def shift_y(a, b, k, lane):
    if k > 0:
        return pltpu.roll(jnp.where(lane < k, b, a), 128 - k, a.ndim - 1)
    return pltpu.roll(jnp.where(lane >= 128 + k, b, a), -k, a.ndim - 1)


def diff_z(f, sub):
    up = jnp.where(sub == 7, f, pltpu.roll(f, 7, f.ndim - 2))
    down = jnp.where(sub == 0, f, pltpu.roll(f, 1, f.ndim - 2))
    return up - down


def strain(dx, dy, dz):
    d = (dx, dy, dz)
    s = [0.5 * d[i][i] for i in range(3)] + [0.25 * (d[j][i] + d[i][j]) for i, j in PAIRS[3:]]
    diag = s[0] * s[0] + s[1] * s[1] + s[2] * s[2]
    off = s[3] * s[3] + s[4] * s[4] + s[5] * s[5]
    return s, jnp.sqrt(2.0 * diag + 4.0 * off)


def contract(a, b):
    return (a[0] * b[0] + a[1] * b[1] + a[2] * b[2]) + 2.0 * (a[3] * b[3] + a[4] * b[4] + a[5] * b[5])


def relax_weight(product):
    inverse = lax.rsqrt(lax.rsqrt(lax.rsqrt(jnp.maximum(product, PRODUCT_FLOOR))))
    return 1.0 / (1.0 + (1.0 / RATE_SCALE) * inverse)


def main_kernel(vel_ref, solid_ref, clip_ref, lo_ref, wrap_ref, hi_ref, relay_ref, far_ref, wide_ref, side_ref,
                near_ref, src_ref, lq_ref, mn_ref, two_ref, two_wrap_ref, stress_ref, new_ref, scratch, old):
    lane = lax.broadcasted_iota(jnp.int32, (8, 128), 1)
    sub = lax.broadcasted_iota(jnp.int32, (8, 128), 0)
    run, even = place()
    here = lax.broadcasted_iota(jnp.int32, (64, 16), 0) % 8
    back = (lax.axis_index("gx") * 8 + here - src_ref[...] + 512) & 255
    spread = (lax.broadcasted_iota(jnp.int32, (16, 128), 1) // 8 == lax.broadcasted_iota(jnp.int32, (16, 128), 0))
    local = jnp.dot((16 + here - back).astype(F32), spread.astype(F32), preferred_element_type=F32)
    local = (local + 0.5).astype(jnp.int32)
    tile = lo_ref[pl.ds(96, 256), :].astype(F32) + lo_ref[pl.ds(352, 256), :].astype(F32)
    wrap = wrap_ref[pl.ds(96, 256), :].astype(F32) + wrap_ref[pl.ds(352, 256), :].astype(F32)
    up1 = jnp.where(run == 0, wrap, tile).reshape(4, 64, 128)
    lower = (lax.axis_index("gy") & 3) < 2
    up2 = decode(jnp.where((run == 0) & lower, two_wrap_ref[...].astype(jnp.int32), two_ref[...].astype(jnp.int32))).reshape(4, 64, 128)
    for z in range(8):
        at = pl.ds(8 * z, 8)
        idx = local[8 * z : 8 * z + 8]
        inner = idx & 7
        for f in range(4):
            own_ref = lq_ref if f < 2 else mn_ref
            own = own_ref[pl.ds(64 * (f % 2) + 8 * z, 8), :]
            got = jnp.take_along_axis(own, inner, axis=0)
            one = jnp.take_along_axis(up1[f, 8 * z : 8 * z + 8], inner, axis=0)
            two = jnp.take_along_axis(up2[f, 8 * z : 8 * z + 8], inner, axis=0)
            old[f, at, :] = jnp.where(idx < 8, two, jnp.where(idx < 16, one, got))
    lo = jnp.where(run == 0, lead(wrap_ref, 96), lead(lo_ref, 96))
    hi = jnp.where(run == 7, lead(relay_ref, 96), lead(hi_ref, 96))
    core = all_rows(own_rows(vel_ref, solid_ref, scratch), lo, hi)
    near = near_ref[...].astype(F32).reshape(4, 8, 128)
    far = jnp.where(run == 0, wide_ref[pl.ds(96, 32), :].astype(F32), far_ref[...].astype(F32)).reshape(4, 8, 128)
    below = jnp.where(lower, lead(side_ref, 96), lead(lo_ref, 96)).reshape(3, 4, 8, 128)
    above = relay_ref[pl.ds(96, 96), :].astype(F32).reshape(3, 4, 8, 128)
    edge = []
    for c in range(3):
        left = jnp.where(even, far[c], near[c])
        right = jnp.where(even, near[c], far[c])
        rows = []
        for i in range(14):
            r = pltpu.roll(right, 128 - 4 * i, 1) if i else right
            l = pltpu.roll(left, 124 - 4 * i, 1)
            value = jnp.where(lane < 64, r, l)
            if i < 3:
                value = jnp.where((run == 0) & ((lane >= 64) == even), below[c, i + 1], value)
            if i > 10:
                value = jnp.where((run == 7) & ((lane >= 64) == even), above[c, i - 11], value)
            rows.append(value)
        edge.append(jnp.stack(rows))
    core = [jnp.stack(rows) for rows in core]

    def chunks(first, last, size):
        return [(k, min(k + size, last)) for k in range(first, last, size)]

    flow = [[[] for _ in range(5)] for _ in range(3)]
    for lo_i, hi_i in chunks(0, 14, ROWS_A):
        for c in range(3):
            a, b = core[c][lo_i:hi_i], edge[c][lo_i:hi_i]
            p1, m1 = shift_y(a, b, 1, lane), shift_y(a, b, -1, lane)
            p2, m2 = shift_y(a, b, 2, lane), shift_y(a, b, -2, lane)
            p3, m3 = shift_y(a, b, 3, lane), shift_y(a, b, -3, lane)
            s1, d1, s2, d2 = p1 + m1, p1 - m1, p2 + m2, p2 - m2
            t = a + s1
            for k, v in enumerate((a + t, t + t + s2, d1 + d1 + d2, d1 + d2 + d2 + (p3 - m3), d1)):
                flow[c][k].append(v)
    flow = [[jnp.concatenate(v, axis=0) for v in per] for per in flow]
    yn, yw, own_flux = ([[] for _ in range(k)] for k in (12, 12, 6))
    for lo_i, hi_i in chunks(1, 13, ROWS_B):
        flux = []
        for t, o in ((core, edge), (edge, core)):
            mid = [t[c][lo_i:hi_i] for c in range(3)]
            dx = [t[c][lo_i + 1 : hi_i + 1] - t[c][lo_i - 1 : hi_i - 1] for c in range(3)]
            if t is core:
                dy = [flow[c][4][lo_i:hi_i] for c in range(3)]
            else:
                oth = [o[c][lo_i:hi_i] for c in range(3)]
                dy = [shift_y(mid[c], oth[c], 1, lane) - shift_y(mid[c], oth[c], -1, lane) for c in range(3)]
            dz = [diff_z(mid[c], sub) for c in range(3)]
            s, mag = strain(dx, dy, dz)
            flux.append([mid[p] * mid[q] for p, q in PAIRS] + [mag * e for e in s])
        for k in range(6):
            own_flux[k].append(flux[0][6 + k])
        for k, (a, b) in enumerate(zip(*flux)):
            s1 = shift_y(a, b, 1, lane) + shift_y(a, b, -1, lane)
            s2 = shift_y(a, b, 2, lane) + shift_y(a, b, -2, lane)
            t = a + s1
            yn[k].append(a + t)
            yw[k].append(t + t + s2)
    yn, yw, own_flux = ([jnp.concatenate(v, axis=0) for v in g] for g in (yn, yw, own_flux))

    def filt_n(r, base, lo_i, hi_i):
        at = lambda k: r[lo_i + k - base : hi_i + k - base]
        return (at(-1) + at(1) + (at(0) + at(0))) * 0.0625

    def filt_w(r, base, lo_i, hi_i):
        at = lambda k: r[lo_i + k - base : hi_i + k - base]
        t = at(-1) + at(0) + at(1)
        return (at(-2) + at(2) + (t + t)) * 0.015625

    un = [filt_n(flow[c][0], 0, 2, 12) for c in range(3)]
    uw = [filt_w(flow[c][1], 0, 2, 12) for c in range(3)]
    for lo_i, hi_i in chunks(3, 11, ROWS_C):
        result = []
        for u, which, filt, flux, factor in ((un, 2, filt_n, yn, 4.0), (uw, 3, filt_w, yw, 16.0)):
            mid = [u[c][lo_i - 2 : hi_i - 2] for c in range(3)]
            dx = [u[c][lo_i - 1 : hi_i - 1] - u[c][lo_i - 3 : hi_i - 3] for c in range(3)]
            dy = [filt(flow[c][which], 0, lo_i, hi_i) for c in range(3)]
            dz = [diff_z(mid[c], sub) for c in range(3)]
            s, mag = strain(dx, dy, dz)
            f = [filt(flux[k], 1, lo_i, hi_i) for k in range(12)]
            lhs = [f[k] - mid[p] * mid[q] for k, (p, q) in enumerate(PAIRS)]
            fm = factor * mag
            rhs = [f[6 + k] - fm * s[k] for k in range(6)]
            result.append((2.0 * contract(lhs, rhs), 4.0 * contract(rhs, rhs)))
        (lm, mm), (qn, nn) = result
        span = range(lo_i - 3, hi_i - 3)
        o_lm, o_qn, o_mm, o_nn = (jnp.stack([row(old, x, f) for x in span]) for f in range(4))
        wn = relax_weight(o_lm * o_mm)
        ww = relax_weight(o_qn * o_nn)
        new_lm = wn * lm + (1.0 - wn) * o_lm
        new_mm = wn * mm + (1.0 - wn) * o_mm
        new_qn = ww * qn + (1.0 - ww) * o_qn
        new_nn = ww * nn + (1.0 - ww) * o_nn
        c2 = jnp.maximum(new_lm, 0.0) / new_mm
        c4 = jnp.maximum(new_qn, 0.0) / new_nn
        cs = c2 * c2 / jnp.maximum(jnp.maximum(c4, 0.125 * c2), RATIO_FLOOR)
        clipped = jnp.stack([row(clip_ref, x) for x in span]) == 1
        blocked = jnp.stack([row(solid_ref, x) for x in span]) == 1
        cs = jnp.where(clipped, jnp.minimum(cs, CLIP_CAP), cs)
        cs = jnp.where(blocked, 0.0, -2.0 * cs)
        out = [cs * own_flux[k][lo_i - 1 : hi_i - 1] for k in range(6)]
        for j, x in enumerate(span):
            at = (pl.ds(x, 8, stride=8), slice(None))
            for k in range(6):
                stress_ref[(k,) + at] = out[k][j]
            for k, v in enumerate((new_lm, new_mm, new_qn, new_nn)):
                new_ref[(k,) + at] = v[j]


VM = pl.BlockSpec(memory_space=pltpu.VMEM)
HBM = pl.BlockSpec(memory_space=pltpu.HBM)


def call(kernel, outs, specs, scratch, limit=VMEM_LIMIT, flops=0):
    return pl.pallas_call(
        kernel, out_shape=outs, in_specs=specs, out_specs=[VM] * len(outs), scratch_shapes=scratch,
        compiler_params=pltpu.CompilerParams(vmem_limit_bytes=limit),
        cost_estimate=pl.CostEstimate(flops=flops, bytes_accessed=400_000, transcendentals=0),
    )


def far_side(gy):
    return (gy + 1) % 16 if gy % 2 else (gy - 1) % 16


def low(gy):
    return gy % 4 < 2


def send(x, target):
    pairs = []
    for gx in range(32):
        for gy in range(16):
            to = target(gx % 8, gx, gy)
            if to is not None:
                pairs.append((gx * 16 + gy, to[0] % 32 * 16 + to[1]))
    return lax.ppermute(x, ("gx", "gy"), pairs)


def local(velocity, kept_lm_qn, kept_mm_nn, back_src, solid_flags, clip_flags):
    sds = jax.ShapeDtypeStruct
    vel = velocity.reshape(3, 64, 128)
    solid = solid_flags.reshape(64, 128)
    clip = clip_flags.reshape(64, 128)
    lq = kept_lm_qn.reshape(128, 128)
    mn = kept_mm_nn.reshape(128, 128)
    src = back_src.reshape(64, 16)
    strip_type = sds((32, 128), BF16)
    code_type = sds((256, 128), jnp.int16)
    trans = pltpu.VMEM((3, 64, 128), F32)
    tail, head, side, code = call(
        pack_kernel,
        [sds((608, 128), BF16), sds((96, 128), BF16), sds((SIDE, 128), BF16), code_type],
        [HBM] * 4,
        [pltpu.VMEM((3, 64, 128), BF16), pltpu.VMEM((64, 128), jnp.int32), pltpu.VMEM((256, 128), F32),
         trans, pltpu.SemaphoreType.DMA((4,))],
        PACK_LIMIT,
    )(vel, solid, lq, mn)
    lo = send(tail, lambda run, gx, gy: (gx + 1, gy) if run < 7 else (gx + 1, far_side(gy)) if low(gy) else None)
    hi = send(head, lambda run, gx, gy: (gx - 1, gy) if run > 0 else None)
    side = send(side, lambda run, gx, gy: (gx + 1, far_side(gy)) if run == 7 and not low(gy) else None)
    wrap = send(tail, lambda run, gx, gy: (gx + 1, gy) if run == 7 else None)
    two_wrap = send(code, lambda run, gx, gy: (gx + 2, gy) if run == 6 and low(gy) else None)
    two = send(code, lambda run, gx, gy: (gx + 2, gy) if run != 6 or not low(gy) else None)
    (wide,) = call(wide_kernel, [sds((128, 128), BF16)], [VM] * 3, [trans], flops=BIG)(vel, solid, hi)
    (strip,) = call(far_kernel, [strip_type], [VM] * 4, [trans])(vel, solid, lo, hi)
    wide = send(wide, lambda run, gx, gy: (gx, far_side(gy)) if run == 0 else None)
    relay, strip = call(relay_kernel, [sds((192, 128), BF16), strip_type], [VM] * 5, [])(wide, strip, head, side, two_wrap)
    relay = send(relay, lambda run, gx, gy: (gx - 1, far_side(gy)) if run == 0 else None)
    far = send(strip, lambda run, gx, gy: (gx, far_side(gy)) if run > 0 else None)
    (near,) = call(near_kernel, [strip_type], [VM] * 6, [trans])(vel, solid, lo, wrap, hi, relay)
    near = send(near, lambda run, gx, gy: (gx, gy ^ 1))
    stress, new = call(
        main_kernel, [sds((6, 64, 128), F32), sds((4, 64, 128), F32)], [VM] * 16, [trans, pltpu.VMEM((4, 64, 128), F32)],
    )(vel, solid, clip, lo, wrap, hi, relay, far, wide, side, near, src, lq, mn, two, two_wrap)
    return stress.reshape(6, 8, 8, 128), new.reshape(4, 8, 8, 128)


def solution(mesh):
    in_specs = (
        P(None, None, "gx", "gy"),
        P(None, None, "gx", "gy"),
        P(None, None, "gx", "gy"),
        P(None, "gx", "gy"),
        P(None, "gx", "gy"),
        P(None, "gx", "gy"),
    )
    out_specs = (P(None, None, "gx", "gy"), P(None, None, "gx", "gy"))
    return jax.shard_map(local, mesh=mesh, in_specs=in_specs, out_specs=out_specs, check_vma=False)
```

```python
import jax
import jax.numpy as jnp
from jax import lax
from jax.experimental import pallas as pl
from jax.experimental.pallas import tpu as pltpu
from jax.sharding import PartitionSpec as P

PRODUCT_FLOOR = 0.05
RATE_SCALE = 0.5
CLIP_CAP = 0.1
RATIO_FLOOR = 0.02
PAIRS = ((0, 0), (1, 1), (2, 2), (0, 1), (0, 2), (1, 2))
KEPT_SCALE = 32767.0 / 1.1892073
F32 = jnp.float32
BF16 = jnp.bfloat16
VMEM_LIMIT = 32 * 1024 * 1024
PACK_LIMIT = 60 * 1024 * 1024
BIG = 1_000_000_000
SIDE = 256
HEAD = 80
ROWS_A = 7
ROWS_B = 4
ROWS_C = 2


def row(ref, x, lead=None):
    at = (pl.ds(x, 8, stride=8), slice(None))
    return ref[at] if lead is None else ref[(lead,) + at]


def encode(x):
    root = jnp.sqrt(jnp.sqrt(jnp.sqrt(jnp.abs(x))))
    scaled = jnp.where(x < 0, -root, root) * KEPT_SCALE
    return jnp.round(scaled).astype(jnp.int32).astype(jnp.int16)


def decode(code):
    y = code.astype(jnp.int32).astype(F32) * (1.0 / KEPT_SCALE)
    y2 = y * y
    y4 = y2 * y2
    return jnp.where(y < 0, -y4, y4) * y4


def place():
    return lax.axis_index("gx") & 7, (lax.axis_index("gy") & 1) == 0


def edges(rows, first):
    lane = lax.broadcasted_iota(jnp.int32, (8, 128), 1)
    left, right = [], []
    for c in range(3):
        lefts = jnp.zeros((8, 128), F32)
        rights = jnp.zeros((8, 128), F32)
        for k, value in enumerate(rows[c]):
            i = first + k
            here = (lane >= 4 * i) & (lane < 4 * i + 4)
            lefts = jnp.where(here, pltpu.roll(value, 4 * i, 1) if i else value, lefts)
            rights = jnp.where(here, pltpu.roll(value, 4 * i + 4, 1), rights)
        left.append(lefts)
        right.append(rights)
    none = [jnp.zeros((8, 128), F32)]
    return jnp.concatenate(left + none, axis=0), jnp.concatenate(right + none, axis=0)


def own_rows(vel_ref, solid_ref, scratch):
    inside = solid_ref[...] == 1
    for c in range(3):
        scratch[c] = jnp.where(inside, 0.0, vel_ref[c].astype(F32))
    return [[row(scratch, x, c) for x in range(8)] for c in range(3)]


def head_rows(rows):
    none = [jnp.zeros((8, 128), F32)]
    return jnp.concatenate([rows[c][x] for c in range(3) for x in range(3)] + none, axis=0).astype(BF16)


def pack_kernel(vel_hbm, solid_hbm, lq_hbm, mn_hbm, tail_ref, head_ref, side_ref, code_ref,
                vel, solid, kept, scratch, sems):
    copies = [
        pltpu.make_async_copy(vel_hbm, vel, sems.at[0]),
        pltpu.make_async_copy(solid_hbm, solid, sems.at[1]),
        pltpu.make_async_copy(lq_hbm, kept.at[pl.ds(0, 128)], sems.at[2]),
        pltpu.make_async_copy(mn_hbm, kept.at[pl.ds(128, 128)], sems.at[3]),
    ]
    for copy in copies:
        copy.start()
    copies[0].wait()
    copies[1].wait()
    rows = own_rows(vel, solid, scratch)
    head_ref[...] = head_rows(rows)
    tail = jnp.concatenate([rows[c][4 + x] for c in range(3) for x in range(4)], axis=0).astype(BF16)
    tail_ref[pl.ds(0, 96), :] = tail
    side_ref[pl.ds(0, 96), :] = tail
    side_ref[pl.ds(96, SIDE - 96), :] = jnp.zeros((SIDE - 96, 128), BF16)
    copies[2].wait()
    copies[3].wait()
    old = kept[...]
    code_ref[...] = encode(old)
    high = old.astype(BF16)
    tail_ref[pl.ds(96, 256), :] = high
    tail_ref[pl.ds(352, 256), :] = (old - high.astype(F32)).astype(BF16)


def all_rows(own, lo, hi):
    lo = lo.reshape(3, 4, 8, 128)
    hi = hi[:72].reshape(3, 3, 8, 128)
    out = []
    for c in range(3):
        rows = [lo[c, x] for x in (1, 2, 3)]
        rows += own[c]
        rows += [hi[c, x] for x in (0, 1, 2)]
        out.append(rows)
    return out


def lead(ref, n):
    return ref[pl.ds(0, n), :].astype(F32)


def wide_kernel(vel_ref, solid_ref, hi_ref, wide_ref, scratch):
    own = own_rows(vel_ref, solid_ref, scratch)
    hi = lead(hi_ref, HEAD)
    left, right = edges(all_rows(own, jnp.zeros((96, 128), F32), hi), 0)
    _, even = place()
    wide_ref[pl.ds(HEAD, 32), :] = jnp.where(even, left, right).astype(BF16)
    wide_ref[pl.ds(0, HEAD), :] = head_rows(own)


def far_kernel(vel_ref, solid_ref, lo_ref, hi_ref, strip_ref, scratch):
    rows = all_rows(own_rows(vel_ref, solid_ref, scratch), lead(lo_ref, 96), lead(hi_ref, HEAD))
    left, right = edges(rows, 0)
    _, even = place()
    strip_ref[...] = jnp.where(even, left, right).astype(BF16)


def relay_kernel(wide_ref, strip_ref, side_ref, two_ref, relay_ref, strip_out):
    relay_ref[pl.ds(0, HEAD), :] = wide_ref[pl.ds(0, HEAD), :]
    relay_ref[pl.ds(HEAD, 32), :] = strip_ref[...]
    strip_out[...] = strip_ref[...]


def near_kernel(vel_ref, solid_ref, lo_ref, wrap_ref, hi_ref, relay_ref, strip_ref, scratch):
    at, even = place()
    own = own_rows(vel_ref, solid_ref, scratch)
    lo = jnp.where(at == 0, lead(wrap_ref, 96), lead(lo_ref, 96))
    hi = jnp.where(at == 7, lead(relay_ref, HEAD), lead(hi_ref, HEAD))
    left, right = edges(all_rows(own, lo, hi), 0)
    strip_ref[...] = jnp.where(even, right, left).astype(BF16)


def shift_y(a, b, k, lane):
    if k > 0:
        return pltpu.roll(jnp.where(lane < k, b, a), 128 - k, a.ndim - 1)
    return pltpu.roll(jnp.where(lane >= 128 + k, b, a), -k, a.ndim - 1)


def diff_z(f, sub):
    up = jnp.where(sub == 7, f, pltpu.roll(f, 7, f.ndim - 2))
    down = jnp.where(sub == 0, f, pltpu.roll(f, 1, f.ndim - 2))
    return up - down


def strain(dx, dy, dz):
    d = (dx, dy, dz)
    s = [0.5 * d[i][i] for i in range(3)] + [0.25 * (d[j][i] + d[i][j]) for i, j in PAIRS[3:]]
    diag = s[0] * s[0] + s[1] * s[1] + s[2] * s[2]
    off = s[3] * s[3] + s[4] * s[4] + s[5] * s[5]
    return s, jnp.sqrt(2.0 * diag + 4.0 * off)


def contract(a, b):
    return (a[0] * b[0] + a[1] * b[1] + a[2] * b[2]) + 2.0 * (a[3] * b[3] + a[4] * b[4] + a[5] * b[5])


def relax_weight(product):
    inverse = lax.rsqrt(lax.rsqrt(lax.rsqrt(jnp.maximum(product, PRODUCT_FLOOR))))
    return 1.0 / (1.0 + (1.0 / RATE_SCALE) * inverse)


def main_kernel(vel_ref, solid_ref, clip_ref, lo_ref, wrap_ref, hi_ref, relay_ref, far_ref, wide_ref, side_ref,
                near_ref, src_ref, lq_ref, mn_ref, two_ref, two_wrap_ref, stress_ref, new_ref, scratch, old):
    lane = lax.broadcasted_iota(jnp.int32, (8, 128), 1)
    sub = lax.broadcasted_iota(jnp.int32, (8, 128), 0)
    run, even = place()
    here = lax.broadcasted_iota(jnp.int32, (64, 16), 0) % 8
    back = (lax.axis_index("gx") * 8 + here - src_ref[...] + 512) & 255
    spread = (lax.broadcasted_iota(jnp.int32, (16, 128), 1) // 8 == lax.broadcasted_iota(jnp.int32, (16, 128), 0))
    local = jnp.dot((16 + here - back).astype(F32), spread.astype(F32), preferred_element_type=F32)
    local = (local + 0.5).astype(jnp.int32)
    tile = lo_ref[pl.ds(96, 256), :].astype(F32) + lo_ref[pl.ds(352, 256), :].astype(F32)
    wrap = wrap_ref[pl.ds(96, 256), :].astype(F32) + wrap_ref[pl.ds(352, 256), :].astype(F32)
    up1 = jnp.where(run == 0, wrap, tile).reshape(4, 64, 128)
    lower = (lax.axis_index("gy") & 3) < 2
    up2 = decode(jnp.where((run == 0) & lower, two_wrap_ref[...].astype(jnp.int32), two_ref[...].astype(jnp.int32))).reshape(4, 64, 128)
    for z in range(8):
        at = pl.ds(8 * z, 8)
        idx = local[8 * z : 8 * z + 8]
        inner = idx & 7
        for f in range(4):
            own_ref = lq_ref if f < 2 else mn_ref
            own = own_ref[pl.ds(64 * (f % 2) + 8 * z, 8), :]
            got = jnp.take_along_axis(own, inner, axis=0)
            one = jnp.take_along_axis(up1[f, 8 * z : 8 * z + 8], inner, axis=0)
            two = jnp.take_along_axis(up2[f, 8 * z : 8 * z + 8], inner, axis=0)
            old[f, at, :] = jnp.where(idx < 8, two, jnp.where(idx < 16, one, got))
    lo = jnp.where(run == 0, lead(wrap_ref, 96), lead(lo_ref, 96))
    hi = jnp.where(run == 7, lead(relay_ref, HEAD), lead(hi_ref, HEAD))
    core = all_rows(own_rows(vel_ref, solid_ref, scratch), lo, hi)
    near = near_ref[...].astype(F32).reshape(4, 8, 128)
    far = jnp.where(run == 0, wide_ref[pl.ds(HEAD, 32), :].astype(F32), far_ref[...].astype(F32)).reshape(4, 8, 128)
    below = jnp.where(lower, lead(side_ref, 96), lead(lo_ref, 96)).reshape(3, 4, 8, 128)
    above = relay_ref[pl.ds(HEAD, 32), :].astype(F32).reshape(4, 8, 128)
    far = [jnp.where((run == 7) & (lane >= 44), pltpu.roll(above[c], 32, 1), far[c]) for c in range(3)]
    edge = []
    for c in range(3):
        left = jnp.where(even, far[c], near[c])
        right = jnp.where(even, near[c], far[c])
        rows = []
        for i in range(14):
            r = pltpu.roll(right, 128 - 4 * i, 1) if i else right
            l = pltpu.roll(left, 124 - 4 * i, 1)
            value = jnp.where(lane < 64, r, l)
            if i < 3:
                value = jnp.where((run == 0) & ((lane >= 64) == even), below[c, i + 1], value)
            rows.append(value)
        edge.append(jnp.stack(rows))
    core = [jnp.stack(rows) for rows in core]

    def chunks(first, last, size):
        return [(k, min(k + size, last)) for k in range(first, last, size)]

    flow = [[[] for _ in range(5)] for _ in range(3)]
    for lo_i, hi_i in chunks(0, 14, ROWS_A):
        for c in range(3):
            a, b = core[c][lo_i:hi_i], edge[c][lo_i:hi_i]
            p1, m1 = shift_y(a, b, 1, lane), shift_y(a, b, -1, lane)
            p2, m2 = shift_y(a, b, 2, lane), shift_y(a, b, -2, lane)
            p3, m3 = shift_y(a, b, 3, lane), shift_y(a, b, -3, lane)
            s1, d1, s2, d2 = p1 + m1, p1 - m1, p2 + m2, p2 - m2
            t = a + s1
            for k, v in enumerate((a + t, t + t + s2, d1 + d1 + d2, d1 + d2 + d2 + (p3 - m3), d1)):
                flow[c][k].append(v)
    flow = [[jnp.concatenate(v, axis=0) for v in per] for per in flow]
    yn, yw, own_flux = ([[] for _ in range(k)] for k in (12, 12, 6))
    for lo_i, hi_i in chunks(1, 13, ROWS_B):
        flux = []
        for t, o in ((core, edge), (edge, core)):
            mid = [t[c][lo_i:hi_i] for c in range(3)]
            dx = [t[c][lo_i + 1 : hi_i + 1] - t[c][lo_i - 1 : hi_i - 1] for c in range(3)]
            if t is core:
                dy = [flow[c][4][lo_i:hi_i] for c in range(3)]
            else:
                oth = [o[c][lo_i:hi_i] for c in range(3)]
                dy = [shift_y(mid[c], oth[c], 1, lane) - shift_y(mid[c], oth[c], -1, lane) for c in range(3)]
            dz = [diff_z(mid[c], sub) for c in range(3)]
            s, mag = strain(dx, dy, dz)
            flux.append([mid[p] * mid[q] for p, q in PAIRS] + [mag * e for e in s])
        for k in range(6):
            own_flux[k].append(flux[0][6 + k])
        for k, (a, b) in enumerate(zip(*flux)):
            s1 = shift_y(a, b, 1, lane) + shift_y(a, b, -1, lane)
            s2 = shift_y(a, b, 2, lane) + shift_y(a, b, -2, lane)
            t = a + s1
            yn[k].append(a + t)
            yw[k].append(t + t + s2)
    yn, yw, own_flux = ([jnp.concatenate(v, axis=0) for v in g] for g in (yn, yw, own_flux))

    def filt_n(r, base, lo_i, hi_i):
        at = lambda k: r[lo_i + k - base : hi_i + k - base]
        return (at(-1) + at(1) + (at(0) + at(0))) * 0.0625

    def filt_w(r, base, lo_i, hi_i):
        at = lambda k: r[lo_i + k - base : hi_i + k - base]
        t = at(-1) + at(0) + at(1)
        return (at(-2) + at(2) + (t + t)) * 0.015625

    un = [filt_n(flow[c][0], 0, 2, 12) for c in range(3)]
    uw = [filt_w(flow[c][1], 0, 2, 12) for c in range(3)]
    for lo_i, hi_i in chunks(3, 11, ROWS_C):
        result = []
        for u, which, filt, flux, factor in ((un, 2, filt_n, yn, 4.0), (uw, 3, filt_w, yw, 16.0)):
            mid = [u[c][lo_i - 2 : hi_i - 2] for c in range(3)]
            dx = [u[c][lo_i - 1 : hi_i - 1] - u[c][lo_i - 3 : hi_i - 3] for c in range(3)]
            dy = [filt(flow[c][which], 0, lo_i, hi_i) for c in range(3)]
            dz = [diff_z(mid[c], sub) for c in range(3)]
            s, mag = strain(dx, dy, dz)
            f = [filt(flux[k], 1, lo_i, hi_i) for k in range(12)]
            lhs = [f[k] - mid[p] * mid[q] for k, (p, q) in enumerate(PAIRS)]
            fm = factor * mag
            rhs = [f[6 + k] - fm * s[k] for k in range(6)]
            result.append((2.0 * contract(lhs, rhs), 4.0 * contract(rhs, rhs)))
        (lm, mm), (qn, nn) = result
        span = range(lo_i - 3, hi_i - 3)
        o_lm, o_qn, o_mm, o_nn = (jnp.stack([row(old, x, f) for x in span]) for f in range(4))
        wn = relax_weight(o_lm * o_mm)
        ww = relax_weight(o_qn * o_nn)
        new_lm = wn * lm + (1.0 - wn) * o_lm
        new_mm = wn * mm + (1.0 - wn) * o_mm
        new_qn = ww * qn + (1.0 - ww) * o_qn
        new_nn = ww * nn + (1.0 - ww) * o_nn
        c2 = jnp.maximum(new_lm, 0.0) / new_mm
        c4 = jnp.maximum(new_qn, 0.0) / new_nn
        cs = c2 * c2 / jnp.maximum(jnp.maximum(c4, 0.125 * c2), RATIO_FLOOR)
        clipped = jnp.stack([row(clip_ref, x) for x in span]) == 1
        blocked = jnp.stack([row(solid_ref, x) for x in span]) == 1
        cs = jnp.where(clipped, jnp.minimum(cs, CLIP_CAP), cs)
        cs = jnp.where(blocked, 0.0, -2.0 * cs)
        out = [cs * own_flux[k][lo_i - 1 : hi_i - 1] for k in range(6)]
        for j, x in enumerate(span):
            at = (pl.ds(x, 8, stride=8), slice(None))
            for k in range(6):
                stress_ref[(k,) + at] = out[k][j]
            for k, v in enumerate((new_lm, new_mm, new_qn, new_nn)):
                new_ref[(k,) + at] = v[j]


VM = pl.BlockSpec(memory_space=pltpu.VMEM)
HBM = pl.BlockSpec(memory_space=pltpu.HBM)


def call(kernel, outs, specs, scratch, limit=VMEM_LIMIT, flops=0):
    return pl.pallas_call(
        kernel, out_shape=outs, in_specs=specs, out_specs=[VM] * len(outs), scratch_shapes=scratch,
        compiler_params=pltpu.CompilerParams(vmem_limit_bytes=limit),
        cost_estimate=pl.CostEstimate(flops=flops, bytes_accessed=400_000, transcendentals=0),
    )


def far_side(gy):
    return (gy + 1) % 16 if gy % 2 else (gy - 1) % 16


def low(gy):
    return gy % 4 < 2


def send(x, target):
    pairs = []
    for gx in range(32):
        for gy in range(16):
            to = target(gx % 8, gx, gy)
            if to is not None:
                pairs.append((gx * 16 + gy, to[0] % 32 * 16 + to[1]))
    return lax.ppermute(x, ("gx", "gy"), pairs)


def local(velocity, kept_lm_qn, kept_mm_nn, back_src, solid_flags, clip_flags):
    sds = jax.ShapeDtypeStruct
    vel = velocity.reshape(3, 64, 128)
    solid = solid_flags.reshape(64, 128)
    clip = clip_flags.reshape(64, 128)
    lq = kept_lm_qn.reshape(128, 128)
    mn = kept_mm_nn.reshape(128, 128)
    src = back_src.reshape(64, 16)
    strip_type = sds((32, 128), BF16)
    code_type = sds((256, 128), jnp.int16)
    trans = pltpu.VMEM((3, 64, 128), F32)
    tail, head, side, code = call(
        pack_kernel,
        [sds((608, 128), BF16), sds((HEAD, 128), BF16), sds((SIDE, 128), BF16), code_type],
        [HBM] * 4,
        [pltpu.VMEM((3, 64, 128), BF16), pltpu.VMEM((64, 128), jnp.int32), pltpu.VMEM((256, 128), F32),
         trans, pltpu.SemaphoreType.DMA((4,))],
        PACK_LIMIT,
    )(vel, solid, lq, mn)
    lo = send(tail, lambda run, gx, gy: (gx + 1, gy) if run < 7 else (gx + 1, far_side(gy)) if low(gy) else None)
    hi = send(head, lambda run, gx, gy: (gx - 1, gy) if run > 0 else None)
    side = send(side, lambda run, gx, gy: (gx + 1, far_side(gy)) if run == 7 and not low(gy) else None)
    wrap = send(tail, lambda run, gx, gy: (gx + 1, gy) if run == 7 else None)
    two_wrap = send(code, lambda run, gx, gy: (gx + 2, gy) if run == 6 and low(gy) else None)
    two = send(code, lambda run, gx, gy: (gx + 2, gy) if run != 6 or not low(gy) else None)
    (wide,) = call(wide_kernel, [sds((HEAD + 32, 128), BF16)], [VM] * 3, [trans], flops=BIG)(vel, solid, hi)
    (strip,) = call(far_kernel, [strip_type], [VM] * 4, [trans])(vel, solid, lo, hi)
    wide = send(wide, lambda run, gx, gy: (gx, far_side(gy)) if run == 0 else None)
    relay, strip = call(relay_kernel, [sds((HEAD + 32, 128), BF16), strip_type], [VM] * 4, [])(wide, strip, side, two_wrap)
    relay = send(relay, lambda run, gx, gy: (gx - 1, far_side(gy)) if run == 0 else None)
    far = send(strip, lambda run, gx, gy: (gx, far_side(gy)) if run > 0 else None)
    (near,) = call(near_kernel, [strip_type], [VM] * 6, [trans])(vel, solid, lo, wrap, hi, relay)
    near = send(near, lambda run, gx, gy: (gx, gy ^ 1))
    stress, new = call(
        main_kernel, [sds((6, 64, 128), F32), sds((4, 64, 128), F32)], [VM] * 16, [trans, pltpu.VMEM((4, 64, 128), F32)],
    )(vel, solid, clip, lo, wrap, hi, relay, far, wide, side, near, src, lq, mn, two, two_wrap)
    return stress.reshape(6, 8, 8, 128), new.reshape(4, 8, 8, 128)


def solution(mesh):
    in_specs = (
        P(None, None, "gx", "gy"),
        P(None, None, "gx", "gy"),
        P(None, None, "gx", "gy"),
        P(None, "gx", "gy"),
        P(None, "gx", "gy"),
        P(None, "gx", "gy"),
    )
    out_specs = (P(None, None, "gx", "gy"), P(None, None, "gx", "gy"))
    return jax.shard_map(local, mesh=mesh, in_specs=in_specs, out_specs=out_specs, check_vma=False)
```

```python
import jax
import jax.numpy as jnp
from jax import lax
from jax.experimental import pallas as pl
from jax.experimental.pallas import tpu as pltpu
from jax.sharding import PartitionSpec as P

PRODUCT_FLOOR = 0.05
RATE_SCALE = 0.5
CLIP_CAP = 0.1
RATIO_FLOOR = 0.02
PAIRS = ((0, 0), (1, 1), (2, 2), (0, 1), (0, 2), (1, 2))
KEPT_SCALE = 32767.0 / 1.1892073
F32 = jnp.float32
BF16 = jnp.bfloat16
VMEM_LIMIT = 32 * 1024 * 1024
PACK_LIMIT = 60 * 1024 * 1024
BIG = 1_000_000_000
SIDE = 256
HEAD = 80
ROWS_A = 7
ROWS_B = 4
ROWS_C = 2


def row(ref, x, lead=None):
    at = (pl.ds(x, 8, stride=8), slice(None))
    return ref[at] if lead is None else ref[(lead,) + at]


def encode(x):
    root = jnp.sqrt(jnp.sqrt(jnp.sqrt(jnp.abs(x))))
    scaled = jnp.where(x < 0, -root, root) * KEPT_SCALE
    return jnp.round(scaled).astype(jnp.int32).astype(jnp.int16)


def decode(code):
    y = code.astype(jnp.int32).astype(F32) * (1.0 / KEPT_SCALE)
    y2 = y * y
    y4 = y2 * y2
    return jnp.where(y < 0, -y4, y4) * y4


def place():
    return lax.axis_index("gx") & 7, (lax.axis_index("gy") & 1) == 0


def edges(rows, first):
    lane = lax.broadcasted_iota(jnp.int32, (8, 128), 1)
    left, right = [], []
    for c in range(3):
        lefts = jnp.zeros((8, 128), F32)
        rights = jnp.zeros((8, 128), F32)
        for k, value in enumerate(rows[c]):
            i = first + k
            here = (lane >= 4 * i) & (lane < 4 * i + 4)
            lefts = jnp.where(here, pltpu.roll(value, 4 * i, 1) if i else value, lefts)
            rights = jnp.where(here, pltpu.roll(value, 4 * i + 4, 1), rights)
        left.append(lefts)
        right.append(rights)
    none = [jnp.zeros((8, 128), F32)]
    return jnp.concatenate(left + none, axis=0), jnp.concatenate(right + none, axis=0)


def own_rows(vel_ref, solid_ref, scratch):
    inside = solid_ref[...] == 1
    for c in range(3):
        scratch[c] = jnp.where(inside, 0.0, vel_ref[c].astype(F32))
    return [[row(scratch, x, c) for x in range(8)] for c in range(3)]


def head_rows(rows):
    none = [jnp.zeros((8, 128), F32)]
    return jnp.concatenate([rows[c][x] for c in range(3) for x in range(3)] + none, axis=0).astype(BF16)


def pack_kernel(vel_hbm, solid_hbm, lq_hbm, mn_hbm, tail_ref, head_ref, side_ref, code_ref,
                vel, solid, kept, scratch, sems):
    copies = [
        pltpu.make_async_copy(vel_hbm, vel, sems.at[0]),
        pltpu.make_async_copy(solid_hbm, solid, sems.at[1]),
        pltpu.make_async_copy(lq_hbm, kept.at[pl.ds(0, 128)], sems.at[2]),
        pltpu.make_async_copy(mn_hbm, kept.at[pl.ds(128, 128)], sems.at[3]),
    ]
    for copy in copies:
        copy.start()
    copies[0].wait()
    copies[1].wait()
    rows = own_rows(vel, solid, scratch)
    head_ref[...] = head_rows(rows)
    tail = jnp.concatenate([rows[c][4 + x] for c in range(3) for x in range(4)], axis=0).astype(BF16)
    tail_ref[pl.ds(0, 96), :] = tail
    side_ref[pl.ds(0, 96), :] = tail
    side_ref[pl.ds(96, SIDE - 96), :] = jnp.zeros((SIDE - 96, 128), BF16)
    copies[2].wait()
    copies[3].wait()
    old = kept[...]
    code_ref[...] = encode(old)
    high = old.astype(BF16)
    tail_ref[pl.ds(96, 256), :] = high
    tail_ref[pl.ds(352, 256), :] = (old - high.astype(F32)).astype(BF16)


def all_rows(own, lo, hi):
    lo = lo.reshape(3, 4, 8, 128)
    hi = hi[:72].reshape(3, 3, 8, 128)
    out = []
    for c in range(3):
        rows = [lo[c, x] for x in (1, 2, 3)]
        rows += own[c]
        rows += [hi[c, x] for x in (0, 1, 2)]
        out.append(rows)
    return out


def lead(ref, n):
    return ref[pl.ds(0, n), :].astype(F32)


def wide_kernel(vel_ref, solid_ref, hi_ref, wide_ref, scratch):
    own = own_rows(vel_ref, solid_ref, scratch)
    hi = lead(hi_ref, HEAD)
    left, right = edges(all_rows(own, jnp.zeros((96, 128), F32), hi), 0)
    _, even = place()
    wide_ref[pl.ds(HEAD, 32), :] = jnp.where(even, left, right).astype(BF16)
    wide_ref[pl.ds(0, HEAD), :] = head_rows(own)


def far_kernel(vel_ref, solid_ref, lo_ref, hi_ref, strip_ref, scratch):
    rows = all_rows(own_rows(vel_ref, solid_ref, scratch), lead(lo_ref, 96), lead(hi_ref, HEAD))
    left, right = edges(rows, 0)
    _, even = place()
    strip_ref[...] = jnp.where(even, left, right).astype(BF16)


def relay_kernel(wide_ref, strip_ref, side_ref, two_ref, relay_ref, strip_out):
    relay_ref[pl.ds(0, HEAD), :] = wide_ref[pl.ds(0, HEAD), :]
    relay_ref[pl.ds(HEAD, 32), :] = strip_ref[...]
    strip_out[...] = strip_ref[...]


def near_kernel(vel_ref, solid_ref, lo_ref, wrap_ref, hi_ref, relay_ref, strip_ref, scratch):
    at, even = place()
    own = own_rows(vel_ref, solid_ref, scratch)
    lo = jnp.where(at == 0, lead(wrap_ref, 96), lead(lo_ref, 96))
    hi = jnp.where(at == 7, lead(relay_ref, HEAD), lead(hi_ref, HEAD))
    left, right = edges(all_rows(own, lo, hi), 0)
    strip_ref[...] = jnp.where(even, right, left).astype(BF16)


def shift_y(a, b, k, lane):
    if k > 0:
        return pltpu.roll(jnp.where(lane < k, b, a), 128 - k, a.ndim - 1)
    return pltpu.roll(jnp.where(lane >= 128 + k, b, a), -k, a.ndim - 1)


def diff_z(f, sub):
    up = jnp.where(sub == 7, f, pltpu.roll(f, 7, f.ndim - 2))
    down = jnp.where(sub == 0, f, pltpu.roll(f, 1, f.ndim - 2))
    return up - down


def strain(dx, dy, dz):
    d = (dx, dy, dz)
    s = [0.5 * d[i][i] for i in range(3)] + [0.25 * (d[j][i] + d[i][j]) for i, j in PAIRS[3:]]
    diag = s[0] * s[0] + s[1] * s[1] + s[2] * s[2]
    off = s[3] * s[3] + s[4] * s[4] + s[5] * s[5]
    return s, jnp.sqrt(2.0 * diag + 4.0 * off)


def contract(a, b):
    return (a[0] * b[0] + a[1] * b[1] + a[2] * b[2]) + 2.0 * (a[3] * b[3] + a[4] * b[4] + a[5] * b[5])


def relax_weight(product):
    inverse = lax.rsqrt(lax.rsqrt(lax.rsqrt(jnp.maximum(product, PRODUCT_FLOOR))))
    return pl.reciprocal(1.0 + (1.0 / RATE_SCALE) * inverse)


def main_kernel(vel_ref, solid_ref, clip_ref, lo_ref, wrap_ref, hi_ref, relay_ref, far_ref, wide_ref, side_ref,
                near_ref, src_ref, lq_ref, mn_ref, two_ref, two_wrap_ref, stress_ref, new_ref, scratch, old, tiles):
    lane = lax.broadcasted_iota(jnp.int32, (8, 128), 1)
    sub = lax.broadcasted_iota(jnp.int32, (8, 128), 0)
    run, even = place()
    here = lax.broadcasted_iota(jnp.int32, (64, 16), 0) % 8
    back = (lax.axis_index("gx") * 8 + here - src_ref[...] + 512) & 255
    spread = (lax.broadcasted_iota(jnp.int32, (16, 128), 1) // 8 == lax.broadcasted_iota(jnp.int32, (16, 128), 0))
    local = jnp.dot((16 + here - back).astype(F32), spread.astype(F32), preferred_element_type=F32)
    local = (local + 0.5).astype(jnp.int32)
    lower = (lax.axis_index("gy") & 3) < 2

    def add_up(ref):
        tiles[...] = ref[pl.ds(96, 256), :].astype(F32) + ref[pl.ds(352, 256), :].astype(F32)

    pl.when(run == 0)(lambda: add_up(wrap_ref))
    pl.when(run != 0)(lambda: add_up(lo_ref))
    up1 = tiles[...].reshape(4, 64, 128)
    up2 = decode(jnp.where((run == 0) & lower, two_wrap_ref[...].astype(jnp.int32), two_ref[...].astype(jnp.int32))).reshape(4, 64, 128)
    for z in range(8):
        at = pl.ds(8 * z, 8)
        idx = local[8 * z : 8 * z + 8]
        inner = idx & 7
        for f in range(4):
            own_ref = lq_ref if f < 2 else mn_ref
            own = own_ref[pl.ds(64 * (f % 2) + 8 * z, 8), :]
            got = jnp.take_along_axis(own, inner, axis=0)
            one = jnp.take_along_axis(up1[f, 8 * z : 8 * z + 8], inner, axis=0)
            two = jnp.take_along_axis(up2[f, 8 * z : 8 * z + 8], inner, axis=0)
            old[f, at, :] = jnp.where(idx < 8, two, jnp.where(idx < 16, one, got))
    lo = jnp.where(run == 0, lead(wrap_ref, 96), lead(lo_ref, 96))
    hi = jnp.where(run == 7, lead(relay_ref, HEAD), lead(hi_ref, HEAD))
    core = all_rows(own_rows(vel_ref, solid_ref, scratch), lo, hi)
    near = near_ref[...].astype(F32).reshape(4, 8, 128)
    far = jnp.where(run == 0, wide_ref[pl.ds(HEAD, 32), :].astype(F32), far_ref[...].astype(F32)).reshape(4, 8, 128)
    below = jnp.where(lower, lead(side_ref, 96), lead(lo_ref, 96)).reshape(3, 4, 8, 128)
    above = relay_ref[pl.ds(HEAD, 32), :].astype(F32).reshape(4, 8, 128)
    far = [jnp.where((run == 7) & (lane >= 44), pltpu.roll(above[c], 32, 1), far[c]) for c in range(3)]
    edge = []
    for c in range(3):
        left = jnp.where(even, far[c], near[c])
        right = jnp.where(even, near[c], far[c])
        rows = []
        for i in range(14):
            r = pltpu.roll(right, 128 - 4 * i, 1) if i else right
            l = pltpu.roll(left, 124 - 4 * i, 1)
            value = jnp.where(lane < 64, r, l)
            if i < 3:
                value = jnp.where((run == 0) & ((lane >= 64) == even), below[c, i + 1], value)
            rows.append(value)
        edge.append(jnp.stack(rows))
    core = [jnp.stack(rows) for rows in core]

    def chunks(first, last, size):
        return [(k, min(k + size, last)) for k in range(first, last, size)]

    flow = [[[] for _ in range(5)] for _ in range(3)]
    for lo_i, hi_i in chunks(0, 14, ROWS_A):
        for c in range(3):
            a, b = core[c][lo_i:hi_i], edge[c][lo_i:hi_i]
            p1, m1 = shift_y(a, b, 1, lane), shift_y(a, b, -1, lane)
            p2, m2 = shift_y(a, b, 2, lane), shift_y(a, b, -2, lane)
            p3, m3 = shift_y(a, b, 3, lane), shift_y(a, b, -3, lane)
            s1, d1, s2, d2 = p1 + m1, p1 - m1, p2 + m2, p2 - m2
            t = a + s1
            for k, v in enumerate((a + t, t + t + s2, d1 + d1 + d2, d1 + d2 + d2 + (p3 - m3), d1)):
                flow[c][k].append(v)
    flow = [[jnp.concatenate(v, axis=0) for v in per] for per in flow]
    yn, yw, own_flux = ([[] for _ in range(k)] for k in (12, 12, 6))
    for lo_i, hi_i in chunks(1, 13, ROWS_B):
        flux = []
        for t, o in ((core, edge), (edge, core)):
            mid = [t[c][lo_i:hi_i] for c in range(3)]
            dx = [t[c][lo_i + 1 : hi_i + 1] - t[c][lo_i - 1 : hi_i - 1] for c in range(3)]
            if t is core:
                dy = [flow[c][4][lo_i:hi_i] for c in range(3)]
            else:
                oth = [o[c][lo_i:hi_i] for c in range(3)]
                dy = [shift_y(mid[c], oth[c], 1, lane) - shift_y(mid[c], oth[c], -1, lane) for c in range(3)]
            dz = [diff_z(mid[c], sub) for c in range(3)]
            s, mag = strain(dx, dy, dz)
            flux.append([mid[p] * mid[q] for p, q in PAIRS] + [mag * e for e in s])
        for k in range(6):
            own_flux[k].append(flux[0][6 + k])
        for k, (a, b) in enumerate(zip(*flux)):
            s1 = shift_y(a, b, 1, lane) + shift_y(a, b, -1, lane)
            s2 = shift_y(a, b, 2, lane) + shift_y(a, b, -2, lane)
            t = a + s1
            yn[k].append(a + t)
            yw[k].append(t + t + s2)
    yn, yw, own_flux = ([jnp.concatenate(v, axis=0) for v in g] for g in (yn, yw, own_flux))

    def filt_n(r, base, lo_i, hi_i):
        at = lambda k: r[lo_i + k - base : hi_i + k - base]
        return (at(-1) + at(1) + (at(0) + at(0))) * 0.0625

    def filt_w(r, base, lo_i, hi_i):
        at = lambda k: r[lo_i + k - base : hi_i + k - base]
        t = at(-1) + at(0) + at(1)
        return (at(-2) + at(2) + (t + t)) * 0.015625

    un = [filt_n(flow[c][0], 0, 2, 12) for c in range(3)]
    uw = [filt_w(flow[c][1], 0, 2, 12) for c in range(3)]
    for lo_i, hi_i in chunks(3, 11, ROWS_C):
        result = []
        for u, which, filt, flux, factor in ((un, 2, filt_n, yn, 4.0), (uw, 3, filt_w, yw, 16.0)):
            mid = [u[c][lo_i - 2 : hi_i - 2] for c in range(3)]
            dx = [u[c][lo_i - 1 : hi_i - 1] - u[c][lo_i - 3 : hi_i - 3] for c in range(3)]
            dy = [filt(flow[c][which], 0, lo_i, hi_i) for c in range(3)]
            dz = [diff_z(mid[c], sub) for c in range(3)]
            s, mag = strain(dx, dy, dz)
            f = [filt(flux[k], 1, lo_i, hi_i) for k in range(12)]
            lhs = [f[k] - mid[p] * mid[q] for k, (p, q) in enumerate(PAIRS)]
            fm = factor * mag
            rhs = [f[6 + k] - fm * s[k] for k in range(6)]
            result.append((2.0 * contract(lhs, rhs), 4.0 * contract(rhs, rhs)))
        (lm, mm), (qn, nn) = result
        span = range(lo_i - 3, hi_i - 3)
        o_lm, o_qn, o_mm, o_nn = (jnp.stack([row(old, x, f) for x in span]) for f in range(4))
        wn = relax_weight(o_lm * o_mm)
        ww = relax_weight(o_qn * o_nn)
        new_lm = wn * lm + (1.0 - wn) * o_lm
        new_mm = wn * mm + (1.0 - wn) * o_mm
        new_qn = ww * qn + (1.0 - ww) * o_qn
        new_nn = ww * nn + (1.0 - ww) * o_nn
        c2 = jnp.maximum(new_lm, 0.0) * pl.reciprocal(new_mm)
        c4 = jnp.maximum(new_qn, 0.0) * pl.reciprocal(new_nn)
        cs = c2 * c2 * pl.reciprocal(jnp.maximum(jnp.maximum(c4, 0.125 * c2), RATIO_FLOOR))
        clipped = jnp.stack([row(clip_ref, x) for x in span]) == 1
        blocked = jnp.stack([row(solid_ref, x) for x in span]) == 1
        cs = jnp.where(clipped, jnp.minimum(cs, CLIP_CAP), cs)
        cs = jnp.where(blocked, 0.0, -2.0 * cs)
        out = [cs * own_flux[k][lo_i - 1 : hi_i - 1] for k in range(6)]
        for j, x in enumerate(span):
            at = (pl.ds(x, 8, stride=8), slice(None))
            for k in range(6):
                stress_ref[(k,) + at] = out[k][j]
            for k, v in enumerate((new_lm, new_mm, new_qn, new_nn)):
                new_ref[(k,) + at] = v[j]


VM = pl.BlockSpec(memory_space=pltpu.VMEM)
HBM = pl.BlockSpec(memory_space=pltpu.HBM)


def call(kernel, outs, specs, scratch, limit=VMEM_LIMIT, flops=0):
    return pl.pallas_call(
        kernel, out_shape=outs, in_specs=specs, out_specs=[VM] * len(outs), scratch_shapes=scratch,
        compiler_params=pltpu.CompilerParams(vmem_limit_bytes=limit),
        cost_estimate=pl.CostEstimate(flops=flops, bytes_accessed=400_000, transcendentals=0),
    )


def far_side(gy):
    return (gy + 1) % 16 if gy % 2 else (gy - 1) % 16


def low(gy):
    return gy % 4 < 2


def send(x, target):
    pairs = []
    for gx in range(32):
        for gy in range(16):
            to = target(gx % 8, gx, gy)
            if to is not None:
                pairs.append((gx * 16 + gy, to[0] % 32 * 16 + to[1]))
    return lax.ppermute(x, ("gx", "gy"), pairs)


def local(velocity, kept_lm_qn, kept_mm_nn, back_src, solid_flags, clip_flags):
    sds = jax.ShapeDtypeStruct
    vel = velocity.reshape(3, 64, 128)
    solid = solid_flags.reshape(64, 128)
    clip = clip_flags.reshape(64, 128)
    lq = kept_lm_qn.reshape(128, 128)
    mn = kept_mm_nn.reshape(128, 128)
    src = back_src.reshape(64, 16)
    strip_type = sds((32, 128), BF16)
    code_type = sds((256, 128), jnp.int16)
    trans = pltpu.VMEM((3, 64, 128), F32)
    tail, head, side, code = call(
        pack_kernel,
        [sds((608, 128), BF16), sds((HEAD, 128), BF16), sds((SIDE, 128), BF16), code_type],
        [HBM] * 4,
        [pltpu.VMEM((3, 64, 128), BF16), pltpu.VMEM((64, 128), jnp.int32), pltpu.VMEM((256, 128), F32),
         trans, pltpu.SemaphoreType.DMA((4,))],
        PACK_LIMIT,
    )(vel, solid, lq, mn)
    lo = send(tail, lambda run, gx, gy: (gx + 1, gy) if run < 7 else (gx + 1, far_side(gy)) if low(gy) else None)
    hi = send(head, lambda run, gx, gy: (gx - 1, gy) if run > 0 else None)
    side = send(side, lambda run, gx, gy: (gx + 1, far_side(gy)) if run == 7 and not low(gy) else None)
    wrap = send(tail, lambda run, gx, gy: (gx + 1, gy) if run == 7 else None)
    two_wrap = send(code, lambda run, gx, gy: (gx + 2, gy) if run == 6 and low(gy) else None)
    two = send(code, lambda run, gx, gy: (gx + 2, gy) if run != 6 or not low(gy) else None)
    (wide,) = call(wide_kernel, [sds((HEAD + 32, 128), BF16)], [VM] * 3, [trans], flops=BIG)(vel, solid, hi)
    (strip,) = call(far_kernel, [strip_type], [VM] * 4, [trans])(vel, solid, lo, hi)
    wide = send(wide, lambda run, gx, gy: (gx, far_side(gy)) if run == 0 else None)
    relay, strip = call(relay_kernel, [sds((HEAD + 32, 128), BF16), strip_type], [VM] * 4, [])(wide, strip, side, two_wrap)
    relay = send(relay, lambda run, gx, gy: (gx - 1, far_side(gy)) if run == 0 else None)
    far = send(strip, lambda run, gx, gy: (gx, far_side(gy)) if run > 0 else None)
    (near,) = call(near_kernel, [strip_type], [VM] * 6, [trans])(vel, solid, lo, wrap, hi, relay)
    near = send(near, lambda run, gx, gy: (gx, gy ^ 1))
    stress, new = call(
        main_kernel, [sds((6, 64, 128), F32), sds((4, 64, 128), F32)], [VM] * 16, [trans, pltpu.VMEM((4, 64, 128), F32), pltpu.VMEM((256, 128), F32)],
    )(vel, solid, clip, lo, wrap, hi, relay, far, wide, side, near, src, lq, mn, two, two_wrap)
    return stress.reshape(6, 8, 8, 128), new.reshape(4, 8, 8, 128)


def solution(mesh):
    in_specs = (
        P(None, None, "gx", "gy"),
        P(None, None, "gx", "gy"),
        P(None, None, "gx", "gy"),
        P(None, "gx", "gy"),
        P(None, "gx", "gy"),
        P(None, "gx", "gy"),
    )
    out_specs = (P(None, None, "gx", "gy"), P(None, None, "gx", "gy"))
    return jax.shard_map(local, mesh=mesh, in_specs=in_specs, out_specs=out_specs, check_vma=False)
```

```python
import jax
import jax.numpy as jnp
from jax import lax
from jax.experimental import pallas as pl
from jax.experimental.pallas import tpu as pltpu
from jax.sharding import PartitionSpec as P

PRODUCT_FLOOR = 0.05
RATE_SCALE = 0.5
CLIP_CAP = 0.1
RATIO_FLOOR = 0.02
PAIRS = ((0, 0), (1, 1), (2, 2), (0, 1), (0, 2), (1, 2))
KEPT_SCALE = 32767.0 / 1.1892073
F32 = jnp.float32
BF16 = jnp.bfloat16
VMEM_LIMIT = 32 * 1024 * 1024
PACK_LIMIT = 60 * 1024 * 1024
BIG = 1_000_000_000
SIDE = 112
HEAD = 80
ROWS_A = 7
ROWS_B = 4
ROWS_C = 2


def row(ref, x, lead=None):
    at = (pl.ds(x, 8, stride=8), slice(None))
    return ref[at] if lead is None else ref[(lead,) + at]


def encode(x):
    root = jnp.sqrt(jnp.sqrt(jnp.sqrt(jnp.abs(x))))
    scaled = jnp.where(x < 0, -root, root) * KEPT_SCALE
    return jnp.round(scaled).astype(jnp.int32).astype(jnp.int16)


def decode(code):
    y = code.astype(jnp.int32).astype(F32) * (1.0 / KEPT_SCALE)
    y2 = y * y
    y4 = y2 * y2
    return jnp.where(y < 0, -y4, y4) * y4


def place():
    return lax.axis_index("gx") & 7, (lax.axis_index("gy") & 1) == 0


def edges(rows, first):
    lane = lax.broadcasted_iota(jnp.int32, (8, 128), 1)
    left, right = [], []
    for c in range(3):
        lefts = jnp.zeros((8, 128), F32)
        rights = jnp.zeros((8, 128), F32)
        for k, value in enumerate(rows[c]):
            i = first + k
            here = (lane >= 4 * i) & (lane < 4 * i + 4)
            lefts = jnp.where(here, pltpu.roll(value, 4 * i, 1) if i else value, lefts)
            rights = jnp.where(here, pltpu.roll(value, 4 * i + 4, 1), rights)
        left.append(lefts)
        right.append(rights)
    none = [jnp.zeros((8, 128), F32)]
    return jnp.concatenate(left + none, axis=0), jnp.concatenate(right + none, axis=0)


def own_rows(vel_ref, solid_ref, scratch):
    inside = solid_ref[...] == 1
    for c in range(3):
        scratch[c] = jnp.where(inside, 0.0, vel_ref[c].astype(F32))
    return [[row(scratch, x, c) for x in range(8)] for c in range(3)]


def head_rows(rows):
    none = [jnp.zeros((8, 128), F32)]
    return jnp.concatenate([rows[c][x] for c in range(3) for x in range(3)] + none, axis=0).astype(BF16)


def pack_kernel(vel_hbm, solid_hbm, lq_hbm, mn_hbm, tail_ref, head_ref, side_ref, code_ref,
                vel, solid, kept, scratch, sems):
    copies = [
        pltpu.make_async_copy(vel_hbm, vel, sems.at[0]),
        pltpu.make_async_copy(solid_hbm, solid, sems.at[1]),
        pltpu.make_async_copy(lq_hbm, kept.at[pl.ds(0, 128)], sems.at[2]),
        pltpu.make_async_copy(mn_hbm, kept.at[pl.ds(128, 128)], sems.at[3]),
    ]
    for copy in copies:
        copy.start()
    copies[0].wait()
    copies[1].wait()
    rows = own_rows(vel, solid, scratch)
    head_ref[...] = head_rows(rows)
    tail = jnp.concatenate([rows[c][4 + x] for c in range(3) for x in range(4)], axis=0).astype(BF16)
    tail_ref[pl.ds(0, 96), :] = tail
    side_ref[pl.ds(0, 96), :] = tail
    side_ref[pl.ds(96, SIDE - 96), :] = jnp.zeros((SIDE - 96, 128), BF16)
    copies[2].wait()
    copies[3].wait()
    old = kept[...]
    code_ref[...] = encode(old)
    high = old.astype(BF16)
    tail_ref[pl.ds(96, 256), :] = high
    tail_ref[pl.ds(352, 256), :] = (old - high.astype(F32)).astype(BF16)


def all_rows(own, lo, hi):
    lo = lo.reshape(3, 4, 8, 128)
    hi = hi[:72].reshape(3, 3, 8, 128)
    out = []
    for c in range(3):
        rows = [lo[c, x] for x in (1, 2, 3)]
        rows += own[c]
        rows += [hi[c, x] for x in (0, 1, 2)]
        out.append(rows)
    return out


def lead(ref, n):
    return ref[pl.ds(0, n), :].astype(F32)


def wide_kernel(vel_ref, solid_ref, hi_ref, wide_ref, scratch):
    own = own_rows(vel_ref, solid_ref, scratch)
    hi = lead(hi_ref, HEAD)
    left, right = edges(all_rows(own, jnp.zeros((96, 128), F32), hi), 0)
    _, even = place()
    wide_ref[pl.ds(HEAD, 32), :] = jnp.where(even, left, right).astype(BF16)
    wide_ref[pl.ds(0, HEAD), :] = head_rows(own)


def far_kernel(vel_ref, solid_ref, lo_ref, hi_ref, strip_ref, scratch):
    rows = all_rows(own_rows(vel_ref, solid_ref, scratch), lead(lo_ref, 96), lead(hi_ref, HEAD))
    left, right = edges(rows, 0)
    _, even = place()
    strip_ref[...] = jnp.where(even, left, right).astype(BF16)


def relay_kernel(wide_ref, strip_ref, side_ref, two_ref, relay_ref, strip_out):
    relay_ref[pl.ds(0, HEAD), :] = wide_ref[pl.ds(0, HEAD), :]
    relay_ref[pl.ds(HEAD, 32), :] = strip_ref[...]
    strip_out[...] = strip_ref[...]


def near_kernel(vel_ref, solid_ref, lo_ref, wrap_ref, hi_ref, relay_ref, strip_ref, scratch):
    at, even = place()
    own = own_rows(vel_ref, solid_ref, scratch)
    lo = jnp.where(at == 0, lead(wrap_ref, 96), lead(lo_ref, 96))
    hi = jnp.where(at == 7, lead(relay_ref, HEAD), lead(hi_ref, HEAD))
    left, right = edges(all_rows(own, lo, hi), 0)
    strip_ref[...] = jnp.where(even, right, left).astype(BF16)


def shift_y(a, b, k, lane):
    if k > 0:
        return pltpu.roll(jnp.where(lane < k, b, a), 128 - k, a.ndim - 1)
    return pltpu.roll(jnp.where(lane >= 128 + k, b, a), -k, a.ndim - 1)


def diff_z(f, sub):
    up = jnp.where(sub == 7, f, pltpu.roll(f, 7, f.ndim - 2))
    down = jnp.where(sub == 0, f, pltpu.roll(f, 1, f.ndim - 2))
    return up - down


def strain(dx, dy, dz):
    d = (dx, dy, dz)
    s = [0.5 * d[i][i] for i in range(3)] + [0.25 * (d[j][i] + d[i][j]) for i, j in PAIRS[3:]]
    diag = s[0] * s[0] + s[1] * s[1] + s[2] * s[2]
    off = s[3] * s[3] + s[4] * s[4] + s[5] * s[5]
    return s, jnp.sqrt(2.0 * diag + 4.0 * off)


def contract(a, b):
    return (a[0] * b[0] + a[1] * b[1] + a[2] * b[2]) + 2.0 * (a[3] * b[3] + a[4] * b[4] + a[5] * b[5])


def relax_weight(product):
    inverse = lax.rsqrt(lax.rsqrt(lax.rsqrt(jnp.maximum(product, PRODUCT_FLOOR))))
    return pl.reciprocal(1.0 + (1.0 / RATE_SCALE) * inverse)


def main_kernel(vel_ref, solid_ref, clip_ref, lo_ref, wrap_ref, hi_ref, relay_ref, far_ref, wide_ref, side_ref,
                near_ref, src_ref, lq_ref, mn_ref, two_ref, two_wrap_ref, stress_ref, new_ref, scratch, old, tiles):
    lane = lax.broadcasted_iota(jnp.int32, (8, 128), 1)
    sub = lax.broadcasted_iota(jnp.int32, (8, 128), 0)
    run, even = place()
    here = lax.broadcasted_iota(jnp.int32, (64, 16), 0) % 8
    back = (lax.axis_index("gx") * 8 + here - src_ref[...] + 512) & 255
    spread = (lax.broadcasted_iota(jnp.int32, (16, 128), 1) // 8 == lax.broadcasted_iota(jnp.int32, (16, 128), 0))
    local = jnp.dot((16 + here - back).astype(F32), spread.astype(F32), preferred_element_type=F32)
    local = (local + 0.5).astype(jnp.int32)
    lower = (lax.axis_index("gy") & 3) < 2

    def add_up(ref):
        tiles[...] = ref[pl.ds(96, 256), :].astype(F32) + ref[pl.ds(352, 256), :].astype(F32)

    pl.when(run == 0)(lambda: add_up(wrap_ref))
    pl.when(run != 0)(lambda: add_up(lo_ref))
    up1 = tiles[...].reshape(4, 64, 128)
    up2 = decode(jnp.where((run == 0) & lower, two_wrap_ref[...].astype(jnp.int32), two_ref[...].astype(jnp.int32))).reshape(4, 64, 128)
    for z in range(8):
        at = pl.ds(8 * z, 8)
        idx = local[8 * z : 8 * z + 8]
        inner = idx & 7
        for f in range(4):
            own_ref = lq_ref if f < 2 else mn_ref
            own = own_ref[pl.ds(64 * (f % 2) + 8 * z, 8), :]
            got = jnp.take_along_axis(own, inner, axis=0)
            one = jnp.take_along_axis(up1[f, 8 * z : 8 * z + 8], inner, axis=0)
            two = jnp.take_along_axis(up2[f, 8 * z : 8 * z + 8], inner, axis=0)
            old[f, at, :] = jnp.where(idx < 8, two, jnp.where(idx < 16, one, got))
    lo = jnp.where(run == 0, lead(wrap_ref, 96), lead(lo_ref, 96))
    hi = jnp.where(run == 7, lead(relay_ref, HEAD), lead(hi_ref, HEAD))
    core = all_rows(own_rows(vel_ref, solid_ref, scratch), lo, hi)
    near = near_ref[...].astype(F32).reshape(4, 8, 128)
    far = jnp.where(run == 0, wide_ref[pl.ds(HEAD, 32), :].astype(F32), far_ref[...].astype(F32)).reshape(4, 8, 128)
    below = jnp.where(lower, lead(side_ref, 96), lead(lo_ref, 96)).reshape(3, 4, 8, 128)
    above = relay_ref[pl.ds(HEAD, 32), :].astype(F32).reshape(4, 8, 128)
    far = [jnp.where((run == 7) & (lane >= 44), pltpu.roll(above[c], 32, 1), far[c]) for c in range(3)]
    edge = []
    for c in range(3):
        left = jnp.where(even, far[c], near[c])
        right = jnp.where(even, near[c], far[c])
        rows = []
        for i in range(14):
            r = pltpu.roll(right, 128 - 4 * i, 1) if i else right
            l = pltpu.roll(left, 124 - 4 * i, 1)
            value = jnp.where(lane < 64, r, l)
            if i < 3:
                value = jnp.where((run == 0) & ((lane >= 64) == even), below[c, i + 1], value)
            rows.append(value)
        edge.append(jnp.stack(rows))
    core = [jnp.stack(rows) for rows in core]

    def chunks(first, last, size):
        return [(k, min(k + size, last)) for k in range(first, last, size)]

    flow = [[[] for _ in range(5)] for _ in range(3)]
    for lo_i, hi_i in chunks(0, 14, ROWS_A):
        for c in range(3):
            a, b = core[c][lo_i:hi_i], edge[c][lo_i:hi_i]
            p1, m1 = shift_y(a, b, 1, lane), shift_y(a, b, -1, lane)
            p2, m2 = shift_y(a, b, 2, lane), shift_y(a, b, -2, lane)
            p3, m3 = shift_y(a, b, 3, lane), shift_y(a, b, -3, lane)
            s1, d1, s2, d2 = p1 + m1, p1 - m1, p2 + m2, p2 - m2
            t = a + s1
            for k, v in enumerate((a + t, t + t + s2, d1 + d1 + d2, d1 + d2 + d2 + (p3 - m3), d1)):
                flow[c][k].append(v)
    flow = [[jnp.concatenate(v, axis=0) for v in per] for per in flow]
    yn, yw, own_flux = ([[] for _ in range(k)] for k in (12, 12, 6))
    for lo_i, hi_i in chunks(1, 13, ROWS_B):
        flux = []
        for t, o in ((core, edge), (edge, core)):
            mid = [t[c][lo_i:hi_i] for c in range(3)]
            dx = [t[c][lo_i + 1 : hi_i + 1] - t[c][lo_i - 1 : hi_i - 1] for c in range(3)]
            if t is core:
                dy = [flow[c][4][lo_i:hi_i] for c in range(3)]
            else:
                oth = [o[c][lo_i:hi_i] for c in range(3)]
                dy = [shift_y(mid[c], oth[c], 1, lane) - shift_y(mid[c], oth[c], -1, lane) for c in range(3)]
            dz = [diff_z(mid[c], sub) for c in range(3)]
            s, mag = strain(dx, dy, dz)
            flux.append([mid[p] * mid[q] for p, q in PAIRS] + [mag * e for e in s])
        for k in range(6):
            own_flux[k].append(flux[0][6 + k])
        for k, (a, b) in enumerate(zip(*flux)):
            s1 = shift_y(a, b, 1, lane) + shift_y(a, b, -1, lane)
            s2 = shift_y(a, b, 2, lane) + shift_y(a, b, -2, lane)
            t = a + s1
            yn[k].append(a + t)
            yw[k].append(t + t + s2)
    yn, yw, own_flux = ([jnp.concatenate(v, axis=0) for v in g] for g in (yn, yw, own_flux))

    def filt_n(r, base, lo_i, hi_i):
        at = lambda k: r[lo_i + k - base : hi_i + k - base]
        return (at(-1) + at(1) + (at(0) + at(0))) * 0.0625

    def filt_w(r, base, lo_i, hi_i):
        at = lambda k: r[lo_i + k - base : hi_i + k - base]
        t = at(-1) + at(0) + at(1)
        return (at(-2) + at(2) + (t + t)) * 0.015625

    un = [filt_n(flow[c][0], 0, 2, 12) for c in range(3)]
    uw = [filt_w(flow[c][1], 0, 2, 12) for c in range(3)]
    for lo_i, hi_i in chunks(3, 11, ROWS_C):
        result = []
        for u, which, filt, flux, factor in ((un, 2, filt_n, yn, 4.0), (uw, 3, filt_w, yw, 16.0)):
            mid = [u[c][lo_i - 2 : hi_i - 2] for c in range(3)]
            dx = [u[c][lo_i - 1 : hi_i - 1] - u[c][lo_i - 3 : hi_i - 3] for c in range(3)]
            dy = [filt(flow[c][which], 0, lo_i, hi_i) for c in range(3)]
            dz = [diff_z(mid[c], sub) for c in range(3)]
            s, mag = strain(dx, dy, dz)
            f = [filt(flux[k], 1, lo_i, hi_i) for k in range(12)]
            lhs = [f[k] - mid[p] * mid[q] for k, (p, q) in enumerate(PAIRS)]
            fm = factor * mag
            rhs = [f[6 + k] - fm * s[k] for k in range(6)]
            result.append((2.0 * contract(lhs, rhs), 4.0 * contract(rhs, rhs)))
        (lm, mm), (qn, nn) = result
        span = range(lo_i - 3, hi_i - 3)
        o_lm, o_qn, o_mm, o_nn = (jnp.stack([row(old, x, f) for x in span]) for f in range(4))
        wn = relax_weight(o_lm * o_mm)
        ww = relax_weight(o_qn * o_nn)
        new_lm = wn * lm + (1.0 - wn) * o_lm
        new_mm = wn * mm + (1.0 - wn) * o_mm
        new_qn = ww * qn + (1.0 - ww) * o_qn
        new_nn = ww * nn + (1.0 - ww) * o_nn
        c2 = jnp.maximum(new_lm, 0.0) * pl.reciprocal(new_mm)
        c4 = jnp.maximum(new_qn, 0.0) * pl.reciprocal(new_nn)
        cs = c2 * c2 * pl.reciprocal(jnp.maximum(jnp.maximum(c4, 0.125 * c2), RATIO_FLOOR))
        clipped = jnp.stack([row(clip_ref, x) for x in span]) == 1
        blocked = jnp.stack([row(solid_ref, x) for x in span]) == 1
        cs = jnp.where(clipped, jnp.minimum(cs, CLIP_CAP), cs)
        cs = jnp.where(blocked, 0.0, -2.0 * cs)
        out = [cs * own_flux[k][lo_i - 1 : hi_i - 1] for k in range(6)]
        for j, x in enumerate(span):
            at = (pl.ds(x, 8, stride=8), slice(None))
            for k in range(6):
                stress_ref[(k,) + at] = out[k][j]
            for k, v in enumerate((new_lm, new_mm, new_qn, new_nn)):
                new_ref[(k,) + at] = v[j]


VM = pl.BlockSpec(memory_space=pltpu.VMEM)
HBM = pl.BlockSpec(memory_space=pltpu.HBM)


def call(kernel, outs, specs, scratch, limit=VMEM_LIMIT, flops=0):
    return pl.pallas_call(
        kernel, out_shape=outs, in_specs=specs, out_specs=[VM] * len(outs), scratch_shapes=scratch,
        compiler_params=pltpu.CompilerParams(vmem_limit_bytes=limit),
        cost_estimate=pl.CostEstimate(flops=flops, bytes_accessed=400_000, transcendentals=0),
    )


def far_side(gy):
    return (gy + 1) % 16 if gy % 2 else (gy - 1) % 16


def low(gy):
    return gy % 4 < 2


def send(x, target):
    pairs = []
    for gx in range(32):
        for gy in range(16):
            to = target(gx % 8, gx, gy)
            if to is not None:
                pairs.append((gx * 16 + gy, to[0] % 32 * 16 + to[1]))
    return lax.ppermute(x, ("gx", "gy"), pairs)


def local(velocity, kept_lm_qn, kept_mm_nn, back_src, solid_flags, clip_flags):
    sds = jax.ShapeDtypeStruct
    vel = velocity.reshape(3, 64, 128)
    solid = solid_flags.reshape(64, 128)
    clip = clip_flags.reshape(64, 128)
    lq = kept_lm_qn.reshape(128, 128)
    mn = kept_mm_nn.reshape(128, 128)
    src = back_src.reshape(64, 16)
    strip_type = sds((32, 128), BF16)
    code_type = sds((256, 128), jnp.int16)
    trans = pltpu.VMEM((3, 64, 128), F32)
    tail, head, side, code = call(
        pack_kernel,
        [sds((608, 128), BF16), sds((HEAD, 128), BF16), sds((SIDE, 128), BF16), code_type],
        [HBM] * 4,
        [pltpu.VMEM((3, 64, 128), BF16), pltpu.VMEM((64, 128), jnp.int32), pltpu.VMEM((256, 128), F32),
         trans, pltpu.SemaphoreType.DMA((4,))],
        PACK_LIMIT,
    )(vel, solid, lq, mn)
    lo = send(tail, lambda run, gx, gy: (gx + 1, gy) if run < 7 else (gx + 1, far_side(gy)) if low(gy) else None)
    hi = send(head, lambda run, gx, gy: (gx - 1, gy) if run > 0 else None)
    side = send(side, lambda run, gx, gy: (gx + 1, far_side(gy)) if run == 7 and not low(gy) else None)
    wrap = send(tail, lambda run, gx, gy: (gx + 1, gy) if run == 7 else None)
    two_wrap = send(code, lambda run, gx, gy: (gx + 2, gy) if run == 6 and low(gy) else None)
    two = send(code, lambda run, gx, gy: (gx + 2, gy) if run != 6 or not low(gy) else None)
    (wide,) = call(wide_kernel, [sds((HEAD + 32, 128), BF16)], [VM] * 3, [trans], flops=BIG)(vel, solid, hi)
    (strip,) = call(far_kernel, [strip_type], [VM] * 4, [trans])(vel, solid, lo, hi)
    wide = send(wide, lambda run, gx, gy: (gx, far_side(gy)) if run == 0 else None)
    relay, strip = call(relay_kernel, [sds((HEAD + 32, 128), BF16), strip_type], [VM] * 4, [])(wide, strip, side, two_wrap)
    relay = send(relay, lambda run, gx, gy: (gx - 1, far_side(gy)) if run == 0 else None)
    far = send(strip, lambda run, gx, gy: (gx, far_side(gy)) if run > 0 else None)
    (near,) = call(near_kernel, [strip_type], [VM] * 6, [trans])(vel, solid, lo, wrap, hi, relay)
    near = send(near, lambda run, gx, gy: (gx, gy ^ 1))
    stress, new = call(
        main_kernel, [sds((6, 64, 128), F32), sds((4, 64, 128), F32)], [VM] * 16, [trans, pltpu.VMEM((4, 64, 128), F32), pltpu.VMEM((256, 128), F32)],
    )(vel, solid, clip, lo, wrap, hi, relay, far, wide, side, near, src, lq, mn, two, two_wrap)
    return stress.reshape(6, 8, 8, 128), new.reshape(4, 8, 8, 128)


def solution(mesh):
    in_specs = (
        P(None, None, "gx", "gy"),
        P(None, None, "gx", "gy"),
        P(None, None, "gx", "gy"),
        P(None, "gx", "gy"),
        P(None, "gx", "gy"),
        P(None, "gx", "gy"),
    )
    out_specs = (P(None, None, "gx", "gy"), P(None, None, "gx", "gy"))
    return jax.shard_map(local, mesh=mesh, in_specs=in_specs, out_specs=out_specs, check_vma=False)
```

```python
import jax
import jax.numpy as jnp
from jax import lax
from jax.experimental import pallas as pl
from jax.experimental.pallas import tpu as pltpu
from jax.sharding import PartitionSpec as P

PRODUCT_FLOOR = 0.05
RATE_SCALE = 0.5
CLIP_CAP = 0.1
RATIO_FLOOR = 0.02
PAIRS = ((0, 0), (1, 1), (2, 2), (0, 1), (0, 2), (1, 2))
KEPT_SCALE = 32767.0 / 1.1892073
F32 = jnp.float32
BF16 = jnp.bfloat16
VMEM_LIMIT = 32 * 1024 * 1024
PACK_LIMIT = 60 * 1024 * 1024
BIG = 1_000_000_000
SIDE = 112
HEAD = 80
ROWS_A = 7
ROWS_B = 4
ROWS_C = 2


def row(ref, x, lead=None):
    at = (pl.ds(x, 8, stride=8), slice(None))
    return ref[at] if lead is None else ref[(lead,) + at]


def encode(x):
    root = jnp.sqrt(jnp.sqrt(jnp.sqrt(jnp.abs(x))))
    scaled = jnp.where(x < 0, -root, root) * KEPT_SCALE
    return jnp.round(scaled).astype(jnp.int32).astype(jnp.int16)


def decode(code):
    y = code.astype(jnp.int32).astype(F32) * (1.0 / KEPT_SCALE)
    y2 = y * y
    y4 = y2 * y2
    return jnp.where(y < 0, -y4, y4) * y4


def place():
    return lax.axis_index("gx") & 7, (lax.axis_index("gy") & 1) == 0


def edges(rows, first):
    lane = lax.broadcasted_iota(jnp.int32, (8, 128), 1)
    left, right = [], []
    for c in range(3):
        lefts = jnp.zeros((8, 128), F32)
        rights = jnp.zeros((8, 128), F32)
        for k, value in enumerate(rows[c]):
            i = first + k
            here = (lane >= 4 * i) & (lane < 4 * i + 4)
            lefts = jnp.where(here, pltpu.roll(value, 4 * i, 1) if i else value, lefts)
            rights = jnp.where(here, pltpu.roll(value, 4 * i + 4, 1), rights)
        left.append(lefts)
        right.append(rights)
    none = [jnp.zeros((8, 128), F32)]
    return jnp.concatenate(left + none, axis=0), jnp.concatenate(right + none, axis=0)


def code_kernel(lq_ref, mn_ref, code_ref):
    code_ref[pl.ds(0, 128), :] = encode(lq_ref[...])
    code_ref[pl.ds(128, 128), :] = encode(mn_ref[...])


def own_rows(vel_ref, solid_ref, scratch):
    inside = solid_ref[...] == 1
    for c in range(3):
        scratch[c] = jnp.where(inside, 0.0, vel_ref[c].astype(F32))
    return [[row(scratch, x, c) for x in range(8)] for c in range(3)]


def head_rows(rows):
    none = [jnp.zeros((8, 128), F32)]
    return jnp.concatenate([rows[c][x] for c in range(3) for x in range(3)] + none, axis=0).astype(BF16)


def pack_kernel(vel_hbm, solid_hbm, lq_hbm, mn_hbm, tail_ref, head_ref, side_ref,
                vel, solid, kept, scratch, sems):
    copies = [
        pltpu.make_async_copy(vel_hbm, vel, sems.at[0]),
        pltpu.make_async_copy(solid_hbm, solid, sems.at[1]),
        pltpu.make_async_copy(lq_hbm, kept.at[pl.ds(0, 128)], sems.at[2]),
        pltpu.make_async_copy(mn_hbm, kept.at[pl.ds(128, 128)], sems.at[3]),
    ]
    for copy in copies:
        copy.start()
    copies[0].wait()
    copies[1].wait()
    rows = own_rows(vel, solid, scratch)
    head_ref[...] = head_rows(rows)
    tail = jnp.concatenate([rows[c][4 + x] for c in range(3) for x in range(4)], axis=0).astype(BF16)
    tail_ref[pl.ds(0, 96), :] = tail
    side_ref[pl.ds(0, 96), :] = tail
    side_ref[pl.ds(96, SIDE - 96), :] = jnp.zeros((SIDE - 96, 128), BF16)
    copies[2].wait()
    copies[3].wait()
    old = kept[...]
    high = old.astype(BF16)
    tail_ref[pl.ds(96, 256), :] = high
    tail_ref[pl.ds(352, 256), :] = (old - high.astype(F32)).astype(BF16)


def all_rows(own, lo, hi):
    lo = lo.reshape(3, 4, 8, 128)
    hi = hi[:72].reshape(3, 3, 8, 128)
    out = []
    for c in range(3):
        rows = [lo[c, x] for x in (1, 2, 3)]
        rows += own[c]
        rows += [hi[c, x] for x in (0, 1, 2)]
        out.append(rows)
    return out


def lead(ref, n):
    return ref[pl.ds(0, n), :].astype(F32)


def wide_kernel(vel_ref, solid_ref, hi_ref, wide_ref, scratch):
    own = own_rows(vel_ref, solid_ref, scratch)
    hi = lead(hi_ref, HEAD)
    left, right = edges(all_rows(own, jnp.zeros((96, 128), F32), hi), 0)
    _, even = place()
    wide_ref[pl.ds(HEAD, 32), :] = jnp.where(even, left, right).astype(BF16)
    wide_ref[pl.ds(0, HEAD), :] = head_rows(own)


def far_kernel(vel_ref, solid_ref, lo_ref, hi_ref, strip_ref, scratch):
    rows = all_rows(own_rows(vel_ref, solid_ref, scratch), lead(lo_ref, 96), lead(hi_ref, HEAD))
    left, right = edges(rows, 0)
    _, even = place()
    strip_ref[...] = jnp.where(even, left, right).astype(BF16)


def relay_kernel(wide_ref, strip_ref, side_ref, two_ref, relay_ref, strip_out):
    relay_ref[pl.ds(0, HEAD), :] = wide_ref[pl.ds(0, HEAD), :]
    relay_ref[pl.ds(HEAD, 32), :] = strip_ref[...]
    strip_out[...] = strip_ref[...]


def near_kernel(vel_ref, solid_ref, lo_ref, wrap_ref, hi_ref, relay_ref, strip_ref, scratch):
    at, even = place()
    own = own_rows(vel_ref, solid_ref, scratch)
    lo = jnp.where(at == 0, lead(wrap_ref, 96), lead(lo_ref, 96))
    hi = jnp.where(at == 7, lead(relay_ref, HEAD), lead(hi_ref, HEAD))
    left, right = edges(all_rows(own, lo, hi), 0)
    strip_ref[...] = jnp.where(even, right, left).astype(BF16)


def shift_y(a, b, k, lane):
    if k > 0:
        return pltpu.roll(jnp.where(lane < k, b, a), 128 - k, a.ndim - 1)
    return pltpu.roll(jnp.where(lane >= 128 + k, b, a), -k, a.ndim - 1)


def diff_z(f, sub):
    up = jnp.where(sub == 7, f, pltpu.roll(f, 7, f.ndim - 2))
    down = jnp.where(sub == 0, f, pltpu.roll(f, 1, f.ndim - 2))
    return up - down


def strain(dx, dy, dz):
    d = (dx, dy, dz)
    s = [0.5 * d[i][i] for i in range(3)] + [0.25 * (d[j][i] + d[i][j]) for i, j in PAIRS[3:]]
    diag = s[0] * s[0] + s[1] * s[1] + s[2] * s[2]
    off = s[3] * s[3] + s[4] * s[4] + s[5] * s[5]
    return s, jnp.sqrt(2.0 * diag + 4.0 * off)


def contract(a, b):
    return (a[0] * b[0] + a[1] * b[1] + a[2] * b[2]) + 2.0 * (a[3] * b[3] + a[4] * b[4] + a[5] * b[5])


def relax_weight(product):
    inverse = lax.rsqrt(lax.rsqrt(lax.rsqrt(jnp.maximum(product, PRODUCT_FLOOR))))
    return pl.reciprocal(1.0 + (1.0 / RATE_SCALE) * inverse)


def main_kernel(vel_ref, solid_ref, clip_ref, lo_ref, wrap_ref, hi_ref, relay_ref, far_ref, wide_ref, side_ref,
                near_ref, src_ref, lq_ref, mn_ref, two_ref, two_wrap_ref, stress_ref, new_ref, scratch, old, tiles):
    lane = lax.broadcasted_iota(jnp.int32, (8, 128), 1)
    sub = lax.broadcasted_iota(jnp.int32, (8, 128), 0)
    run, even = place()
    here = lax.broadcasted_iota(jnp.int32, (64, 16), 0) % 8
    back = (lax.axis_index("gx") * 8 + here - src_ref[...] + 512) & 255
    spread = (lax.broadcasted_iota(jnp.int32, (16, 128), 1) // 8 == lax.broadcasted_iota(jnp.int32, (16, 128), 0))
    local = jnp.dot((16 + here - back).astype(F32), spread.astype(F32), preferred_element_type=F32)
    local = (local + 0.5).astype(jnp.int32)
    lower = (lax.axis_index("gy") & 3) < 2

    def add_up(ref):
        tiles[...] = ref[pl.ds(96, 256), :].astype(F32) + ref[pl.ds(352, 256), :].astype(F32)

    pl.when(run == 0)(lambda: add_up(wrap_ref))
    pl.when(run != 0)(lambda: add_up(lo_ref))
    up1 = tiles[...].reshape(4, 64, 128)
    up2 = decode(jnp.where((run == 0) & lower, two_wrap_ref[...].astype(jnp.int32), two_ref[...].astype(jnp.int32))).reshape(4, 64, 128)
    for z in range(8):
        at = pl.ds(8 * z, 8)
        idx = local[8 * z : 8 * z + 8]
        inner = idx & 7
        for f in range(4):
            own_ref = lq_ref if f < 2 else mn_ref
            own = own_ref[pl.ds(64 * (f % 2) + 8 * z, 8), :]
            got = jnp.take_along_axis(own, inner, axis=0)
            one = jnp.take_along_axis(up1[f, 8 * z : 8 * z + 8], inner, axis=0)
            two = jnp.take_along_axis(up2[f, 8 * z : 8 * z + 8], inner, axis=0)
            old[f, at, :] = jnp.where(idx < 8, two, jnp.where(idx < 16, one, got))
    lo = jnp.where(run == 0, lead(wrap_ref, 96), lead(lo_ref, 96))
    hi = jnp.where(run == 7, lead(relay_ref, HEAD), lead(hi_ref, HEAD))
    core = all_rows(own_rows(vel_ref, solid_ref, scratch), lo, hi)
    near = near_ref[...].astype(F32).reshape(4, 8, 128)
    far = jnp.where(run == 0, wide_ref[pl.ds(HEAD, 32), :].astype(F32), far_ref[...].astype(F32)).reshape(4, 8, 128)
    below = jnp.where(lower, lead(side_ref, 96), lead(lo_ref, 96)).reshape(3, 4, 8, 128)
    above = relay_ref[pl.ds(HEAD, 32), :].astype(F32).reshape(4, 8, 128)
    far = [jnp.where((run == 7) & (lane >= 44), pltpu.roll(above[c], 32, 1), far[c]) for c in range(3)]
    edge = []
    for c in range(3):
        left = jnp.where(even, far[c], near[c])
        right = jnp.where(even, near[c], far[c])
        rows = []
        for i in range(14):
            r = pltpu.roll(right, 128 - 4 * i, 1) if i else right
            l = pltpu.roll(left, 124 - 4 * i, 1)
            value = jnp.where(lane < 64, r, l)
            if i < 3:
                value = jnp.where((run == 0) & ((lane >= 64) == even), below[c, i + 1], value)
            rows.append(value)
        edge.append(jnp.stack(rows))
    core = [jnp.stack(rows) for rows in core]

    def chunks(first, last, size):
        return [(k, min(k + size, last)) for k in range(first, last, size)]

    flow = [[[] for _ in range(5)] for _ in range(3)]
    for lo_i, hi_i in chunks(0, 14, ROWS_A):
        for c in range(3):
            a, b = core[c][lo_i:hi_i], edge[c][lo_i:hi_i]
            p1, m1 = shift_y(a, b, 1, lane), shift_y(a, b, -1, lane)
            p2, m2 = shift_y(a, b, 2, lane), shift_y(a, b, -2, lane)
            p3, m3 = shift_y(a, b, 3, lane), shift_y(a, b, -3, lane)
            s1, d1, s2, d2 = p1 + m1, p1 - m1, p2 + m2, p2 - m2
            t = a + s1
            for k, v in enumerate((a + t, t + t + s2, d1 + d1 + d2, d1 + d2 + d2 + (p3 - m3), d1)):
                flow[c][k].append(v)
    flow = [[jnp.concatenate(v, axis=0) for v in per] for per in flow]
    yn, yw, own_flux = ([[] for _ in range(k)] for k in (12, 12, 6))
    for lo_i, hi_i in chunks(1, 13, ROWS_B):
        flux = []
        for t, o in ((core, edge), (edge, core)):
            mid = [t[c][lo_i:hi_i] for c in range(3)]
            dx = [t[c][lo_i + 1 : hi_i + 1] - t[c][lo_i - 1 : hi_i - 1] for c in range(3)]
            if t is core:
                dy = [flow[c][4][lo_i:hi_i] for c in range(3)]
            else:
                oth = [o[c][lo_i:hi_i] for c in range(3)]
                dy = [shift_y(mid[c], oth[c], 1, lane) - shift_y(mid[c], oth[c], -1, lane) for c in range(3)]
            dz = [diff_z(mid[c], sub) for c in range(3)]
            s, mag = strain(dx, dy, dz)
            flux.append([mid[p] * mid[q] for p, q in PAIRS] + [mag * e for e in s])
        for k in range(6):
            own_flux[k].append(flux[0][6 + k])
        for k, (a, b) in enumerate(zip(*flux)):
            s1 = shift_y(a, b, 1, lane) + shift_y(a, b, -1, lane)
            s2 = shift_y(a, b, 2, lane) + shift_y(a, b, -2, lane)
            t = a + s1
            yn[k].append(a + t)
            yw[k].append(t + t + s2)
    yn, yw, own_flux = ([jnp.concatenate(v, axis=0) for v in g] for g in (yn, yw, own_flux))

    def filt_n(r, base, lo_i, hi_i):
        at = lambda k: r[lo_i + k - base : hi_i + k - base]
        return (at(-1) + at(1) + (at(0) + at(0))) * 0.0625

    def filt_w(r, base, lo_i, hi_i):
        at = lambda k: r[lo_i + k - base : hi_i + k - base]
        t = at(-1) + at(0) + at(1)
        return (at(-2) + at(2) + (t + t)) * 0.015625

    un = [filt_n(flow[c][0], 0, 2, 12) for c in range(3)]
    uw = [filt_w(flow[c][1], 0, 2, 12) for c in range(3)]
    for lo_i, hi_i in chunks(3, 11, ROWS_C):
        result = []
        for u, which, filt, flux, factor in ((un, 2, filt_n, yn, 4.0), (uw, 3, filt_w, yw, 16.0)):
            mid = [u[c][lo_i - 2 : hi_i - 2] for c in range(3)]
            dx = [u[c][lo_i - 1 : hi_i - 1] - u[c][lo_i - 3 : hi_i - 3] for c in range(3)]
            dy = [filt(flow[c][which], 0, lo_i, hi_i) for c in range(3)]
            dz = [diff_z(mid[c], sub) for c in range(3)]
            s, mag = strain(dx, dy, dz)
            f = [filt(flux[k], 1, lo_i, hi_i) for k in range(12)]
            lhs = [f[k] - mid[p] * mid[q] for k, (p, q) in enumerate(PAIRS)]
            fm = factor * mag
            rhs = [f[6 + k] - fm * s[k] for k in range(6)]
            result.append((2.0 * contract(lhs, rhs), 4.0 * contract(rhs, rhs)))
        (lm, mm), (qn, nn) = result
        span = range(lo_i - 3, hi_i - 3)
        o_lm, o_qn, o_mm, o_nn = (jnp.stack([row(old, x, f) for x in span]) for f in range(4))
        wn = relax_weight(o_lm * o_mm)
        ww = relax_weight(o_qn * o_nn)
        new_lm = wn * lm + (1.0 - wn) * o_lm
        new_mm = wn * mm + (1.0 - wn) * o_mm
        new_qn = ww * qn + (1.0 - ww) * o_qn
        new_nn = ww * nn + (1.0 - ww) * o_nn
        c2 = jnp.maximum(new_lm, 0.0) * pl.reciprocal(new_mm)
        c4 = jnp.maximum(new_qn, 0.0) * pl.reciprocal(new_nn)
        cs = c2 * c2 * pl.reciprocal(jnp.maximum(jnp.maximum(c4, 0.125 * c2), RATIO_FLOOR))
        clipped = jnp.stack([row(clip_ref, x) for x in span]) == 1
        blocked = jnp.stack([row(solid_ref, x) for x in span]) == 1
        cs = jnp.where(clipped, jnp.minimum(cs, CLIP_CAP), cs)
        cs = jnp.where(blocked, 0.0, -2.0 * cs)
        out = [cs * own_flux[k][lo_i - 1 : hi_i - 1] for k in range(6)]
        for j, x in enumerate(span):
            at = (pl.ds(x, 8, stride=8), slice(None))
            for k in range(6):
                stress_ref[(k,) + at] = out[k][j]
            for k, v in enumerate((new_lm, new_mm, new_qn, new_nn)):
                new_ref[(k,) + at] = v[j]


VM = pl.BlockSpec(memory_space=pltpu.VMEM)
HBM = pl.BlockSpec(memory_space=pltpu.HBM)


def call(kernel, outs, specs, scratch, limit=VMEM_LIMIT, flops=0):
    return pl.pallas_call(
        kernel, out_shape=outs, in_specs=specs, out_specs=[VM] * len(outs), scratch_shapes=scratch,
        compiler_params=pltpu.CompilerParams(vmem_limit_bytes=limit),
        cost_estimate=pl.CostEstimate(flops=flops, bytes_accessed=400_000, transcendentals=0),
    )


def far_side(gy):
    return (gy + 1) % 16 if gy % 2 else (gy - 1) % 16


def low(gy):
    return gy % 4 < 2


def send(x, target):
    pairs = []
    for gx in range(32):
        for gy in range(16):
            to = target(gx % 8, gx, gy)
            if to is not None:
                pairs.append((gx * 16 + gy, to[0] % 32 * 16 + to[1]))
    return lax.ppermute(x, ("gx", "gy"), pairs)


def local(velocity, kept_lm_qn, kept_mm_nn, back_src, solid_flags, clip_flags):
    sds = jax.ShapeDtypeStruct
    vel = velocity.reshape(3, 64, 128)
    solid = solid_flags.reshape(64, 128)
    clip = clip_flags.reshape(64, 128)
    lq = kept_lm_qn.reshape(128, 128)
    mn = kept_mm_nn.reshape(128, 128)
    src = back_src.reshape(64, 16)
    strip_type = sds((32, 128), BF16)
    code_type = sds((256, 128), jnp.int16)
    trans = pltpu.VMEM((3, 64, 128), F32)
    tail, head, side = call(
        pack_kernel,
        [sds((608, 128), BF16), sds((HEAD, 128), BF16), sds((SIDE, 128), BF16)],
        [HBM] * 4,
        [pltpu.VMEM((3, 64, 128), BF16), pltpu.VMEM((64, 128), jnp.int32), pltpu.VMEM((256, 128), F32),
         trans, pltpu.SemaphoreType.DMA((4,))],
        PACK_LIMIT,
    )(vel, solid, lq, mn)
    lo = send(tail, lambda run, gx, gy: (gx + 1, gy) if run < 7 else (gx + 1, far_side(gy)) if low(gy) else None)
    hi = send(head, lambda run, gx, gy: (gx - 1, gy) if run > 0 else None)
    side = send(side, lambda run, gx, gy: (gx + 1, far_side(gy)) if run == 7 and not low(gy) else None)
    wrap = send(tail, lambda run, gx, gy: (gx + 1, gy) if run == 7 else None)
    (code,) = call(code_kernel, [code_type], [VM] * 2, [])(lq, mn)
    two_wrap = send(code, lambda run, gx, gy: (gx + 2, gy) if run == 6 and low(gy) else None)
    two = send(code, lambda run, gx, gy: (gx + 2, gy) if run != 6 or not low(gy) else None)
    (wide,) = call(wide_kernel, [sds((HEAD + 32, 128), BF16)], [VM] * 3, [trans], flops=BIG)(vel, solid, hi)
    (strip,) = call(far_kernel, [strip_type], [VM] * 4, [trans])(vel, solid, lo, hi)
    wide = send(wide, lambda run, gx, gy: (gx, far_side(gy)) if run == 0 else None)
    relay, strip = call(relay_kernel, [sds((HEAD + 32, 128), BF16), strip_type], [VM] * 4, [])(wide, strip, side, two_wrap)
    relay = send(relay, lambda run, gx, gy: (gx - 1, far_side(gy)) if run == 0 else None)
    far = send(strip, lambda run, gx, gy: (gx, far_side(gy)) if run > 0 else None)
    (near,) = call(near_kernel, [strip_type], [VM] * 6, [trans])(vel, solid, lo, wrap, hi, relay)
    near = send(near, lambda run, gx, gy: (gx, gy ^ 1))
    stress, new = call(
        main_kernel, [sds((6, 64, 128), F32), sds((4, 64, 128), F32)], [VM] * 16, [trans, pltpu.VMEM((4, 64, 128), F32), pltpu.VMEM((256, 128), F32)],
    )(vel, solid, clip, lo, wrap, hi, relay, far, wide, side, near, src, lq, mn, two, two_wrap)
    return stress.reshape(6, 8, 8, 128), new.reshape(4, 8, 8, 128)


def solution(mesh):
    in_specs = (
        P(None, None, "gx", "gy"),
        P(None, None, "gx", "gy"),
        P(None, None, "gx", "gy"),
        P(None, "gx", "gy"),
        P(None, "gx", "gy"),
        P(None, "gx", "gy"),
    )
    out_specs = (P(None, None, "gx", "gy"), P(None, None, "gx", "gy"))
    return jax.shard_map(local, mesh=mesh, in_specs=in_specs, out_specs=out_specs, check_vma=False)
```
